32 devices in a mesh: scale: 4 (over z), img: 8 (over y, x, core).
Axes of the slice: x: 2, y: 2, z: 4, core: 2. Of those that a mesh axis runs over, the one named last changes fastest.
Arguments:
- images: bfloat16 [4, 64, 256, 512], P('scale', 'img'), may hold values from -6 to 6
- valid_mask: int32 [64, 256], P('img'), may hold values from 0 to 1, as said below
- scale_cols: int32 [4], replicated, may hold values from 1 to 256, as said below
- boxes: int32 [128], P('img'), may hold values from -1 to 2047, as said below
- normal_targets: float32 [3, 64, 256], P(None, 'img'), may hold values from -6 to 6
- dense_targets: bfloat16 [64, 256, 1792], P('img', None, 'scale'), may hold values from -6 to 6
- affine_scale: float32 [2, 512], replicated, may hold values from 0.5 to 1.5
- affine_shift: float32 [2, 512], replicated, may hold values from -3 to 3
- conv_bf16: bfloat16 [2, 9, 512, 512], replicated, may hold values from -0.09375 to 0.09375
- head_bf16: bfloat16 [7, 512, 256], replicated, may hold values from -0.25 to 0.25
- vectors: float32 [2304], replicated
- vec_m: float32 [2304], replicated
- vec_v: float32 [2304], replicated
- master: float32 [64, 512, 256], P(('scale', 'img')), may hold values from -0.15625 to 0.15625
- slot_m: float32 [64, 512, 256], P(('scale', 'img'))
- slot_v: float32 [64, 512, 256], P(('scale', 'img'))
- basis_left: float32 [64, 512, 512], P(('scale', 'img'))
- basis_right: float32 [64, 256, 256], P(('scale', 'img'))
- owner_slot: int32 [43], replicated, may hold values from 0 to 63, as said below
Outputs:
- loss: float32 [2], replicated
- grad_norm: float32 [], replicated
- vec_new: float32 [2304], replicated
- vec_m_new: float32 [2304], replicated
- vec_v_new: float32 [2304], replicated
- master_new: float32 [64, 512, 256], P(('scale', 'img'))
- slot_m_new: float32 [64, 512, 256], P(('scale', 'img'))
- slot_v_new: float32 [64, 512, 256], P(('scale', 'img'))
- conv_copy: bfloat16 [2, 9, 512, 512], replicated
- head_copy: bfloat16 [7, 512, 256], replicated
The draws below stay inside these ranges and needn't reach their ends.
Inputs may be any that keep to these rules, and one draw needn't show every extreme that they name: scale_cols[0] = 256; scale s has between 256 / 2^(s+1) (at least 1) and 256 / 2^s valid columns. `boxes`: in each device's 16 box slots the valid entries come first and at least one is valid; some device has all 16 valid; padding is -1. `owner_slot`: distinct slots. `valid_mask`: at least one pixel is valid.
All inputs are finite; a program needn't handle non-finite values.
Results may differ from the reference program's by a relative error of at most 0.00086.
Values may be sent and summed in bfloat16 or wider, within the bound.
No kernel may reach another device: no remote copies, remote signals or barrier semaphores. Data moves between devices by JAX's collectives and lax.ppermute only.
A program may use at most 192 MiB of HBM per device.

```python
import jax
import jax.numpy as jnp
from jax import lax

C = 512
HC = 256
HEADS = 7
TAPS = 9
LAYERS = 2
STEP = 5
ROWS_DEV = 8
WID = 256
BOX = 16
HEIGHT = 64
SCALES = 4
NBLK = 43
SLOTS = 64
VEC = 2304


clip_level = 0.001


def grad_size():
    total = LAYERS * TAPS * C * C + HEADS * C * HC + C + HEADS * HC
    return clip_level / total ** 0.5


def draw_valid_mask(key, part):
    key = jax.random.fold_in(key, 11)
    row_iota = jnp.arange(HEIGHT, dtype=jnp.int32)
    col_iota = jnp.arange(WID, dtype=jnp.int32)
    percent = 30 + 60 * row_iota // HEIGHT
    rolled = jax.random.randint(key, (HEIGHT, WID), 0, 100)
    first_pixel = (row_iota[:, None] == 0) & (col_iota[None, :] == 0)
    return jnp.where(first_pixel, 1, (rolled < percent[:, None]).astype(jnp.int32)).astype(jnp.int32)


def draw_scale_cols(key, part):
    key = jax.random.fold_in(key, 12)
    scale_iota = jnp.arange(SCALES, dtype=jnp.int32)
    upper = jnp.right_shift(jnp.int32(WID), scale_iota)
    lower = jnp.maximum(upper // 2, 1)
    picked = jax.random.randint(key, (SCALES,), lower, upper + 1)
    return jnp.where(scale_iota == 0, WID, picked).astype(jnp.int32)


def draw_boxes(key, part):
    key = jax.random.fold_in(key, 13)
    first, second, third = jax.random.split(key, 3)
    blocks = HEIGHT // ROWS_DEV
    counts = jax.random.randint(first, (blocks,), 1, BOX + 1)
    full = jax.random.randint(second, (), 0, blocks)
    block_iota = jnp.arange(blocks, dtype=jnp.int32)
    counts = jnp.where(block_iota == full, BOX, counts)
    counts = jnp.where(block_iota == (full + 1) % blocks, 1, counts)
    pixels = jax.random.randint(third, (blocks, BOX), 0, ROWS_DEV * WID)
    slot_iota = jnp.arange(BOX, dtype=jnp.int32)
    pixels = jnp.where((block_iota[:, None] == full) & (slot_iota[None, :] == 0), ROWS_DEV * WID - 1, pixels)
    listed = jnp.where(slot_iota[None, :] < counts[:, None], pixels, -1)
    return listed.reshape(blocks * BOX).astype(jnp.int32)


def draw_vectors(key, part):
    key = jax.random.fold_in(key, 14)
    first, second = jax.random.split(key)
    gamma = jnp.exp(jax.random.uniform(first, (C,), jnp.float32, -0.5, 0.5))
    bias = 0.3 * jax.random.normal(second, (HEADS * HC,), jnp.float32)
    return jnp.concatenate([gamma, bias])


def draw_vec_m(key, part):
    key = jax.random.fold_in(key, 15)
    return 4.0 * grad_size() * jax.random.normal(key, (VEC,), jnp.float32)


def draw_vec_v(key, part):
    key = jax.random.fold_in(key, 16)
    scale = 4.0 * grad_size()
    return scale * scale * jax.random.uniform(key, (VEC,), jnp.float32, 1.0, 4.0)


def draw_slot_m(key, part):
    key = jax.random.fold_in(key, 17)
    return grad_size() * jax.random.normal(key, (SLOTS, C, HC), jnp.float32)


def draw_slot_v(key, part):
    key = jax.random.fold_in(key, 18)
    scale = grad_size()
    return scale * scale * jax.random.uniform(key, (SLOTS, C, HC), jnp.float32, 1.0, 4.0)


def orthogonal(key, count, order):
    perm_key, sign_key = jax.random.split(key)
    perm_keys = jax.random.split(perm_key, count)
    shuffled = jax.vmap(lambda one_key: jax.random.permutation(one_key, order))(perm_keys).astype(jnp.int32)
    signs = 2.0 * jax.random.randint(sign_key, (count, order), 0, 2).astype(jnp.float32) - 1.0
    freq = jnp.arange(order, dtype=jnp.int32)
    column_gain = jnp.where(freq == 0, (1.0 / order) ** 0.5, (2.0 / order) ** 0.5).astype(jnp.float32)
    place = shuffled.astype(jnp.float32) + 0.5
    angle = jnp.pi / order * place[:, :, None] * freq.astype(jnp.float32)[None, None, :]
    return signs[:, :, None] * column_gain[None, None, :] * jnp.cos(angle)


def draw_basis_left(key, part):
    key = jax.random.fold_in(key, 19)
    return orthogonal(key, SLOTS, C)


def draw_basis_right(key, part):
    key = jax.random.fold_in(key, 20)
    return orthogonal(key, SLOTS, HC)


def draw_owner_slot(key, part):
    key = jax.random.fold_in(key, 21)
    return jax.random.permutation(key, SLOTS)[:NBLK].astype(jnp.int32)


def shard_levels(rng, extent, shards, low, largest):
    gain = 1.0
    for dim, blocks in shards:
        heights = jax.random.uniform(jax.random.fold_in(jax.random.fold_in(rng, 6), dim), (blocks,), jnp.float32, low / len(shards), largest / len(shards))
        gain = gain * jnp.repeat(jnp.exp(heights), extent[dim] // blocks).reshape((-1,) + (1,) * (len(extent) - 1 - dim))
    return gain


def normal_values(own_key, extent, scale, reach, cuts=(), held_as=jnp.bfloat16):
    values = scale * jax.random.normal(own_key, extent, jnp.float32)
    if cuts:
        values = values * shard_levels(own_key, extent, cuts, -0.22, 0.18)
    return jnp.clip(values, -reach, reach).astype(held_as)


def setup_inputs(seed: int = 0) -> dict:
    key_list = jax.random.split(jax.random.key(seed), 20)
    images = normal_values(key_list[0], (SCALES, HEIGHT, WID, C), 1.0, 6.0, ((0, 4), (1, 8)))
    valid_mask = draw_valid_mask(jax.random.fold_in(key_list[19], 71), 0)
    scale_cols = draw_scale_cols(jax.random.fold_in(key_list[19], 71), 0)
    boxes = draw_boxes(jax.random.fold_in(key_list[19], 71), 0)
    normal_targets = normal_values(key_list[4], (3, HEIGHT, WID), 1.0, 6.0, ((1, 8),), jnp.float32)
    dense_targets = normal_values(key_list[5], (HEIGHT, WID, HEADS * HC), 1.0, 6.0, ((0, 8), (2, 4)))
    affine_scale = jnp.clip(1.0 + 0.1 * jax.random.normal(key_list[6], (LAYERS, C), jnp.float32), 0.5, 1.5)
    affine_shift = normal_values(key_list[7], (LAYERS, C), 0.5, 3.0, (), jnp.float32)
    conv_bf16 = normal_values(key_list[8], (LAYERS, TAPS, C, C), (TAPS * C) ** -0.5, 0.09375)
    head_bf16 = normal_values(key_list[9], (HEADS, C, HC), C ** -0.5, 0.25)
    vectors = draw_vectors(jax.random.fold_in(key_list[19], 71), 0)
    vec_m = draw_vec_m(jax.random.fold_in(key_list[19], 71), 0)
    vec_v = draw_vec_v(jax.random.fold_in(key_list[19], 71), 0)
    master = normal_values(key_list[13], (SLOTS, C, HC), (3 * C) ** -0.5, 0.15625, ((0, 32),), jnp.float32)
    slot_m = draw_slot_m(jax.random.fold_in(key_list[19], 71), 0)
    slot_v = draw_slot_v(jax.random.fold_in(key_list[19], 71), 0)
    basis_left = draw_basis_left(jax.random.fold_in(key_list[19], 71), 0)
    basis_right = draw_basis_right(jax.random.fold_in(key_list[19], 71), 0)
    owner_slot = draw_owner_slot(jax.random.fold_in(key_list[19], 71), 0)
    return dict(images=images, valid_mask=valid_mask, scale_cols=scale_cols, boxes=boxes, normal_targets=normal_targets, dense_targets=dense_targets, affine_scale=affine_scale, affine_shift=affine_shift, conv_bf16=conv_bf16, head_bf16=head_bf16, vectors=vectors, vec_m=vec_m, vec_v=vec_v, master=master, slot_m=slot_m, slot_v=slot_v, basis_left=basis_left, basis_right=basis_right, owner_slot=owner_slot)


@jax.custom_vjp
def low(v):
    return lax.optimization_barrier(v.astype(jnp.bfloat16)).astype(jnp.float32)

@jax.custom_vjp
def low_back(v):
    return v

def low_keep(v):
    return (low(v), None)

def low_pass(kept, grad):
    return (grad,)

def back_keep(v):
    return (v, None)

def back_low(kept, grad):
    return (low(grad),)
low.defvjp(low_keep, low_pass)
low_back.defvjp(back_keep, back_low)
beta_one = 0.5
beta_two = 0.5
adam_eps = 1e-08
rate_matrix = 0.01
rate_vector = 0.2
weight_decay = 0.01
clip_level = 0.001
box_weight = 2.0
norm_eps = 1e-05
highest = lax.Precision.HIGHEST

def column_table(columns, width):
    fine_idx = jnp.arange(width, dtype=jnp.int32)
    numer = jnp.maximum((2 * fine_idx + 1) * columns - width, 0)
    lower = numer // (2 * width)
    frac = (numer % (2 * width)).astype(jnp.float32) / (2.0 * width)
    upper = jnp.minimum(lower + 1, columns - 1)
    coarse = fine_idx[:, None]
    return (1.0 - frac)[None, :] * (coarse == lower[None, :]).astype(jnp.float32) + frac[None, :] * (coarse == upper[None, :]).astype(jnp.float32)

def conv_full(inputs, weights):
    padded = jnp.pad(inputs, ((1, 1), (1, 1), (0, 0)))
    total = jnp.zeros(inputs.shape[:2] + (weights.shape[2],), jnp.float32)
    for tap_idx in range(TAPS):
        row_off, col_off = (tap_idx // 3, tap_idx % 3)
        window = padded[row_off:row_off + HEIGHT, col_off:col_off + WID]
        total = total + jnp.einsum('hwc,cd->hwd', window, weights[tap_idx], precision=highest)
    return total

def cosine_terms(predict, targets, mask_f):
    target_last = jnp.moveaxis(targets, 0, -1)
    inner = lax.optimization_barrier(jnp.sum(predict * target_last, -1))
    cosine = inner * lax.rsqrt((lax.optimization_barrier(jnp.sum(predict * predict, -1)) + 1.0) * (lax.optimization_barrier(jnp.sum(target_last * target_last, -1)) + 1.0))
    return jnp.sum(mask_f * (1.0 - cosine))

def forward(conv_w, head_w, vec, images_f, aff_scale, aff_shift, scale_cols, targets, normals, weight, mask_f, count):
    gamma = vec[:C]
    bias = vec[C:]
    joined = jnp.zeros((HEIGHT, WID, HEADS * HC), jnp.float32)
    col_iota = jnp.arange(WID, dtype=jnp.int32)
    for scale_idx in range(SCALES):
        columns = scale_cols[scale_idx]
        col_mask = (col_iota < columns).astype(jnp.float32)[None, :, None]
        current = images_f[scale_idx] * col_mask
        result = current
        for depth_idx in range(LAYERS):
            pre = low_back(conv_full(current, conv_w[depth_idx]))
            result = jax.nn.gelu(pre * aff_scale[depth_idx] + aff_shift[depth_idx]) * col_mask
            if depth_idx + 1 < LAYERS:
                current = low(result)
        tapped = low(gamma * result * lax.rsqrt(lax.optimization_barrier(jnp.mean(result * result, -1, keepdims=True)) + norm_eps))
        projected = low_back(jnp.einsum('hwc,tcd->hwtd', tapped, head_w, precision=highest))
        heads_out = projected.reshape(HEIGHT, WID, HEADS * HC) + bias
        joined = joined + jnp.einsum('ij,hik->hjk', column_table(columns, WID), heads_out, precision=highest)
    dense = 0.5 * jnp.sum(weight[:, :, None] * (joined - targets) ** 2)
    normal = cosine_terms(joined[:, :, 0:3], normals, mask_f)
    loss_sum = dense / (HEADS * HC) + normal
    return (loss_sum / count, loss_sum)

def to_blocks(conv_part, head_part):
    split = conv_part.reshape(LAYERS, TAPS, C, 2, HC).transpose(0, 1, 3, 2, 4).reshape(LAYERS * TAPS * 2, C, HC)
    return jnp.concatenate([split, head_part], 0)

def from_blocks(blocks):
    count_conv = LAYERS * TAPS * 2
    conv_part = blocks[:count_conv].reshape(LAYERS, TAPS, 2, C, HC).transpose(0, 1, 3, 2, 4).reshape(LAYERS, TAPS, C, C)
    return (conv_part, blocks[count_conv:])

def soap_update(master, moment, second, left, right, grads):
    turned = jnp.einsum('sij,sik->sjk', left, grads, precision=highest)
    turned = jnp.einsum('sjk,skl->sjl', turned, right, precision=highest)
    moment = beta_one * moment + (1.0 - beta_one) * turned
    second = beta_two * second + (1.0 - beta_two) * turned * turned
    ratio = moment / (1.0 - beta_one ** STEP) / (jnp.sqrt(second / (1.0 - beta_two ** STEP)) + adam_eps)
    back = jnp.einsum('sij,sjk->sik', left, ratio, precision=highest)
    back = jnp.einsum('sik,slk->sil', back, right, precision=highest)
    return (master - rate_matrix * (back + weight_decay * master), moment, second)

def vector_update(params, moment, second, grads):
    moment = beta_one * moment + (1.0 - beta_one) * grads
    second = beta_two * second + (1.0 - beta_two) * grads * grads
    ratio = moment / (1.0 - beta_one ** STEP) / (jnp.sqrt(second / (1.0 - beta_two ** STEP)) + adam_eps)
    return (params - rate_vector * (ratio + weight_decay * params), moment, second)

def reference(images, valid_mask, scale_cols, boxes, normal_targets, dense_targets, affine_scale, affine_shift, conv_bf16, head_bf16, vectors, vec_m, vec_v, master, slot_m, slot_v, basis_left, basis_right, owner_slot):
    mask_f = valid_mask.astype(jnp.float32)
    count = jnp.sum(mask_f)
    box_rows = boxes.reshape(HEIGHT // ROWS_DEV, BOX)
    pixels = jnp.arange(ROWS_DEV * WID, dtype=jnp.int32)
    hits = lax.optimization_barrier(jnp.sum((box_rows[:, :, None] == pixels[None, None, :]).astype(jnp.float32), 1)).reshape(HEIGHT, WID)
    weight = mask_f + box_weight * hits
    images_f = images.astype(jnp.float32)
    targets = dense_targets.astype(jnp.float32)

    def loss_of(conv_w, head_w, vec):
        return forward(conv_w, head_w, vec, images_f, affine_scale, affine_shift, scale_cols, targets, normal_targets, weight, mask_f, count)
    loss_mean, pull, loss_sum = jax.vjp(loss_of, conv_bf16.astype(jnp.float32), head_bf16.astype(jnp.float32), vectors, has_aux=True)
    grad_conv, grad_head, grad_vec = pull(jnp.ones_like(loss_mean))
    squares = jnp.sum(grad_conv * grad_conv) + jnp.sum(grad_head * grad_head) + jnp.sum(grad_vec * grad_vec)
    grad_norm = jnp.sqrt(squares)
    factor = clip_level / jnp.maximum(grad_norm, clip_level)
    vec_new, vec_m_new, vec_v_new = vector_update(vectors, vec_m, vec_v, grad_vec * factor)
    blocks = to_blocks(grad_conv, grad_head) * factor
    slot_grads = jnp.zeros((SLOTS, C, HC), jnp.float32).at[owner_slot].set(blocks)
    master_new, slot_m_new, slot_v_new = soap_update(master, slot_m, slot_v, basis_left, basis_right, slot_grads)
    conv_copy, head_copy = from_blocks(master_new[owner_slot].astype(jnp.bfloat16))
    loss = jnp.stack([loss_sum, count])
    return (loss, grad_norm, vec_new, vec_m_new, vec_v_new, master_new, slot_m_new, slot_v_new, conv_copy, head_copy)
```

```python
import jax
import jax.numpy as jnp
from jax import lax
from jax.sharding import PartitionSpec as P

STEP = 5

beta_one = 0.5
beta_two = 0.5
adam_eps = 1e-08
rate_matrix = 0.01
rate_vector = 0.2
weight_decay = 0.01
clip_level = 0.001
box_weight = 2.0
norm_eps = 1e-05
highest = lax.Precision.HIGHEST
bf16 = jnp.bfloat16
f32 = jnp.float32
AXES = ("scale", "img")
GAP = 16
CODE = 32767.0


class Layout:
    def __init__(self, scales, imgs):
        self.scales = scales
        self.imgs = imgs

    def pos(self, group, scale):
        return scale if group % 2 == 0 else self.scales - 1 - scale

    def dev(self, scale, img):
        return scale * self.imgs + img

    def at(self, group, place, core):
        return self.dev(self.pos(group, place), 2 * group + core)

    def all_devices(self):
        return [(s, i) for s in range(self.scales) for i in range(self.imgs)]

    def swap(self, bit):
        return [(self.dev(s, i), self.dev(s, i ^ bit)) for s, i in self.all_devices()]

    def turn(self, step):
        return [
            (self.dev(s, i), self.dev((s + step) % self.scales, i)) for s, i in self.all_devices()
        ]

    def scale_swap(self, bit):
        return [(self.dev(s, i), self.dev(s ^ bit, i)) for s, i in self.all_devices()]

    def rows_round(self, shift, sources):
        pairs = []
        for s in sources:
            for i in range(self.imgs):
                group, core = i // 2, i % 2
                piece = (shift + s) % self.scales
                place = (self.scales // 2) * core + piece // 2
                pairs.append((self.dev(s, i), self.at(group, place, piece % 2)))
        return pairs

    def row_order(self):
        groups = self.imgs // 2
        return [
            self.at(j, place, c) for j in range(groups) for place in range(self.scales) for c in range(2)
        ]

    def down(self):
        order = self.row_order()
        return list(zip(order[:-1], order[1:]))

    def up(self):
        order = self.row_order()
        return list(zip(order[1:], order[:-1]))


def permute(value, pairs):
    return lax.ppermute(value, AXES, pairs)


def after(value, *others):
    return lax.optimization_barrier((value, *others))[0]


def column_table(columns, width, coarse_width):
    fine_idx = jnp.arange(width, dtype=jnp.int32)
    numer = jnp.maximum((2 * fine_idx + 1) * columns - width, 0)
    lower = numer // (2 * width)
    frac = (numer % (2 * width)).astype(f32) / (2.0 * width)
    upper = jnp.minimum(lower + 1, columns - 1)
    coarse = jnp.arange(coarse_width, dtype=jnp.int32)[:, None]
    return (1.0 - frac)[None, :] * (coarse == lower[None, :]).astype(f32) + frac[None, :] * (
        coarse == upper[None, :]
    ).astype(f32)


def halves(value):
    high = value.astype(bf16)
    return high, (value - high.astype(f32)).astype(bf16)


def conv_rows(padded, weights):
    kernel = weights.reshape(3, 3, weights.shape[1], weights.shape[2])
    return lax.conv_general_dilated(
        padded[None],
        kernel,
        (1, 1),
        ((0, 0), (1, 1)),
        dimension_numbers=("NHWC", "HWIO", "NHWC"),
        preferred_element_type=f32,
    )[0]


def conv_rows_back(padded, weights):
    kernel = lax.rev(weights.reshape(3, 3, weights.shape[1], weights.shape[2]), (0, 1))
    return lax.conv_general_dilated(
        padded[None],
        kernel,
        (1, 1),
        ((0, 0), (1, 1)),
        dimension_numbers=("NHWC", "HWOI", "NHWC"),
        preferred_element_type=f32,
    )[0]


def kernel_grad(padded_pair, grad_pair):
    rows, cols = grad_pair.shape[1], grad_pair.shape[2]
    wide = jnp.pad(padded_pair, ((0, 0), (0, 0), (1, 1), (0, 0)))
    grads = []
    for tap in range(9):
        a, b = tap // 3, tap % 3
        window = wide[:, a : a + rows, b : b + cols]
        grads.append(
            jnp.einsum("prwc,prwd->cd", window, grad_pair, preferred_element_type=f32)
        )
    return jnp.stack(grads)


def activate(pre, gain, shift, col_mask):
    return jax.nn.gelu(pre * gain + shift) * col_mask


def tap_norm(result, gamma):
    return gamma * result * lax.rsqrt(jnp.mean(result * result, -1, keepdims=True) + norm_eps)


def cosine_terms(predict, target_last, mask_f):
    inner = jnp.sum(predict * target_last, -1)
    cosine = inner * lax.rsqrt(
        (jnp.sum(predict * predict, -1) + 1.0) * (jnp.sum(target_last * target_last, -1) + 1.0)
    )
    return jnp.sum(mask_f * (1.0 - cosine))


def encode(value):
    n, r, cols = value.shape
    top = jnp.max(jnp.abs(value), 1)
    power = jnp.clip(jnp.ceil(jnp.log2(top)), -100.0, 110.0)
    step = jnp.exp2(-power) * CODE
    codes = jnp.clip(jnp.round(value * step[:, None, :]), -CODE, CODE).astype(jnp.int16)
    pad = -n % 16
    powers = jnp.pad(power.astype(jnp.int16), ((0, pad), (0, 0)))
    return jnp.concatenate([codes.reshape(n * r, cols), powers], 0)


def decode(rows, n):
    pad = -n % 16
    total, cols = rows.shape
    r = (total - n - pad) // n
    power = rows[n * r : n * r + n].astype(f32)
    step = jnp.exp2(power) * (1.0 / CODE)
    return rows[: n * r].reshape(n, r, cols).astype(f32) * step[:, None, :]


def pick(value, index, axis):
    return lax.dynamic_index_in_dim(value, index, axis, keepdims=False)


def reduce_piece(part, split, place, lay):
    x, y, z = place
    n, rows, cols = part.shape
    scales = lay.scales
    eighth = rows // 4
    v = part.reshape(n, 2, 2, eighth, cols)
    va, vb = v[..., :split], v[..., split:]
    wa, wb = split, cols - split
    send_a = encode(pick(va, 1 - x, 1).reshape(n, 2 * eighth, wa))
    send_b = encode(pick(vb, 1 - y, 2).reshape(n, 2 * eighth, wb))
    got_a = permute(send_a, lay.swap(2))
    got_b = permute(send_b, lay.swap(4))
    keep_a = pick(va, x, 1) + decode(got_a, n).reshape(n, 2, eighth, wa)
    keep_b = pick(vb, y, 2) + decode(got_b, n).reshape(n, 2, eighth, wb)
    send_a = encode(pick(keep_a, 1 - y, 1))
    send_b = encode(pick(keep_b, 1 - x, 1))
    got_a = permute(send_a, lay.swap(4))
    got_b = permute(send_b, lay.swap(2))
    keep_a = pick(keep_a, y, 1) + decode(got_a, n)
    keep_b = pick(keep_b, x, 1) + decode(got_b, n)
    keep = jnp.concatenate([keep_a, keep_b], -1).reshape(n, scales, eighth // scales, cols)
    total = pick(keep, z, 1)
    for step in range(1, scales):
        send = encode(pick(keep, (z + step) % scales, 1))
        total = total + decode(permute(send, lay.turn(step)), n)
    return total


def core_trade(total, core, lay):
    n, rows, cols = total.shape
    v = total.reshape(n, 2, rows // 2, cols)
    own = pick(v, core, 1)
    other = permute(pick(v, 1 - core, 1), lay.swap(1))
    first = jnp.where(core == 0, own, other)
    second = jnp.where(core == 0, other, own)
    return jnp.stack([first, second])


def from_blocks(blocks, depth, taps):
    count_conv = depth * taps * 2
    chans, half = (blocks.shape[1], blocks.shape[2])
    conv_part = (
        blocks[:count_conv]
        .reshape(depth, taps, 2, chans, half)
        .transpose(0, 1, 3, 2, 4)
        .reshape(depth, taps, chans, 2 * half)
    )
    return (conv_part, blocks[count_conv:])


def soap_update(master, moment, second, left, right, grads):
    turned = jnp.einsum("sij,sik->sjk", left, grads, precision=highest)
    turned = jnp.einsum("sjk,skl->sjl", turned, right, precision=highest)
    moment = beta_one * moment + (1.0 - beta_one) * turned
    second = beta_two * second + (1.0 - beta_two) * turned * turned
    ratio = moment / (1.0 - beta_one**STEP) / (jnp.sqrt(second / (1.0 - beta_two**STEP)) + adam_eps)
    back = jnp.einsum("sij,sjk->sik", left, ratio, precision=highest)
    back = jnp.einsum("sik,slk->sil", back, right, precision=highest)
    return (master - rate_matrix * (back + weight_decay * master), moment, second)


def vector_update(params, moment, second, grads):
    moment = beta_one * moment + (1.0 - beta_one) * grads
    second = beta_two * second + (1.0 - beta_two) * grads * grads
    ratio = moment / (1.0 - beta_one**STEP) / (jnp.sqrt(second / (1.0 - beta_two**STEP)) + adam_eps)
    return (params - rate_vector * (ratio + weight_decay * params), moment, second)


def butterfly(value, lay):
    bit = 1
    while bit < lay.imgs:
        value = value + permute(value, lay.swap(bit))
        bit *= 2
    bit = 1
    while bit < lay.scales:
        value = value + permute(value, lay.scale_swap(bit))
        bit *= 2
    return value


def local(
    images,
    valid_mask,
    scale_cols,
    boxes,
    normal_targets,
    dense_targets,
    affine_scale,
    affine_shift,
    conv_bf16,
    head_bf16,
    vectors,
    vec_m,
    vec_v,
    master,
    slot_m,
    slot_v,
    basis_left,
    basis_right,
    owner_slot,
):
    held, width, chans = (images.shape[1], images.shape[2], images.shape[3])
    heads_count, head_width = (head_bf16.shape[0], head_bf16.shape[2])
    wide = heads_count * head_width
    depth, taps = (conv_bf16.shape[0], conv_bf16.shape[1])
    scales, imgs = lax.axis_size("scale"), lax.axis_size("img")
    lay = Layout(scales, imgs)
    rows = held // scales
    z = lax.axis_index("scale")
    img = lax.axis_index("img")
    group, core = img // 2, img % 2
    place = jnp.where(group % 2 == 0, z, scales - 1 - z)
    mine = 2 * (place % 2) + core

    widths = [width >> s for s in range(scales)]
    starts = []
    at = 0
    for w in widths:
        starts.append(at)
        at += w + GAP
    cols = at - GAP
    col_iota = jnp.arange(cols, dtype=jnp.int32)
    valid_col = jnp.zeros((cols,), jnp.bool_)
    for s in range(scales):
        valid_col |= (col_iota >= starts[s]) & (col_iota < starts[s] + scale_cols[s])
    col_mask = valid_col.astype(f32)[None, :, None]

    own = images[0]
    fine = [
        permute(own[rows * k : rows * (k + 1)], lay.rows_round(k, [0])) for k in range(scales)
    ]
    coarse = []
    for k in range(scales):
        piece = (k + z) % scales
        send = lax.dynamic_slice_in_dim(own[:, : widths[1]], piece * rows, rows, 0)
        coarse.append(permute(send, lay.rows_round(k, range(1, scales))))
    parts = [(fine[0] + fine[1]) + (fine[2] + fine[3])]
    for s in range(1, scales):
        got = 0.0
        for k in range(scales):
            got = got + jnp.where((mine - k) % scales == s, coarse[k][:, : widths[s]], 0)
        parts.append(got.astype(bf16))
    spread = []
    for s in range(scales):
        spread.append(parts[s])
        if s + 1 < scales:
            spread.append(jnp.zeros((rows, GAP, chans), bf16))
    x_zero = jnp.concatenate(spread, 1) * col_mask.astype(bf16)

    target_base = after(dense_targets, x_zero)
    arrived = []
    for k in range(scales):
        piece = (k + z) % scales
        send = lax.dynamic_slice_in_dim(target_base, piece * rows, rows, 0)
        arrived.append(permute(send, lay.rows_round(k, range(scales))))
    stacked_targets = jnp.stack(arrived)
    target = jnp.concatenate(
        [pick(stacked_targets, (mine - s) % scales, 0) for s in range(scales)], -1
    )

    mask_all = valid_mask.astype(f32)
    pixels = jnp.arange(held * width, dtype=jnp.int32)
    hits = jnp.sum((boxes[:, None] == pixels[None, :]).astype(f32), 0).reshape(held, width)
    packed = jnp.concatenate(
        [mask_all[None], (mask_all + box_weight * hits)[None], normal_targets], 0
    )
    packed_other = permute(packed, lay.swap(1))
    from_own = place // (scales // 2) == core
    packed = jnp.where(from_own, packed, packed_other)
    packed = lax.dynamic_slice_in_dim(packed, mine * rows, rows, 1)
    mask_f, weight = packed[0], packed[1]
    normals = jnp.moveaxis(packed[2:], 0, -1)
    count = jnp.full((8, 128), jnp.sum(mask_all), f32)
    bit = 1
    while bit < imgs:
        count = count + permute(count, lay.swap(bit))
        bit *= 2
    count = count[0, 0]

    current = x_zero
    kept = []
    result = None
    for depth_idx in range(depth):
        above = permute(current[rows - 1 :], lay.down())
        below = permute(current[:1], lay.up())
        padded = jnp.concatenate([above, current, below], 0)
        pre = conv_rows(padded, conv_bf16[depth_idx])
        result = activate(pre, affine_scale[depth_idx], affine_shift[depth_idx], col_mask)
        pair = jnp.stack([padded, permute(padded, lay.swap(1))])
        kept.append((pair, pre))
        current = result.astype(bf16)
    gamma = vectors[:chans]
    bias = vectors[chans:]
    tapped, tap_pull = jax.vjp(tap_norm, result, gamma)
    tapped_low = tapped.astype(bf16)

    tables = []
    for s in range(scales):
        tables.append(column_table(scale_cols[s], width, widths[s]))
        if s + 1 < scales:
            tables.append(jnp.zeros((GAP, width), f32))
    table = jnp.concatenate(tables, 0)
    table_high, table_low = halves(table)
    raised = jnp.einsum("ij,ric->rjc", table_high, tapped_low, preferred_element_type=f32)
    raised += jnp.einsum("ij,ric->rjc", table_low, tapped_low, preferred_element_type=f32)
    raised_high, raised_low = halves(raised)
    heads = head_bf16.transpose(1, 0, 2).reshape(chans, wide)
    joined = (
        jnp.einsum("rjc,ck->rjk", raised_high, heads, preferred_element_type=f32)
        + jnp.einsum("rjc,ck->rjk", raised_low, heads, preferred_element_type=f32)
        + scales * bias
    )

    def local_loss(joined_part):
        dense = 0.5 * jnp.sum(weight[:, :, None] * (joined_part - target.astype(f32)) ** 2)
        normal = cosine_terms(joined_part[:, :, 0:3], normals, mask_f)
        return ((dense / wide + normal) / count, jnp.stack([dense, normal]))

    loss_local, loss_pull, loss_parts = jax.vjp(local_loss, joined, has_aux=True)
    (grad_joined,) = loss_pull(jnp.ones_like(loss_local))
    grad_bias = scales * jnp.sum(grad_joined, (0, 1))
    grad_low = grad_joined.astype(bf16)
    grad_raised = jnp.einsum("rjk,ck->rjc", grad_low, heads, preferred_element_type=f32)
    grad_tapped = jnp.einsum(
        "ij,rjc->ric", table, grad_raised, precision=lax.Precision.HIGH
    )
    half_wide = wide // 2
    raised_pair = jnp.stack([raised_high, permute(raised_high, lay.swap(1))])
    grad_mine = lax.dynamic_slice_in_dim(grad_low, core * half_wide, half_wide, 2)
    grad_give = lax.dynamic_slice_in_dim(grad_low, (1 - core) * half_wide, half_wide, 2)
    grad_pair = jnp.stack([grad_mine, permute(grad_give, lay.swap(1))])
    head_grad = jnp.einsum("prjc,prjk->ck", raised_pair, grad_pair, preferred_element_type=f32)

    grad_result, grad_gamma = tap_pull(grad_tapped)
    half = chans // 2
    conv_grads = [None] * depth
    for depth_idx in reversed(range(depth)):
        pair, pre = kept[depth_idx]
        _, act_pull = jax.vjp(
            lambda value: activate(
                value, affine_scale[depth_idx], affine_shift[depth_idx], col_mask
            ),
            pre,
        )
        (grad_pre,) = act_pull(grad_result)
        grad_pre = grad_pre.astype(bf16)
        if depth_idx > 0:
            above = permute(grad_pre[rows - 1 :], lay.down())
            below = permute(grad_pre[:1], lay.up())
        grad_mine = lax.dynamic_slice_in_dim(grad_pre, core * half, half, 2)
        grad_give = lax.dynamic_slice_in_dim(grad_pre, (1 - core) * half, half, 2)
        grad_pair = jnp.stack([grad_mine, permute(grad_give, lay.swap(1))])
        conv_grads[depth_idx] = kernel_grad(pair, grad_pair)
        if depth_idx > 0:
            grad_padded = jnp.concatenate([above, grad_pre, below], 0)
            grad_result = conv_rows_back(grad_padded, conv_bf16[depth_idx])

    vec_rows = jnp.concatenate(
        [grad_gamma, grad_bias, loss_parts, jnp.zeros((-(chans + wide + 2) % 1024,), f32)]
    ).reshape(-1, 128)
    vec_sum = butterfly(vec_rows, lay).reshape(-1)
    grad_vec = vec_sum[: chans + wide]
    totals = vec_sum[chans + wide : chans + wide + 2]
    vec_squares = jnp.sum(grad_vec * grad_vec)

    blocks_count = owner_slot.shape[0]
    slots_here = master.shape[0]
    slots = slots_here * scales * imgs
    slot_ids = jnp.arange(slots, dtype=jnp.int32)
    match = slot_ids[:, None] == owner_slot[None, :]
    block_of = jnp.sum(
        jnp.where(match, jnp.arange(blocks_count, dtype=jnp.int32)[None, :], 0), 1
    )
    owned_f = jnp.any(match, 1).astype(f32)

    if imgs == 8 and scales == 4:
        x, y = (img // 2) % 2, img // 4
        where = (x, y, z)
        head_final = reduce_piece(head_grad[None], 4 * 128, where, lay)
        finals = [None] * depth
        for depth_idx in reversed(range(depth)):
            finals[depth_idx] = reduce_piece(conv_grads[depth_idx], half // 2, where, lay)
        conv_rows_final = jnp.stack([core_trade(v, core, lay) for v in finals])
        head_rows = core_trade(head_final, core, lay)
        fine_rows = conv_rows_final.shape[3]
        conv_blocks = conv_rows_final.transpose(0, 2, 1, 3, 4).reshape(-1, fine_rows, half)
        head_blocks = (
            head_rows[:, 0]
            .transpose(1, 0, 2)
            .reshape(fine_rows, heads_count, head_width)
            .transpose(1, 0, 2)
        )
        blocks = jnp.concatenate([conv_blocks, head_blocks], 0)
        squares = jnp.sum(blocks * blocks)
        by_slot = blocks[block_of] * owned_f[:, None, None]
        devices = scales * imgs
        top = jnp.max(jnp.abs(by_slot), 1)
        power = jnp.clip(jnp.ceil(jnp.log2(top)), -100.0, 110.0)
        step = jnp.exp2(-power) * CODE
        codes = jnp.clip(jnp.round(by_slot * step[:, None, :]), -CODE, CODE).astype(jnp.int16)
        codes = codes.reshape(devices, slots_here * fine_rows, half)
        powers = power.astype(jnp.int16).reshape(devices, slots_here, half)
        log_sq = jnp.log2(jnp.maximum(squares, 1e-37))
        sq_pow = jnp.floor(log_sq)
        mant = jnp.maximum(squares, 1e-37) * jnp.exp2(-sq_pow) * 8192.0
        mant_high = jnp.floor(mant)
        mant_low = jnp.floor((mant - mant_high) * 16384.0)
        sq_row = jnp.stack([sq_pow, mant_high, mant_low]).astype(jnp.int16)
        sq_row = jnp.broadcast_to(jnp.pad(sq_row, (0, half - 3))[None, None], (devices, 1, half))
        payload = jnp.concatenate([codes, powers, sq_row], 1)
        payload = jnp.pad(payload, ((0, 0), (0, -payload.shape[1] % 16), (0, 0)))
        got = lax.all_to_all(payload, AXES, 0, 0, tiled=True)
        code_rows = slots_here * fine_rows
        got_pow = got[:, code_rows : code_rows + slots_here].astype(f32)
        got_sq = got[:, code_rows + slots_here, 0:3].astype(f32)
        all_squares = (
            (got_sq[:, 1] + got_sq[:, 2] * (1.0 / 16384.0)) * (1.0 / 8192.0) * jnp.exp2(got_sq[:, 0])
        )
        squares_sum = jnp.sum(all_squares) + vec_squares
        values = got[:, :code_rows].reshape(devices, slots_here, fine_rows, half).astype(f32)
        values = values * (jnp.exp2(got_pow) * (1.0 / CODE))[:, :, None, :]
        owned = (
            values.reshape(scales, 2, 2, 2, slots_here, fine_rows, half)
            .transpose(4, 2, 1, 0, 3, 5, 6)
            .reshape(slots_here, chans, half)
        )
    else:
        both = []
        for depth_idx in range(depth):
            own_half = conv_grads[depth_idx]
            none = jnp.zeros_like(own_half)
            both.append(
                jnp.stack(
                    [jnp.where(core == 0, own_half, none), jnp.where(core == 1, own_half, none)], 1
                )
            )
        head_full = jnp.concatenate(
            [
                jnp.where(core == 0, head_grad, 0.0),
                jnp.where(core == 1, head_grad, 0.0),
            ],
            1,
        )
        blocks = jnp.concatenate(
            [v.reshape(-1, chans, half) for v in both]
            + [head_full.reshape(chans, heads_count, head_width).transpose(1, 0, 2)],
            0,
        )
        by_slot = blocks[block_of] * owned_f[:, None, None]
        owned = lax.psum_scatter(by_slot, AXES, scatter_dimension=0, tiled=True)
        squares_sum = lax.psum(jnp.sum(owned * owned), AXES) + vec_squares

    grad_norm = jnp.sqrt(squares_sum)
    factor = clip_level / jnp.maximum(grad_norm, clip_level)
    vec_new, vec_m_new, vec_v_new = vector_update(vectors, vec_m, vec_v, grad_vec * factor)
    master_new, slot_m_new, slot_v_new = soap_update(
        master, slot_m, slot_v, basis_left, basis_right, owned * factor
    )
    fresh = master_new.astype(bf16)
    every = lax.all_gather(fresh, AXES, axis=0, tiled=True)
    store = every[owner_slot]
    conv_copy, head_copy = from_blocks(store, depth, taps)
    loss = jnp.stack([totals[0] / wide + totals[1], count])
    return (
        loss,
        grad_norm,
        vec_new,
        vec_m_new,
        vec_v_new,
        master_new,
        slot_m_new,
        slot_v_new,
        conv_copy,
        head_copy,
    )


def solution(mesh):
    in_specs = (
        P("scale", "img", None, None),
        P("img", None),
        P(),
        P("img"),
        P(None, "img", None),
        P("img", None, "scale"),
        P(),
        P(),
        P(),
        P(),
        P(),
        P(),
        P(),
        P(("scale", "img"), None, None),
        P(("scale", "img"), None, None),
        P(("scale", "img"), None, None),
        P(("scale", "img"), None, None),
        P(("scale", "img"), None, None),
        P(),
    )
    out_specs = (
        P(),
        P(),
        P(),
        P(),
        P(),
        P(("scale", "img"), None, None),
        P(("scale", "img"), None, None),
        P(("scale", "img"), None, None),
        P(),
        P(),
    )
    return jax.shard_map(local, mesh=mesh, in_specs=in_specs, out_specs=out_specs, check_vma=False)
```

```python
import jax
import jax.numpy as jnp
from jax import lax
from jax.experimental import pallas as pl
from jax.experimental.pallas import tpu as pltpu
from jax.sharding import PartitionSpec as P

STEP = 5

beta_one = 0.5
beta_two = 0.5
adam_eps = 1e-08
rate_matrix = 0.01
rate_vector = 0.2
weight_decay = 0.01
clip_level = 0.001
box_weight = 2.0
norm_eps = 1e-05
highest = lax.Precision.HIGHEST
bf16 = jnp.bfloat16
f32 = jnp.float32
AXES = ("scale", "img")
GAP = 16
CODE = 32767.0
VMEM_BYTES = 56 * 2**20


class Layout:
    def __init__(self, scales, imgs):
        self.scales = scales
        self.imgs = imgs

    def pos(self, group, scale):
        return scale if group % 2 == 0 else self.scales - 1 - scale

    def dev(self, scale, img):
        return scale * self.imgs + img

    def at(self, group, place, core):
        return self.dev(self.pos(group, place), 2 * group + core)

    def all_devices(self):
        return [(s, i) for s in range(self.scales) for i in range(self.imgs)]

    def swap(self, bit):
        return [(self.dev(s, i), self.dev(s, i ^ bit)) for s, i in self.all_devices()]

    def turn(self, step):
        return [
            (self.dev(s, i), self.dev((s + step) % self.scales, i)) for s, i in self.all_devices()
        ]

    def scale_swap(self, bit):
        return [(self.dev(s, i), self.dev(s ^ bit, i)) for s, i in self.all_devices()]

    def rows_round(self, shift, sources):
        pairs = []
        for s in sources:
            for i in range(self.imgs):
                group, core = i // 2, i % 2
                piece = (shift + s) % self.scales
                place = (self.scales // 2) * core + piece // 2
                pairs.append((self.dev(s, i), self.at(group, place, piece % 2)))
        return pairs

    def row_order(self):
        groups = self.imgs // 2
        return [
            self.at(j, place, c) for j in range(groups) for place in range(self.scales) for c in range(2)
        ]

    def outward(self):
        order = self.row_order()
        pairs = []
        for at in range(1, len(order) - 1, 2):
            pairs += [(order[at], order[at + 1]), (order[at + 1], order[at])]
        return pairs


def permute(value, pairs):
    return lax.ppermute(value, AXES, pairs)


def after(value, *others):
    return lax.optimization_barrier((value, *others))[0]


def table_kernel(starts, widths, width, cols_ref, up_high, up_low, down_high, down_low):
    def table(shape, coarse_axis):
        place = lax.broadcasted_iota(jnp.int32, shape, coarse_axis)
        fine = lax.broadcasted_iota(jnp.int32, shape, 1 - coarse_axis)
        total = jnp.zeros(shape, f32)
        bits = (2 * width).bit_length() - 1
        for s, (start, span) in enumerate(zip(starts, widths)):
            columns = cols_ref[s]
            numer = jnp.maximum((2 * fine + 1) * columns - width, 0)
            lower = lax.shift_right_logical(numer, bits)
            frac = (numer - lax.shift_left(lower, bits)).astype(f32) * (0.5 / width)
            upper = jnp.minimum(lower + 1, columns - 1)
            coarse = place - start
            inside = (coarse >= 0) & (coarse < span)
            part = jnp.where(coarse == lower, 1.0 - frac, 0.0) + jnp.where(coarse == upper, frac, 0.0)
            total += jnp.where(inside, part, 0.0)
        return halves(total)

    up_high[...], up_low[...] = table(up_high.shape, 1)
    down_high[...], down_low[...] = table(down_high.shape, 0)


def table_call(scale_cols, starts, widths, width, cols):
    vmem = pl.BlockSpec(memory_space=pltpu.VMEM)
    return pl.pallas_call(
        lambda *refs: table_kernel(starts, widths, width, *refs),
        in_specs=[pl.BlockSpec(memory_space=pltpu.SMEM)],
        out_specs=[vmem] * 4,
        out_shape=[jax.ShapeDtypeStruct((width, cols), bf16)] * 2
        + [jax.ShapeDtypeStruct((cols, width), bf16)] * 2,
        name="tables",
    )(scale_cols)


def halves(value):
    high = value.astype(bf16)
    return high, (value - high.astype(f32)).astype(bf16)


def whole(shape):
    return pl.BlockSpec(shape, lambda *_: (0,) * len(shape))


def spread_taps(store, at, row, cols, chans):
    base = pl.multiple_of(at * cols, 16)
    value = row.astype(f32)
    store[pl.ds(base, cols), pl.ds(0, chans)] = pltpu.roll(value, 1, 0).astype(bf16)
    store[pl.ds(base, cols), pl.ds(chans, chans)] = row
    store[pl.ds(base, cols), pl.ds(2 * chans, chans)] = pltpu.roll(value, cols - 1, 0).astype(bf16)


def load_taps(rows, cols, chans, core, cur, partner, outer, taps):
    for r in range(rows):
        spread_taps(taps, r + 1, cur[pl.ds(r * cols, cols), :], cols, chans)
    outside = (rows + 1) * core
    spread_taps(taps, outside, outer[...], cols, chans)
    inside = pl.multiple_of((rows - 1) * core * cols, 16)
    spread_taps(taps, rows + 1 - outside, partner[pl.ds(inside, cols), :], cols, chans)


def fetch(source, layer, target, sems):
    copies = [pltpu.make_async_copy(source.at[layer, a], target.at[a], sems.at[a]) for a in range(3)]
    for copy in copies:
        copy.start()
    return copies


def conv_into(pre, taps, weights, copies, cols):
    size = pre.shape[0]
    for a in range(3):
        copies[a].wait()
        value = jnp.dot(taps[pl.ds(a * cols, size), :], weights[a], preferred_element_type=f32)
        if a == 0:
            pre[...] = value
        else:
            pre[...] += value


def gelu_slope(u):
    root = 0.7978845608028654
    bend = 0.044715
    th = jnp.tanh(root * (u + bend * u * u * u))
    return 0.5 * (1.0 + th) + 0.5 * u * (1.0 - th * th) * root * (1.0 + 3.0 * bend * u * u)


def first_conv_kernel(
    rows, cols, chans, layer, core_ref, cur, partner, outer, gain, shift, mask, w_hbm, pre, out, taps, w, sems
):
    copies = fetch(w_hbm, layer, w, sems)
    load_taps(rows, cols, chans, core_ref[0], cur, partner, outer, taps)
    out[pl.ds(0, cols), :] = outer[...]
    conv_into(pre, taps, w, copies, cols)

    def body(i, carry):
        at = pl.ds(pl.multiple_of(i * 32, 32), 32)
        u = pre[at, :] * gain[...] + shift[...]
        to = pl.ds(pl.multiple_of(cols + i * 32, 32), 32)
        out[to, :] = (jax.nn.gelu(u) * mask[at, :]).astype(bf16)
        return carry

    lax.fori_loop(0, rows * cols // 32, body, 0)


def back_conv_kernel(
    rows, cols, chans, layer, core_ref, cur, partner, outer, gain, shift, mask, pre_in, w_hbm, out, taps, w, sems, acc
):
    copies = fetch(w_hbm, layer, w, sems)
    size = rows * cols
    cur = cur.at[pl.ds(cols, size)]
    partner = partner.at[pl.ds(cols, size)]
    load_taps(rows, cols, chans, core_ref[0], cur, partner, outer, taps)
    for a in range(3):
        copies[2 - a].wait()
        value = 0.0
        for b in range(3):
            value += lax.dot_general(
                taps[pl.ds(a * cols, size), b * chans : (b + 1) * chans],
                w[2 - a, (2 - b) * chans : (3 - b) * chans, :],
                (((1,), (1,)), ((), ())),
                preferred_element_type=f32,
            )
        if a == 0:
            acc[...] = value
        else:
            acc[...] += value

    def body(i, carry):
        at = pl.ds(pl.multiple_of(i * 32, 32), 32)
        u = pre_in[at, :] * gain[...] + shift[...]
        out[at, :] = (acc[at, :] * mask[at, :] * gelu_slope(u) * gain[...]).astype(bf16)
        return carry

    lax.fori_loop(0, size // 32, body, 0)


def conv_call(kernel, core, cur, partner, outer, gain, shift, mask, more, weights, layer, shapes, acc, name):
    cols, chans = outer.shape
    rows = 2
    size = rows * cols
    scratch = [
        pltpu.VMEM(((rows + 2) * cols, 3 * chans), bf16),
        pltpu.VMEM((3, 3 * chans, chans), bf16),
        pltpu.SemaphoreType.DMA((3,)),
    ]
    if acc:
        scratch.append(pltpu.VMEM((size, chans), f32))
    vmem = pl.BlockSpec(memory_space=pltpu.VMEM)
    return pl.pallas_call(
        lambda *refs: kernel(rows, cols, chans, layer, *refs),
        in_specs=[pl.BlockSpec(memory_space=pltpu.SMEM)]
        + [vmem] * (6 + len(more))
        + [pl.BlockSpec(memory_space=pl.ANY)],
        out_specs=[vmem for _ in shapes],
        out_shape=shapes,
        scratch_shapes=scratch,
        compiler_params=pltpu.CompilerParams(vmem_limit_bytes=VMEM_BYTES),
        cost_estimate=pl.CostEstimate(flops=1, bytes_accessed=1, transcendentals=0),
        name=name,
    )(core, cur, partner, outer, gain, shift, mask, *more, weights)


def head_kernel(
    rows,
    cols,
    width,
    scales,
    layer,
    core_ref,
    mine_ref,
    cur,
    partner,
    outer,
    gain,
    shift,
    mask,
    gamma,
    bias,
    weight,
    valid,
    normals,
    heads_hbm,
    first_hbm,
    second_hbm,
    third_hbm,
    fourth_hbm,
    up_high_hbm,
    up_low_hbm,
    down_high_hbm,
    down_low_hbm,
    w_hbm,
    out,
    mine,
    pack,
    dgamma,
    dbias,
    sums,
    taps,
    w,
    sems,
    pre,
    y_ref,
    tapped,
    raised_high,
    raised_low,
    dj_low,
    back,
    target,
    heads,
    target_in,
    up_high,
    up_low,
    down_high,
    down_low,
    more_sems,
    target_sems,
):
    chans = outer.shape[1]
    size = rows * cols
    core = core_ref[0]
    copies = fetch(w_hbm, layer, w, sems)
    pairs = (
        (up_high_hbm, up_high),
        (up_low_hbm, up_low),
        (heads_hbm, heads),
        (down_high_hbm, down_high),
        (down_low_hbm, down_low),
    )
    loads = [pltpu.make_async_copy(a, b, more_sems.at[i]) for i, (a, b) in enumerate(pairs)]
    for load in loads:
        load.start()
    arrived = (first_hbm, second_hbm, third_hbm, fourth_hbm)
    for s in range(scales):
        for k in range(scales):

            @pl.when(lax.rem(mine_ref[0] - s - k + 2 * scales, scales) == 0)
            def _(s=s, k=k):
                pltpu.make_async_copy(arrived[k], target_in.at[s], target_sems.at[s]).start()

    cur = cur.at[pl.ds(cols, size)]
    partner = partner.at[pl.ds(cols, size)]
    load_taps(rows, cols, chans, core, cur, partner, outer, taps)
    out[pl.ds(0, cols), :] = outer[...]
    conv_into(pre, taps, w, copies, cols)

    def forward(i, carry):
        at = pl.ds(pl.multiple_of(i * 32, 32), 32)
        u = pre[at, :] * gain[...] + shift[...]
        y = jax.nn.gelu(u) * mask[at, :]
        y_ref[at, :] = y
        scale = lax.rsqrt(jnp.mean(y * y, -1, keepdims=True) + norm_eps)
        tapped[at, :] = (gamma[...] * y * scale).astype(bf16)
        return carry

    lax.fori_loop(0, size // 32, forward, 0)
    for load in loads:
        load.wait()
    for s in range(scales):
        pltpu.make_async_copy(arrived[s], target_in.at[s], target_sems.at[s]).wait()
    part = target_in.shape[2]
    for s in range(scales):
        target[:, s * part : (s + 1) * part] = target_in[s]

    half_wide = mine.shape[1]
    for r in range(rows):
        line = tapped[pl.ds(r * cols, cols), :]
        value = jnp.dot(up_high[...], line, preferred_element_type=f32)
        value += jnp.dot(up_low[...], line, preferred_element_type=f32)
        high = value.astype(bf16)
        raised_high[pl.ds(r * width, width), :] = high
        pack[pl.ds(r * width, width), pl.ds(half_wide, chans)] = high
        raised_low[pl.ds(r * width, width), :] = (value - high.astype(f32)).astype(bf16)

    step = heads.shape[2]
    wide = heads.shape[0] * step
    dense = jnp.zeros((1, step), f32)
    normal = jnp.zeros((1, 1), f32)
    for t in range(wide // step):
        joined = jnp.dot(raised_high[...], heads[t], preferred_element_type=f32)
        joined += jnp.dot(raised_low[...], heads[t], preferred_element_type=f32)
        joined += float(scales) * bias[:, t * step : (t + 1) * step]
        diff = joined - target[:, t * step : (t + 1) * step].astype(f32)
        pulled = weight[...] * diff
        dense += jnp.sum(pulled * diff, 0, keepdims=True)
        grad = pulled * (1.0 / wide)
        if t == 0:
            lane = lax.broadcasted_iota(jnp.int32, (joined.shape[0], 128), 1)
            n = jnp.where(lane < 3, joined[:, :128], 0.0)
            other = normals[...]
            inner = jnp.sum(n * other, -1, keepdims=True)
            own_sq = jnp.sum(n * n, -1, keepdims=True) + 1.0
            other_sq = jnp.sum(other * other, -1, keepdims=True) + 1.0
            root = lax.rsqrt(own_sq * other_sq)
            normal += jnp.sum(valid[...] * (1.0 - inner * root), 0, keepdims=True)
            turn = valid[...] * root * (inner / own_sq * n - other)
            grad = jnp.concatenate([grad[:, :128] + turn, grad[:, 128:]], 1)
        dbias[:, t * step : (t + 1) * step] = float(scales) * jnp.sum(grad, 0, keepdims=True)
        dj_low[:, t * step : (t + 1) * step] = grad.astype(bf16)
        half = step // 2
        first, second = grad[:, :half], grad[:, half:]
        mine[:, t * half : (t + 1) * half] = jnp.where(core == 0, first, second).astype(bf16)
        pack[:, t * half : (t + 1) * half] = jnp.where(core == 0, second, first).astype(bf16)
    lane = lax.broadcasted_iota(jnp.int32, (1, 128), 1)
    total = 0.5 * jnp.sum(dense, 1, keepdims=True)
    sums[...] = jnp.where(lane == 0, total, jnp.where(lane == 1, normal, 0.0))

    draised = 0.0
    for t in range(heads.shape[0]):
        draised += lax.dot_general(
            dj_low[:, t * step : (t + 1) * step],
            heads[t],
            (((1,), (1,)), ((), ())),
            preferred_element_type=f32,
        )
    for r in range(rows):
        part = draised[r * width : (r + 1) * width]
        high = part.astype(bf16)
        low = (part - high.astype(f32)).astype(bf16)
        value = jnp.dot(down_high[...], high, preferred_element_type=f32)
        value += jnp.dot(down_low[...], high, preferred_element_type=f32)
        value += jnp.dot(down_high[...], low, preferred_element_type=f32)
        back[pl.ds(r * cols, cols), :] = value

    def backward(i, carry):
        at = pl.ds(pl.multiple_of(i * 32, 32), 32)
        y = y_ref[at, :]
        dt = back[at, :]
        scale = lax.rsqrt(jnp.mean(y * y, -1, keepdims=True) + norm_eps)
        dty = dt * y
        pull = jnp.mean(gamma[...] * dty, -1, keepdims=True)
        dy = gamma[...] * dt * scale - y * (scale * scale * scale * pull)
        u = pre[at, :] * gain[...] + shift[...]
        to = pl.ds(pl.multiple_of(cols + i * 32, 32), 32)
        out[to, :] = (dy * mask[at, :] * gelu_slope(u) * gain[...]).astype(bf16)
        return carry + jnp.sum(dty * scale, 0, keepdims=True)

    dgamma[...] = lax.fori_loop(0, size // 32, backward, jnp.zeros((1, chans), f32))


def head_call(core, mine, cur, partner, outer, vectors, pixel, heads, target, tables, weights, layer):
    cols, chans = outer.shape
    rows = 2
    size = rows * cols
    width = tables[0].shape[0]
    wide = heads.shape[0] * heads.shape[2]
    pixels = rows * width
    scales = len(target)
    vmem = pl.BlockSpec(memory_space=pltpu.VMEM)
    anywhere = pl.BlockSpec(memory_space=pl.ANY)
    shapes = [
        jax.ShapeDtypeStruct((size + cols, chans), bf16),
        jax.ShapeDtypeStruct((pixels, wide // 2), bf16),
        jax.ShapeDtypeStruct((pixels, wide // 2 + chans), bf16),
        jax.ShapeDtypeStruct((1, chans), f32),
        jax.ShapeDtypeStruct((1, wide), f32),
        jax.ShapeDtypeStruct((1, 128), f32),
    ]
    return pl.pallas_call(
        lambda *refs: head_kernel(rows, cols, width, scales, layer, *refs),
        in_specs=[pl.BlockSpec(memory_space=pltpu.SMEM)] * 2 + [vmem] * 11 + [anywhere] * (6 + scales),
        out_specs=[vmem for _ in shapes],
        out_shape=shapes,
        scratch_shapes=[
            pltpu.VMEM(((rows + 2) * cols, 3 * chans), bf16),
            pltpu.VMEM((3, 3 * chans, chans), bf16),
            pltpu.SemaphoreType.DMA((3,)),
            pltpu.VMEM((size, chans), f32),
            pltpu.VMEM((size, chans), f32),
            pltpu.VMEM((size, chans), bf16),
            pltpu.VMEM((pixels, chans), bf16),
            pltpu.VMEM((pixels, chans), bf16),
            pltpu.VMEM((pixels, wide), bf16),
            pltpu.VMEM((size, chans), f32),
            pltpu.VMEM((pixels, wide), bf16),
            pltpu.VMEM(heads.shape, bf16),
            pltpu.VMEM((scales, *target[0].shape), bf16),
        ]
        + [pltpu.VMEM(table.shape, bf16) for table in tables]
        + [pltpu.SemaphoreType.DMA((5,)), pltpu.SemaphoreType.DMA((scales,))],
        compiler_params=pltpu.CompilerParams(vmem_limit_bytes=VMEM_BYTES),
        cost_estimate=pl.CostEstimate(flops=1, bytes_accessed=1, transcendentals=0),
        name="head_rows",
    )(core, mine, cur, partner, outer, *vectors, *pixel, heads, *target, *tables, weights)


def kernel_grad_kernel(
    rows, cols, chans, part, x_at, g_at, core_ref, cur, partner, outer, far, g_own, g_far, out, taps, grads
):
    step = pl.program_id(0)
    core = core_ref[0]
    size = rows * cols

    @pl.when(step == 0)
    def _():
        own_at = 1 + rows * core
        far_at = 1 + rows * (1 - core)
        for r in range(rows):
            at = pl.ds(x_at + r * cols, cols)
            spread_taps(taps, own_at + r, cur[at, :], cols, chans)
            spread_taps(taps, far_at + r, partner[at, :], cols, chans)
        spread_taps(taps, (2 * rows + 1) * core, outer[...], cols, chans)
        spread_taps(taps, (2 * rows + 1) * (1 - core), far[...], cols, chans)
        for h in range(grads.shape[1] // part):
            lanes = pl.ds(pl.multiple_of((2 * h + core) * part, part), part)
            own_rows = pl.ds(pl.multiple_of(core * size, 16), size)
            far_rows = pl.ds(pl.multiple_of((1 - core) * size, 16), size)
            grads[own_rows, h * part : (h + 1) * part] = g_own[pl.ds(g_at, size), lanes]
            grads[far_rows, h * part : (h + 1) * part] = g_far[pl.ds(g_at, size), lanes]

    window = taps[pl.ds(pl.multiple_of(step * cols, 16), 2 * size), :]
    value = lax.dot_general(
        grads[...], window, (((0,), (0,)), ((), ())), preferred_element_type=f32
    )
    for b in range(3):
        out[b] = value[:, b * chans : (b + 1) * chans]


def kernel_grad(core, cur, partner, outer, far, g_own, g_far, part):
    cols, chans = outer.shape
    rows = 2
    size = rows * cols
    outs = g_own.shape[1] // 2
    x_at, g_at = cur.shape[0] - size, g_own.shape[0] - size
    return pl.pallas_call(
        lambda *refs: kernel_grad_kernel(rows, cols, chans, part, x_at, g_at, *refs),
        grid=(3,),
        in_specs=[
            pl.BlockSpec(memory_space=pltpu.SMEM),
            whole(cur.shape),
            whole(cur.shape),
            whole((cols, chans)),
            pl.BlockSpec((cols, chans), lambda i: (0, 0)),
            whole(g_own.shape),
            whole(g_own.shape),
        ],
        out_specs=pl.BlockSpec((3, outs, chans), lambda i: (i, 0, 0)),
        out_shape=jax.ShapeDtypeStruct((9, outs, chans), f32),
        scratch_shapes=[
            pltpu.VMEM(((2 * rows + 2) * cols, 3 * chans), bf16),
            pltpu.VMEM((2 * size, outs), bf16),
        ],
        compiler_params=pltpu.CompilerParams(vmem_limit_bytes=VMEM_BYTES),
        cost_estimate=pl.CostEstimate(flops=1, bytes_accessed=1, transcendentals=0),
        name="kernel_grad",
    )(core, cur, partner, outer, far, g_own, g_far)


def head_grad_kernel(mine, own, got, out):
    half = mine.shape[1]
    dims = (((0,), (0,)), ((), ()))
    value = lax.dot_general(mine[...], own[:, half:], dims, preferred_element_type=f32)
    out[...] = value + lax.dot_general(
        got[:, :half], got[:, half:], dims, preferred_element_type=f32
    )


def head_grad_call(mine, own, got):
    vmem = pl.BlockSpec(memory_space=pltpu.VMEM)
    half = mine.shape[1]
    chans = own.shape[1] - half
    return pl.pallas_call(
        head_grad_kernel,
        in_specs=[vmem] * 3,
        out_specs=vmem,
        out_shape=jax.ShapeDtypeStruct((half, chans), f32),
        compiler_params=pltpu.CompilerParams(vmem_limit_bytes=VMEM_BYTES),
        cost_estimate=pl.CostEstimate(flops=1, bytes_accessed=1, transcendentals=0),
        name="head_grad",
    )(mine, own, got)


def coded(value):
    top = jnp.max(jnp.abs(value), 0, keepdims=True)
    power = jnp.clip(jnp.ceil(jnp.log2(top)), -100.0, 110.0)
    codes = jnp.clip(jnp.round(value * (jnp.exp2(-power) * CODE)), -CODE, CODE)
    return codes.astype(jnp.int32), power.astype(jnp.int32)


def route_kernel(devices, here, block_of, blocks, out):
    lanes = 128
    groups = blocks.shape[2] // lanes
    unit = groups * blocks.shape[1]
    total = jnp.zeros(blocks.shape[1:], f32)
    for b in range(blocks.shape[0]):
        total += blocks[b] * blocks[b]
    squares = jnp.maximum(jnp.sum(jnp.sum(total, 0, keepdims=True), 1, keepdims=True), 1e-37)
    sq_pow = jnp.floor(jnp.log2(squares))
    mant = squares * jnp.exp2(-sq_pow) * 8192.0
    mant_high = jnp.floor(mant)
    mant_low = jnp.floor((mant - mant_high) * 16384.0)
    row = lax.broadcasted_iota(jnp.int32, (16, lanes), 0)
    lane = lax.broadcasted_iota(jnp.int32, (16, lanes), 1)
    base = jnp.where(lane == 0, sq_pow, jnp.where(lane == 1, mant_high, mant_low)).astype(jnp.int32)
    base = jnp.where(row == here, base, 0)

    def body(d, carry):
        tail = base
        for k in range(here):
            b = block_of[here * d + k]
            value = blocks[jnp.maximum(b, 0)] * (b >= 0).astype(f32)
            value = jnp.concatenate(
                [value[:, g * lanes : (g + 1) * lanes] for g in range(groups)], 0
            )
            codes, power = coded(value)
            out[d, pl.ds(k * unit, unit), :] = codes.astype(jnp.int16)
            tail = jnp.where(row == k, power, tail)
        out[d, pl.ds(here * unit, 16), :] = tail.astype(jnp.int16)
        return carry

    lax.fori_loop(0, devices, body, 0, unroll=4)


def route_call(blocks, block_of, devices):
    here = block_of.shape[0] // devices
    rows = here * blocks.shape[1] * blocks.shape[2] // 128 + 16
    vmem = pl.BlockSpec(memory_space=pltpu.VMEM)
    return pl.pallas_call(
        lambda *refs: route_kernel(devices, here, *refs),
        in_specs=[pl.BlockSpec(memory_space=pltpu.SMEM), vmem],
        out_specs=vmem,
        out_shape=jax.ShapeDtypeStruct((devices, rows, 128), jnp.int16),
        compiler_params=pltpu.CompilerParams(vmem_limit_bytes=VMEM_BYTES),
        name="route",
    )(block_of, blocks)


def dot_split(a, b, dims):
    dims = (dims, ((), ()))
    value = lax.dot_general(a[0], b[0], dims, preferred_element_type=f32)
    value += lax.dot_general(a[1], b[0], dims, preferred_element_type=f32)
    return value + lax.dot_general(a[0], b[1], dims, preferred_element_type=f32)


def update_kernel(
    starts, scalars, got, master, moment, second, left, right, master_new, moment_new, second_new, fresh, norm, grads, sums
):
    here, chans, half = master.shape
    lanes = 128
    groups = chans // lanes
    unit = (got.shape[1] - 16) // here
    fine = unit // groups
    for d, start in enumerate(starts):
        tail = got[d, pl.ds(here * unit, 16), :].astype(jnp.int32).astype(f32)
        sums[pl.ds(d, 1), :] = tail[here : here + 1]
        for k in range(here):
            value = got[d, pl.ds(k * unit, unit), :].astype(jnp.int32).astype(f32)
            value = value * (jnp.exp2(tail[k : k + 1]) * (1.0 / CODE))
            for g in range(groups):
                grads[k, pl.ds(start, fine), g * lanes : (g + 1) * lanes] = value[g * fine : (g + 1) * fine]
    rows = sums[...]
    lane = lax.broadcasted_iota(jnp.int32, rows.shape, 1)

    def column(index):
        return jnp.sum(jnp.where(lane == index, rows, 0.0), 1, keepdims=True)

    squares = (column(1) + column(2) * (1.0 / 16384.0)) * (1.0 / 8192.0) * jnp.exp2(column(0))
    squares = jnp.sum(squares, 0, keepdims=True) + scalars[0]
    grad_norm = jnp.sqrt(squares) / scalars[1]
    factor = clip_level / jnp.maximum(grad_norm, clip_level) / scalars[1]
    place = lax.broadcasted_iota(jnp.int32, (1, lanes), 1)
    norm[...] = jnp.where(place == 0, grad_norm, factor)
    for k in range(here):
        side = halves(left[k])
        other = halves(right[k])
        turned = dot_split(side, halves(grads[k]), ((0,), (1,)))
        turned = dot_split(halves(turned), other, ((1,), (0,))) * factor
        first = beta_one * moment[k] + (1.0 - beta_one) * turned
        spread = beta_two * second[k] + (1.0 - beta_two) * turned * turned
        moment_new[k] = first
        second_new[k] = spread
        ratio = (first / (1.0 - beta_one**STEP)) / (jnp.sqrt(spread / (1.0 - beta_two**STEP)) + adam_eps)
        back = dot_split(side, halves(ratio), ((1,), (0,)))
        back = dot_split(halves(back), other, ((1,), (1,)))
        value = master[k] - rate_matrix * (back + weight_decay * master[k])
        master_new[k] = value
        fresh[k] = value.astype(bf16)


def update_call(scalars, got, starts, master, moment, second, left, right):
    vmem = pl.BlockSpec(memory_space=pltpu.VMEM)
    here, chans, half = master.shape
    like = jax.ShapeDtypeStruct(master.shape, f32)
    return pl.pallas_call(
        lambda *refs: update_kernel(starts, *refs),
        in_specs=[pl.BlockSpec(memory_space=pltpu.SMEM)] + [vmem] * 6,
        out_specs=[vmem] * 5,
        out_shape=[
            like,
            like,
            like,
            jax.ShapeDtypeStruct(master.shape, bf16),
            jax.ShapeDtypeStruct((1, 128), f32),
        ],
        scratch_shapes=[
            pltpu.VMEM((here, half, chans), f32),
            pltpu.VMEM((len(starts), 128), f32),
        ],
        compiler_params=pltpu.CompilerParams(vmem_limit_bytes=VMEM_BYTES),
        name="update",
    )(scalars, got, master, moment, second, left, right)


def place_kernel(depth, taps, half, arrays, array, item, *refs):
    sources = refs[:arrays]
    conv, head, conv_store, head_store, in_sems, out_sems = refs[arrays:]
    blocks = array.shape[0]
    count = 2 * depth * taps

    def load(b, source):
        if b < count:
            target = conv_store.at[b // 2, :, pl.ds((b % 2) * half, half)]
        else:
            target = head_store.at[b - count]
        return pltpu.make_async_copy(source, target, in_sems.at[b])

    for b in range(blocks):
        for g in range(arrays):

            @pl.when(array[b] == g)
            def _(b=b, g=g):
                load(b, sources[g].at[item[b]]).start()

    stores = []
    for b in range(blocks):
        load(b, sources[0].at[0]).wait()
        if b >= count:
            stores.append(
                pltpu.make_async_copy(
                    head_store.at[b - count], head.at[b - count], out_sems.at[len(stores)]
                )
            )
            stores[-1].start()
        elif b % 2 == 1:
            tap = b // 2
            stores.append(
                pltpu.make_async_copy(
                    conv_store.at[tap], conv.at[tap // taps, tap % taps], out_sems.at[len(stores)]
                )
            )
            stores[-1].start()
    for store in stores:
        store.wait()


def place_blocks(sources, array, item, depth, taps):
    blocks = array.shape[0]
    chans, half = sources[0].shape[1:]
    heads = blocks - 2 * depth * taps
    anywhere = pl.BlockSpec(memory_space=pl.ANY)
    smem = pl.BlockSpec(memory_space=pltpu.SMEM)
    return pl.pallas_call(
        lambda *refs: place_kernel(depth, taps, half, len(sources), *refs),
        in_specs=[smem, smem] + [anywhere] * len(sources),
        out_specs=[anywhere, anywhere],
        out_shape=[
            jax.ShapeDtypeStruct((depth, taps, chans, 2 * half), bf16),
            jax.ShapeDtypeStruct((heads, chans, half), bf16),
        ],
        scratch_shapes=[
            pltpu.VMEM((depth * taps, chans, 2 * half), bf16),
            pltpu.VMEM((heads, chans, half), bf16),
            pltpu.SemaphoreType.DMA((blocks,)),
            pltpu.SemaphoreType.DMA((depth * taps + heads,)),
        ],
        compiler_params=pltpu.CompilerParams(vmem_limit_bytes=VMEM_BYTES),
        name="place_blocks",
    )(array, item, *sources)


def spread_slots(own, lay, z, beside):
    def line(value, pairs):
        return permute(
            value, [(lay.dev(a, i), lay.dev(b, i)) for a, b in pairs for i in range(lay.imgs)]
        )

    def over_x(value):
        return permute(value, lay.swap(2))

    def over_y(value):
        return permute(value, lay.swap(4))

    inner = (z == 1) | (z == 2)
    z_one = line(own, [(0, 1), (1, 0), (2, 3), (3, 2)])
    x_own = over_x(own)
    y_own = over_y(own)
    middle_own = line(own, [(1, 2), (2, 1)])
    middle_one = line(z_one, [(1, 2), (2, 1)])
    xy_own = over_x(y_own)
    y_one = over_y(z_one)
    outer_own = line(middle_own, [(1, 0), (2, 3)])
    outer_one = line(middle_one, [(1, 0), (2, 3)])
    z_two = jnp.where(inner, middle_one, outer_own)
    x_one = over_x(z_one)
    y_two = over_y(after(z_two, *beside))
    x_two = over_x(z_two)
    z_three = jnp.where(inner, middle_own, outer_one)
    xy_one = over_y(x_one)
    y_three = over_y(z_three)
    x_three = over_x(z_three)
    xy_three = over_y(x_three)
    xy_two = over_x(y_two)
    bundles = [
        jnp.concatenate(v, 0)
        for v in (
            (own, z_one, x_own, y_own),
            (z_two, z_three, xy_own, x_one),
            (y_one, x_two, y_two, xy_one),
            (x_three, y_three, xy_two, xy_three),
        )
    ]
    return bundles + [permute(v, lay.swap(1)) for v in bundles]


PLACES = (0, 1, 4, 5, 3, 8, 10, 13, 2, 7, 9, 12, 6, 11, 14, 15)


def encode(value):
    n, r, cols = value.shape
    top = jnp.max(jnp.abs(value), 1)
    power = jnp.clip(jnp.ceil(jnp.log2(top)), -100.0, 110.0)
    step = jnp.exp2(-power) * CODE
    codes = jnp.clip(jnp.round(value * step[:, None, :]), -CODE, CODE).astype(jnp.int16)
    pad = -n % 16
    powers = jnp.pad(power.astype(jnp.int16), ((0, pad), (0, 0)))
    return jnp.concatenate([codes.reshape(n * r, cols), powers], 0)


def decode(rows, n):
    pad = -n % 16
    total, cols = rows.shape
    r = (total - n - pad) // n
    power = rows[n * r : n * r + n].astype(f32)
    step = jnp.exp2(power) * (1.0 / CODE)
    return rows[: n * r].reshape(n, r, cols).astype(f32) * step[:, None, :]


def pick(value, index, axis):
    return lax.dynamic_index_in_dim(value, index, axis, keepdims=False)


class Sum:
    def __init__(self, parts, place, lay):
        self.x, self.y, self.z = place
        self.lay = lay
        self.counts = [part.shape[0] for part in parts]
        self.rows, cols = parts[0].shape[1:]
        self.w = cols // 2
        quarter = self.rows // 4
        self.va, self.vb = [], []
        sends = ([], [])
        for part in parts:
            n = part.shape[0]
            v = part.reshape(n, 2, 2, quarter, cols)
            va, vb = v[..., : self.w], v[..., self.w :]
            shape = (n, 2 * quarter, self.w)
            sends[0].append(encode(pick(va, 1 - self.x, 1).reshape(shape)))
            sends[1].append(encode(pick(vb, 1 - self.y, 2).reshape(shape)))
            self.va.append(va)
            self.vb.append(vb)
        self.send = [jnp.concatenate(send, 0) if len(send) > 1 else send[0] for send in sends]

    def split(self, rows_sent, r):
        at = 0
        out = []
        for n in self.counts:
            size = n * r + n + (-n % 16)
            out.append(decode(rows_sent[at : at + size], n))
            at += size
        return out

    def first(self):
        self.got = [permute(self.send[0], self.lay.swap(2)), permute(self.send[1], self.lay.swap(4))]

    def second(self, *wait):
        got = lax.optimization_barrier((*self.got, *wait))
        quarter = self.rows // 4
        got_a, got_b = self.split(got[0], 2 * quarter), self.split(got[1], 2 * quarter)
        send_a, send_b, self.keep = [], [], []
        for n, va, vb, ga, gb in zip(self.counts, self.va, self.vb, got_a, got_b):
            keep_a = pick(va, self.x, 1) + ga.reshape(n, 2, quarter, self.w)
            keep_b = pick(vb, self.y, 2) + gb.reshape(n, 2, quarter, self.w)
            send_a.append(encode(pick(keep_a, 1 - self.y, 1)))
            send_b.append(encode(pick(keep_b, 1 - self.x, 1)))
            self.keep.append((pick(keep_a, self.y, 1), pick(keep_b, self.x, 1)))
        self.send = [jnp.concatenate(v, 0) if len(v) > 1 else v[0] for v in (send_a, send_b)]
        self.got = [permute(self.send[0], self.lay.swap(4)), permute(self.send[1], self.lay.swap(2))]

    def third(self, *wait):
        got = lax.optimization_barrier((*self.got, *wait))
        quarter = self.rows // 4
        got_a, got_b = self.split(got[0], quarter), self.split(got[1], quarter)
        return [
            jnp.concatenate([keep_a + ga, keep_b + gb], -1)
            for (keep_a, keep_b), ga, gb in zip(self.keep, got_a, got_b)
        ]


def line_sum(keeps, scales):
    keep = jnp.concatenate(keeps, 0) if len(keeps) > 1 else keeps[0]
    n, rows, cols = keep.shape
    r = rows // scales
    keep = keep.reshape(n, scales, r, cols)
    top = jnp.max(jnp.abs(keep), 2)
    power = jnp.clip(jnp.ceil(jnp.log2(top)), -100.0, 110.0)
    step = jnp.exp2(-power) * CODE
    codes = jnp.clip(jnp.round(keep * step[:, :, None, :]), -CODE, CODE).astype(jnp.int16)
    codes = codes.transpose(1, 0, 2, 3).reshape(scales, n * r, cols)
    powers = jnp.pad(power.astype(jnp.int16).transpose(1, 0, 2), ((0, 0), (0, -n % 16), (0, 0)))
    got = lax.all_to_all(jnp.concatenate([codes, powers], 1), "scale", 0, 0, tiled=True)
    values = got[:, : n * r].reshape(scales, n, r, cols).astype(f32)
    step = jnp.exp2(got[:, n * r : n * r + n].astype(f32)) * (1.0 / CODE)
    return jnp.sum(values * step[:, :, None, :], 0)


def soap_update(master, moment, second, left, right, grads):
    turned = jnp.einsum("sij,ski->sjk", left, grads, precision=highest)
    turned = jnp.einsum("sjk,skl->sjl", turned, right, precision=highest)
    moment = beta_one * moment + (1.0 - beta_one) * turned
    second = beta_two * second + (1.0 - beta_two) * turned * turned
    ratio = moment / (1.0 - beta_one**STEP) / (jnp.sqrt(second / (1.0 - beta_two**STEP)) + adam_eps)
    back = jnp.einsum("sij,sjk->sik", left, ratio, precision=highest)
    back = jnp.einsum("sik,slk->sil", back, right, precision=highest)
    return (master - rate_matrix * (back + weight_decay * master), moment, second)


def vector_update(params, moment, second, grads):
    moment = beta_one * moment + (1.0 - beta_one) * grads
    second = beta_two * second + (1.0 - beta_two) * grads * grads
    ratio = moment / (1.0 - beta_one**STEP) / (jnp.sqrt(second / (1.0 - beta_two**STEP)) + adam_eps)
    return (params - rate_vector * (ratio + weight_decay * params), moment, second)


def butterfly(value, lay):
    bit = 1
    while bit < lay.imgs:
        value = value + permute(value, lay.swap(bit))
        bit *= 2
    bit = 1
    while bit < lay.scales:
        value = value + permute(value, lay.scale_swap(bit))
        bit *= 2
    return value


def local(
    images,
    valid_mask,
    scale_cols,
    boxes,
    normal_targets,
    dense_targets,
    affine_scale,
    affine_shift,
    conv_bf16,
    head_bf16,
    vectors,
    vec_m,
    vec_v,
    master,
    slot_m,
    slot_v,
    basis_left,
    basis_right,
    owner_slot,
):
    held, width, chans = (images.shape[1], images.shape[2], images.shape[3])
    heads_count, head_width = (head_bf16.shape[0], head_bf16.shape[2])
    wide = heads_count * head_width
    depth, taps = (conv_bf16.shape[0], conv_bf16.shape[1])
    scales, imgs = lax.axis_size("scale"), lax.axis_size("img")
    lay = Layout(scales, imgs)
    rows = held // scales
    z = lax.axis_index("scale")
    img = lax.axis_index("img")
    group, core = img // 2, img % 2
    place = jnp.where(group % 2 == 0, z, scales - 1 - z)
    mine = 2 * (place % 2) + core

    widths = [width >> s for s in range(scales)]
    starts = []
    at = 0
    for w in widths:
        starts.append(at)
        at += w + GAP
    cols = at
    col_iota = jnp.arange(cols, dtype=jnp.int32)
    valid_col = jnp.zeros((cols,), jnp.bool_)
    for s in range(scales):
        valid_col |= (col_iota >= starts[s]) & (col_iota < starts[s] + scale_cols[s])
    col_mask = valid_col.astype(f32)[None, :, None]

    own = images[0]
    fine = [
        permute(own[rows * k : rows * (k + 1)], lay.rows_round(k, [0])) for k in range(scales)
    ]
    coarse = []
    for k in range(scales):
        piece = (k + z) % scales
        send = lax.dynamic_slice_in_dim(own[:, : widths[1]], piece * rows, rows, 0)
        coarse.append(permute(send, lay.rows_round(k, range(1, scales))))
    parts = [(fine[0] + fine[1]) + (fine[2] + fine[3])]
    for s in range(1, scales):
        got = 0.0
        for k in range(scales):
            got = got + jnp.where((mine - k) % scales == s, coarse[k][:, : widths[s]], 0)
        parts.append(got.astype(bf16))
    spread = []
    for s in range(scales):
        spread.append(parts[s])
        spread.append(jnp.zeros((rows, GAP, chans), bf16))
    x_zero = (jnp.concatenate(spread, 1) * col_mask.astype(bf16)).reshape(rows * cols, chans)

    arrived = []
    for k in range(scales):
        piece = (k + z) % scales
        send = lax.dynamic_slice_in_dim(dense_targets, piece * rows, rows, 0)
        send = after(send, fine[1])
        got = permute(send, lay.rows_round(k, range(scales)))
        arrived.append(got.reshape(rows * width, dense_targets.shape[2]))
    hold = arrived[:2]

    valid_mask, boxes, normal_targets, scale_cols, *_ = lax.optimization_barrier(
        (valid_mask, boxes, normal_targets, scale_cols, *fine, *coarse)
    )

    mask_all = valid_mask.astype(f32)
    pixels = jnp.arange(held * width, dtype=jnp.int32)
    hits = jnp.sum((boxes[:, None] == pixels[None, :]).astype(f32), 0).reshape(held, width)
    packed = jnp.concatenate(
        [mask_all[None], (mask_all + box_weight * hits)[None], normal_targets], 0
    )
    packed_other = permute(packed, lay.swap(1))
    from_own = place // (scales // 2) == core
    packed = jnp.where(from_own, packed, packed_other)
    packed = lax.dynamic_slice_in_dim(packed, mine * rows, rows, 1).reshape(5, rows * width)
    valid, weight = packed[0][:, None], packed[1][:, None]
    normals = jnp.pad(packed[2:].T, ((0, 0), (0, 128 - 3)))
    tables = table_call(scale_cols, starts, widths, width, cols)
    gamma = vectors[:chans]
    bias = vectors[chans:]
    core_here = core.reshape(1)
    flat_mask = jnp.broadcast_to(col_mask, (rows, cols, 1)).reshape(rows * cols, 1)

    all_taps = conv_bf16.reshape(depth, 3, 3 * chans, chans)

    size = rows * cols

    def neighbours(value):
        partner = permute(value, lay.swap(1))
        at = value.shape[0] - size + core * (rows - 1) * cols
        return partner, permute(lax.dynamic_slice_in_dim(value, at, cols, 0), lay.outward())

    def gain_of(depth_idx):
        return affine_scale[depth_idx].reshape(1, chans), affine_shift[depth_idx].reshape(1, chans)

    pre_shape = jax.ShapeDtypeStruct((size, chans), f32)
    buffer_shape = jax.ShapeDtypeStruct((size + cols, chans), bf16)
    grad_shape = jax.ShapeDtypeStruct((size, chans), bf16)
    partner_zero, outer_zero = neighbours(x_zero)
    outer_zero = after(outer_zero, *hold)
    pre_zero, x_one = conv_call(
        first_conv_kernel,
        core_here,
        x_zero,
        partner_zero,
        outer_zero,
        *gain_of(0),
        flat_mask,
        [],
        all_taps,
        0,
        [pre_shape, buffer_shape],
        False,
        "conv_rows",
    )
    partner_one, outer_one = neighbours(x_one)
    grad_one, grad_mine, grad_pack, grad_gamma, grad_bias, loss_parts = head_call(
        core_here,
        mine.reshape(1),
        x_one,
        partner_one,
        outer_one,
        (*gain_of(1), flat_mask, gamma.reshape(1, chans), bias.reshape(1, wide)),
        (weight, valid, normals),
        head_bf16,
        arrived,
        tables,
        all_taps,
        1,
    )
    part = head_width // 2
    half = chans // 2
    staged = imgs == 8 and scales == 4
    x, y = (img // 2) % 2, img // 4
    where = (x, y, z)
    grad_partner, grad_outer = neighbours(grad_one)
    pack_got = permute(grad_pack, lay.swap(1))
    conv_grad_one = kernel_grad(
        core_here, x_one, partner_one, outer_one, grad_partner, grad_one, grad_partner, part
    )
    if staged:
        early = Sum([conv_grad_one.reshape(2 * taps, part, chans)], where, lay)
        early.first()
        grad_outer = after(grad_outer, *early.send)
    (grad_zero,) = conv_call(
        back_conv_kernel,
        core_here,
        grad_one,
        grad_partner,
        grad_outer,
        *gain_of(0),
        flat_mask,
        [pre_zero],
        all_taps,
        1,
        [grad_shape],
        True,
        "conv_back",
    )
    grad_zero_partner = permute(grad_zero, lay.swap(1))
    head_grad = head_grad_call(grad_mine, grad_pack, after(pack_got, grad_zero))
    if staged:
        middle = Sum([head_grad.reshape(heads_count, part, chans)], where, lay)
        middle.first()
        early.second(*middle.send)
        grad_zero_partner = after(grad_zero_partner, *early.send)
    conv_grad_zero = kernel_grad(
        core_here,
        x_zero,
        partner_zero,
        outer_zero,
        partner_one,
        grad_zero,
        grad_zero_partner,
        part,
    )
    if staged:
        late = Sum([conv_grad_zero.reshape(2 * taps, part, chans)], where, lay)
        late.first()
    grad_gamma, grad_bias = grad_gamma.reshape(chans), grad_bias.reshape(wide)
    own_count = jnp.where(z == 0, jnp.sum(mask_all), 0.0).reshape(1)
    loss_parts = jnp.concatenate([loss_parts[0, :2], own_count])

    vec_rows = jnp.concatenate(
        [grad_gamma, grad_bias, loss_parts, jnp.zeros((-(chans + wide + 3) % 1024,), f32)]
    ).reshape(-1, 128)
    vec_sum = butterfly(vec_rows, lay).reshape(-1)
    totals = vec_sum[chans + wide : chans + wide + 2]
    count = vec_sum[chans + wide + 2]
    grad_vec = vec_sum[: chans + wide]
    vec_squares = jnp.sum(grad_vec * grad_vec)

    blocks_count = owner_slot.shape[0]
    slots_here = master.shape[0]
    slots = slots_here * scales * imgs
    slot_ids = jnp.arange(slots, dtype=jnp.int32)
    match = slot_ids[:, None] == owner_slot[None, :]
    block_of = jnp.sum(
        jnp.where(match, jnp.arange(blocks_count, dtype=jnp.int32)[None, :], 0), 1
    )
    owned_f = jnp.any(match, 1).astype(f32)

    if staged:
        early_total = line_sum(early.third(*late.send), scales)
        middle.second(*late.send)
        late.second()
        late_total = line_sum(late.third() + middle.third(), scales)
        blocks = jnp.concatenate([late_total[: 2 * taps], early_total, late_total[2 * taps :]], 0)
        payload = route_call(blocks, jnp.where(owned_f > 0, block_of, -1), scales * imgs)
        got = lax.all_to_all(payload, AXES, 0, 0, tiled=True)
        starts_here = [
            (i % 2) * (half // 2) + (i // 2 % 2) * (half // 4) + (i // 4) * (half // 8) + s * (half // 32)
            for s, i in lay.all_devices()
        ]
        master_new, slot_m_new, slot_v_new, fresh, norm = update_call(
            jnp.stack([vec_squares, count]),
            got,
            starts_here,
            master,
            slot_m,
            slot_v,
            basis_left,
            basis_right,
        )
        grad_norm, factor = norm[0, 0], norm[0, 1]
        vec_out = vector_update(vectors, vec_m, vec_v, grad_vec * factor)
        sources = spread_slots(fresh, lay, z, vec_out)
        owner = owner_slot // slots_here
        other_img = owner % imgs
        turn = other_img ^ img
        step = ((turn >> 1) & 1) * 8 + (turn >> 2) * 4 + ((owner // imgs) ^ z)
        place = jnp.sum(
            jnp.where(
                step[:, None] == jnp.arange(16, dtype=jnp.int32)[None, :],
                jnp.asarray(PLACES, jnp.int32)[None, :],
                0,
            ),
            1,
        )
        array = place // 4 + 4 * (turn & 1)
        item = (place % 4) * slots_here + owner_slot % slots_here
    else:
        parts = jnp.concatenate(
            [v.reshape(2 * taps, part, chans) for v in (conv_grad_zero, conv_grad_one)]
            + [head_grad.reshape(heads_count, part, chans)],
            0,
        )
        none = jnp.zeros_like(parts)
        blocks = jnp.concatenate(
            [jnp.where(core == 0, parts, none), jnp.where(core == 1, parts, none)], 1
        )
        by_slot = blocks[block_of] * owned_f[:, None, None]
        owned = lax.psum_scatter(by_slot, AXES, scatter_dimension=0, tiled=True)
        squares_sum = lax.psum(jnp.sum(owned * owned), AXES) + vec_squares

        grad_norm = jnp.sqrt(squares_sum) / count
        factor = clip_level / jnp.maximum(grad_norm, clip_level) / count
        master_new, slot_m_new, slot_v_new = soap_update(
            master, slot_m, slot_v, basis_left, basis_right, owned * factor
        )
        sources = [lax.all_gather(master_new.astype(bf16), AXES, axis=0, tiled=True)]
        array, item = jnp.zeros_like(owner_slot), owner_slot
        vec_out = vector_update(vectors, vec_m, vec_v, grad_vec * factor)
    vec_new, vec_m_new, vec_v_new = vec_out
    conv_copy, head_copy = place_blocks(sources, array, item, depth, taps)
    loss = jnp.stack([totals[0] / wide + totals[1], count])
    return (
        loss,
        grad_norm,
        vec_new,
        vec_m_new,
        vec_v_new,
        master_new,
        slot_m_new,
        slot_v_new,
        conv_copy,
        head_copy,
    )


def solution(mesh):
    in_specs = (
        P("scale", "img", None, None),
        P("img", None),
        P(),
        P("img"),
        P(None, "img", None),
        P("img", None, "scale"),
        P(),
        P(),
        P(),
        P(),
        P(),
        P(),
        P(),
        P(("scale", "img"), None, None),
        P(("scale", "img"), None, None),
        P(("scale", "img"), None, None),
        P(("scale", "img"), None, None),
        P(("scale", "img"), None, None),
        P(),
    )
    out_specs = (
        P(),
        P(),
        P(),
        P(),
        P(),
        P(("scale", "img"), None, None),
        P(("scale", "img"), None, None),
        P(("scale", "img"), None, None),
        P(),
        P(),
    )
    return jax.shard_map(local, mesh=mesh, in_specs=in_specs, out_specs=out_specs, check_vma=False)
```

```python
import jax
import jax.numpy as jnp
from jax import lax
from jax.experimental import pallas as pl
from jax.experimental.pallas import tpu as pltpu
from jax.sharding import PartitionSpec as P

STEP = 5

beta_one = 0.5
beta_two = 0.5
adam_eps = 1e-08
rate_matrix = 0.01
rate_vector = 0.2
weight_decay = 0.01
clip_level = 0.001
box_weight = 2.0
norm_eps = 1e-05
highest = lax.Precision.HIGHEST
bf16 = jnp.bfloat16
f32 = jnp.float32
AXES = ("scale", "img")
GAP = 16
CODE = 32767.0
CHUNK = 544
VMEM_BYTES = 56 * 2**20
COST = pl.CostEstimate(flops=5 * 10**9, bytes_accessed=10**6, transcendentals=0)
TINY = pl.CostEstimate(flops=1, bytes_accessed=1, transcendentals=0)
LONG = pl.CostEstimate(flops=10**11, bytes_accessed=10**6, transcendentals=0)


class Layout:
    def __init__(self, scales, imgs):
        self.scales = scales
        self.imgs = imgs

    def pos(self, group, scale):
        return scale if group % 2 == 0 else self.scales - 1 - scale

    def dev(self, scale, img):
        return scale * self.imgs + img

    def at(self, group, place, core):
        return self.dev(self.pos(group, place), 2 * group + core)

    def all_devices(self):
        return [(s, i) for s in range(self.scales) for i in range(self.imgs)]

    def swap(self, bit):
        return [(self.dev(s, i), self.dev(s, i ^ bit)) for s, i in self.all_devices()]

    def turn(self, step):
        return [
            (self.dev(s, i), self.dev((s + step) % self.scales, i)) for s, i in self.all_devices()
        ]

    def scale_swap(self, bit):
        return [(self.dev(s, i), self.dev(s ^ bit, i)) for s, i in self.all_devices()]

    def rows_round(self, shift, sources):
        pairs = []
        for s in sources:
            for i in range(self.imgs):
                group, core = i // 2, i % 2
                piece = (shift + s) % self.scales
                place = (self.scales // 2) * core + piece // 2
                pairs.append((self.dev(s, i), self.at(group, place, piece % 2)))
        return pairs

    def chip_round(self, shift):
        pairs = []
        for s, i in self.all_devices():
            place = 2 * (i % 2) + (shift + s) % 2
            pairs.append((self.dev(s, i), self.at(i // 2, place, s // 2)))
        return pairs

    def row_order(self):
        groups = self.imgs // 2
        return [
            self.at(j, place, c) for j in range(groups) for place in range(self.scales) for c in range(2)
        ]

    def outward(self):
        order = self.row_order()
        pairs = []
        for at in range(1, len(order) - 1, 2):
            pairs += [(order[at], order[at + 1]), (order[at + 1], order[at])]
        return pairs


def permute(value, pairs):
    return lax.ppermute(value, AXES, pairs)


def after(value, *others):
    return lax.optimization_barrier((value, *others))[0]


def table_kernel(starts, widths, width, cols_ref, up_high, up_low, down_high, down_low):
    def table(shape, coarse_axis):
        place = lax.broadcasted_iota(jnp.int32, shape, coarse_axis)
        fine = lax.broadcasted_iota(jnp.int32, shape, 1 - coarse_axis)
        total = jnp.zeros(shape, f32)
        bits = (2 * width).bit_length() - 1
        for s, (start, span) in enumerate(zip(starts, widths)):
            columns = cols_ref[s]
            numer = jnp.maximum((2 * fine + 1) * columns - width, 0)
            lower = lax.shift_right_logical(numer, bits)
            frac = (numer - lax.shift_left(lower, bits)).astype(f32) * (0.5 / width)
            upper = jnp.minimum(lower + 1, columns - 1)
            coarse = place - start
            inside = (coarse >= 0) & (coarse < span)
            part = jnp.where(coarse == lower, 1.0 - frac, 0.0) + jnp.where(coarse == upper, frac, 0.0)
            total += jnp.where(inside, part, 0.0)
        return halves(total)

    up_high[...], up_low[...] = table(up_high.shape, 1)
    down_high[...], down_low[...] = table(down_high.shape, 0)


def table_call(scale_cols, starts, widths, width, cols):
    vmem = pl.BlockSpec(memory_space=pltpu.VMEM)
    return pl.pallas_call(
        lambda *refs: table_kernel(starts, widths, width, *refs),
        in_specs=[pl.BlockSpec(memory_space=pltpu.SMEM)],
        out_specs=[vmem] * 4,
        out_shape=[jax.ShapeDtypeStruct((width, cols), bf16)] * 2
        + [jax.ShapeDtypeStruct((cols, width), bf16)] * 2,
        cost_estimate=TINY,
        name="tables",
    )(scale_cols)


def halves(value):
    high = value.astype(bf16)
    return high, (value - high.astype(f32)).astype(bf16)


def whole(shape):
    return pl.BlockSpec(shape, lambda *_: (0,) * len(shape))


def spread_taps(store, at, row, cols, chans):
    base = pl.multiple_of(at * cols, 16)
    value = row.astype(f32)
    store[pl.ds(base, cols), pl.ds(0, chans)] = pltpu.roll(value, 1, 0).astype(bf16)
    store[pl.ds(base, cols), pl.ds(chans, chans)] = row
    store[pl.ds(base, cols), pl.ds(2 * chans, chans)] = pltpu.roll(value, cols - 1, 0).astype(bf16)


def load_taps(rows, cols, chans, core, cur, partner, outer, taps):
    for r in range(rows):
        spread_taps(taps, r + 1, cur[pl.ds(r * cols, cols), :], cols, chans)
    outside = (rows + 1) * core
    spread_taps(taps, outside, outer[...], cols, chans)
    inside = pl.multiple_of((rows - 1) * core * cols, 16)
    spread_taps(taps, rows + 1 - outside, partner[pl.ds(inside, cols), :], cols, chans)


def fetch(source, layer, target, sems):
    copies = [pltpu.make_async_copy(source.at[layer, a], target.at[a], sems.at[a]) for a in range(3)]
    for copy in copies:
        copy.start()
    return copies


def conv_into(pre, taps, weights, copies, cols):
    size = pre.shape[0]
    for a in range(3):
        copies[a].wait()
        value = jnp.dot(taps[pl.ds(a * cols, size), :], weights[a], preferred_element_type=f32)
        if a == 0:
            pre[...] = value
        else:
            pre[...] += value


def gelu_slope(u):
    root = 0.7978845608028654
    bend = 0.044715
    th = jnp.tanh(root * (u + bend * u * u * u))
    return 0.5 * (1.0 + th) + 0.5 * u * (1.0 - th * th) * root * (1.0 + 3.0 * bend * u * u)


def face(buffer, facing, core, rows, cols):
    at = pl.multiple_of(cols + core * (rows - 1) * cols, 16)
    facing[...] = buffer[pl.ds(at, cols), :]


def first_conv_kernel(
    rows, cols, chans, layer, core_ref, cur, partner, outer, gain, shift, mask, w_hbm, pre, out, facing, taps, w, sems
):
    copies = fetch(w_hbm, layer, w, sems)
    load_taps(rows, cols, chans, core_ref[0], cur, partner, outer, taps)
    out[pl.ds(0, cols), :] = outer[...]
    conv_into(pre, taps, w, copies, cols)

    def body(i, carry):
        at = pl.ds(pl.multiple_of(i * CHUNK, 16), CHUNK)
        u = pre[at, :] * gain[...] + shift[...]
        to = pl.ds(pl.multiple_of(cols + i * CHUNK, 16), CHUNK)
        out[to, :] = (jax.nn.gelu(u) * mask[at, :]).astype(bf16)
        return carry

    lax.fori_loop(0, rows * cols // CHUNK, body, 0)
    face(out, facing, core_ref[0], rows, cols)


def back_conv_kernel(
    rows, cols, chans, layer, core_ref, cur, partner, outer, gain, shift, mask, pre_in, w_hbm, out, taps, w, sems, acc
):
    copies = fetch(w_hbm, layer, w, sems)
    size = rows * cols
    cur = cur.at[pl.ds(cols, size)]
    partner = partner.at[pl.ds(cols, size)]
    load_taps(rows, cols, chans, core_ref[0], cur, partner, outer, taps)
    for a in range(3):
        copies[2 - a].wait()
        value = 0.0
        for b in range(3):
            value += lax.dot_general(
                taps[pl.ds(a * cols, size), b * chans : (b + 1) * chans],
                w[2 - a, (2 - b) * chans : (3 - b) * chans, :],
                (((1,), (1,)), ((), ())),
                preferred_element_type=f32,
            )
        if a == 0:
            acc[...] = value
        else:
            acc[...] += value

    def body(i, carry):
        at = pl.ds(pl.multiple_of(i * CHUNK, 16), CHUNK)
        u = pre_in[at, :] * gain[...] + shift[...]
        out[at, :] = (acc[at, :] * mask[at, :] * gelu_slope(u) * gain[...]).astype(bf16)
        return carry

    lax.fori_loop(0, size // CHUNK, body, 0)


def conv_call(kernel, core, cur, partner, outer, gain, shift, mask, more, weights, layer, shapes, acc, name):
    cols, chans = outer.shape
    rows = 2
    size = rows * cols
    scratch = [
        pltpu.VMEM(((rows + 2) * cols, 3 * chans), bf16),
        pltpu.VMEM((3, 3 * chans, chans), bf16),
        pltpu.SemaphoreType.DMA((3,)),
    ]
    if acc:
        scratch.append(pltpu.VMEM((size, chans), f32))
    vmem = pl.BlockSpec(memory_space=pltpu.VMEM)
    return pl.pallas_call(
        lambda *refs: kernel(rows, cols, chans, layer, *refs),
        in_specs=[pl.BlockSpec(memory_space=pltpu.SMEM)]
        + [vmem] * (6 + len(more))
        + [pl.BlockSpec(memory_space=pl.ANY)],
        out_specs=[vmem for _ in shapes],
        out_shape=shapes,
        scratch_shapes=scratch,
        compiler_params=pltpu.CompilerParams(vmem_limit_bytes=VMEM_BYTES),
        cost_estimate=COST if acc else TINY,
        name=name,
    )(core, cur, partner, outer, gain, shift, mask, *more, weights)


def head_kernel(
    rows,
    cols,
    width,
    scales,
    layer,
    core_ref,
    place_ref,
    cur,
    partner,
    outer,
    gain,
    shift,
    mask,
    gamma,
    bias,
    weight,
    valid,
    normals,
    heads_hbm,
    first_hbm,
    second_hbm,
    traded_hbm,
    up_high_hbm,
    up_low_hbm,
    down_high_hbm,
    down_low_hbm,
    w_hbm,
    out,
    facing,
    mine,
    pack,
    dgamma,
    dbias,
    sums,
    taps,
    w,
    sems,
    pre,
    y_ref,
    tapped,
    raised_high,
    raised_low,
    dj_low,
    back,
    target,
    heads,
    target_in,
    up_high,
    up_low,
    down_high,
    down_low,
    more_sems,
    target_sems,
):
    chans = outer.shape[1]
    size = rows * cols
    core = core_ref[0]
    copies = fetch(w_hbm, layer, w, sems)
    pairs = (
        (up_high_hbm, up_high),
        (up_low_hbm, up_low),
        (heads_hbm, heads),
        (down_high_hbm, down_high),
        (down_low_hbm, down_low),
    )
    loads = [pltpu.make_async_copy(a, b, more_sems.at[i]) for i, (a, b) in enumerate(pairs)]
    for load in loads:
        load.start()
    kept = (first_hbm, second_hbm)
    for s in range(scales):
        for r in range(2):
            turn = lax.rem(place_ref[0] + s, 2) == r

            @pl.when((core == s // 2) & turn)
            def _(s=s, r=r):
                pltpu.make_async_copy(kept[r].at[core], target_in.at[s], target_sems.at[s]).start()

            @pl.when((core != s // 2) & turn)
            def _(s=s, r=r):
                pltpu.make_async_copy(traded_hbm.at[r], target_in.at[s], target_sems.at[s]).start()

    cur = cur.at[pl.ds(cols, size)]
    partner = partner.at[pl.ds(cols, size)]
    load_taps(rows, cols, chans, core, cur, partner, outer, taps)
    out[pl.ds(0, cols), :] = outer[...]
    conv_into(pre, taps, w, copies, cols)

    def forward(i, carry):
        at = pl.ds(0, size)
        u = pre[at, :] * gain[...] + shift[...]
        y = jax.nn.gelu(u) * mask[at, :]
        y_ref[at, :] = y
        scale = lax.rsqrt(jnp.mean(y * y, -1, keepdims=True) + norm_eps)
        tapped[at, :] = (gamma[...] * y * scale).astype(bf16)
        return carry

    forward(0, 0)
    for load in loads:
        load.wait()
    for s in range(scales):
        pltpu.make_async_copy(traded_hbm.at[0], target_in.at[s], target_sems.at[s]).wait()
    part = target_in.shape[2]
    for s in range(scales):
        target[:, s * part : (s + 1) * part] = target_in[s]

    half_wide = mine.shape[1]
    for r in range(rows):
        line = tapped[pl.ds(r * cols, cols), :]
        value = jnp.dot(up_high[...], line, preferred_element_type=f32)
        value += jnp.dot(up_low[...], line, preferred_element_type=f32)
        high = value.astype(bf16)
        raised_high[pl.ds(r * width, width), :] = high
        pack[pl.ds(r * width, width), pl.ds(half_wide, chans)] = high
        raised_low[pl.ds(r * width, width), :] = (value - high.astype(f32)).astype(bf16)

    step = heads.shape[2]
    wide = heads.shape[0] * step
    dense = jnp.zeros((1, step), f32)
    normal = jnp.zeros((1, 1), f32)
    for t in range(wide // step):
        joined = jnp.dot(raised_high[...], heads[t], preferred_element_type=f32)
        joined += jnp.dot(raised_low[...], heads[t], preferred_element_type=f32)
        joined += float(scales) * bias[:, t * step : (t + 1) * step]
        diff = joined - target[:, t * step : (t + 1) * step].astype(f32)
        pulled = weight[...] * diff
        dense += jnp.sum(pulled * diff, 0, keepdims=True)
        grad = pulled * (1.0 / wide)
        if t == 0:
            lane = lax.broadcasted_iota(jnp.int32, (joined.shape[0], 128), 1)
            n = jnp.where(lane < 3, joined[:, :128], 0.0)
            other = normals[...]
            inner = jnp.sum(n * other, -1, keepdims=True)
            own_sq = jnp.sum(n * n, -1, keepdims=True) + 1.0
            other_sq = jnp.sum(other * other, -1, keepdims=True) + 1.0
            root = lax.rsqrt(own_sq * other_sq)
            normal += jnp.sum(valid[...] * (1.0 - inner * root), 0, keepdims=True)
            turn = valid[...] * root * (inner / own_sq * n - other)
            grad = jnp.concatenate([grad[:, :128] + turn, grad[:, 128:]], 1)
        dbias[:, t * step : (t + 1) * step] = float(scales) * jnp.sum(grad, 0, keepdims=True)
        dj_low[:, t * step : (t + 1) * step] = grad.astype(bf16)
        half = step // 2
        first, second = grad[:, :half], grad[:, half:]
        mine[:, t * half : (t + 1) * half] = jnp.where(core == 0, first, second).astype(bf16)
        pack[:, t * half : (t + 1) * half] = jnp.where(core == 0, second, first).astype(bf16)
    lane = lax.broadcasted_iota(jnp.int32, (1, 128), 1)
    total = 0.5 * jnp.sum(dense, 1, keepdims=True)
    sums[...] = jnp.where(lane == 0, total, jnp.where(lane == 1, normal, 0.0))

    draised = 0.0
    for t in range(heads.shape[0]):
        draised += lax.dot_general(
            dj_low[:, t * step : (t + 1) * step],
            heads[t],
            (((1,), (1,)), ((), ())),
            preferred_element_type=f32,
        )
    for r in range(rows):
        part = draised[r * width : (r + 1) * width]
        high = part.astype(bf16)
        low = (part - high.astype(f32)).astype(bf16)
        value = jnp.dot(down_high[...], high, preferred_element_type=f32)
        value += jnp.dot(down_low[...], high, preferred_element_type=f32)
        value += jnp.dot(down_high[...], low, preferred_element_type=f32)
        back[pl.ds(r * cols, cols), :] = value

    def backward(i, carry):
        at = pl.ds(0, size)
        y = y_ref[at, :]
        dt = back[at, :]
        scale = lax.rsqrt(jnp.mean(y * y, -1, keepdims=True) + norm_eps)
        dty = dt * y
        pull = jnp.mean(gamma[...] * dty, -1, keepdims=True)
        dy = gamma[...] * dt * scale - y * (scale * scale * scale * pull)
        u = pre[at, :] * gain[...] + shift[...]
        to = pl.ds(cols, size)
        out[to, :] = (dy * mask[at, :] * gelu_slope(u) * gain[...]).astype(bf16)
        return carry + jnp.sum(dty * scale, 0, keepdims=True)

    dgamma[...] = backward(0, jnp.zeros((1, chans), f32))
    face(out, facing, core, rows, cols)


def head_call(core, place, cur, partner, outer, vectors, pixel, heads, target, tables, weights, layer):
    cols, chans = outer.shape
    rows = 2
    size = rows * cols
    width = tables[0].shape[0]
    wide = heads.shape[0] * heads.shape[2]
    pixels = rows * width
    scales = wide // target[0].shape[2]
    vmem = pl.BlockSpec(memory_space=pltpu.VMEM)
    anywhere = pl.BlockSpec(memory_space=pl.ANY)
    shapes = [
        jax.ShapeDtypeStruct((size + cols, chans), bf16),
        jax.ShapeDtypeStruct((cols, chans), bf16),
        jax.ShapeDtypeStruct((pixels, wide // 2), bf16),
        jax.ShapeDtypeStruct((pixels, wide // 2 + chans), bf16),
        jax.ShapeDtypeStruct((1, chans), f32),
        jax.ShapeDtypeStruct((1, wide), f32),
        jax.ShapeDtypeStruct((1, 128), f32),
    ]
    return pl.pallas_call(
        lambda *refs: head_kernel(rows, cols, width, scales, layer, *refs),
        in_specs=[pl.BlockSpec(memory_space=pltpu.SMEM)] * 2 + [vmem] * 11 + [anywhere] * 9,
        out_specs=[vmem for _ in shapes],
        out_shape=shapes,
        scratch_shapes=[
            pltpu.VMEM(((rows + 2) * cols, 3 * chans), bf16),
            pltpu.VMEM((3, 3 * chans, chans), bf16),
            pltpu.SemaphoreType.DMA((3,)),
            pltpu.VMEM((size, chans), f32),
            pltpu.VMEM((size, chans), f32),
            pltpu.VMEM((size, chans), bf16),
            pltpu.VMEM((pixels, chans), bf16),
            pltpu.VMEM((pixels, chans), bf16),
            pltpu.VMEM((pixels, wide), bf16),
            pltpu.VMEM((size, chans), f32),
            pltpu.VMEM((pixels, wide), bf16),
            pltpu.VMEM(heads.shape, bf16),
            pltpu.VMEM((scales, *target[0].shape[1:]), bf16),
        ]
        + [pltpu.VMEM(table.shape, bf16) for table in tables]
        + [pltpu.SemaphoreType.DMA((5,)), pltpu.SemaphoreType.DMA((scales,))],
        compiler_params=pltpu.CompilerParams(vmem_limit_bytes=VMEM_BYTES),
        cost_estimate=COST,
        name="head_rows",
    )(core, place, cur, partner, outer, *vectors, *pixel, heads, *target, *tables, weights)


def coded(value):
    top = jnp.max(jnp.abs(value), 0, keepdims=True)
    power = jnp.clip(jnp.ceil(jnp.log2(top)), -100.0, 110.0)
    codes = jnp.clip(jnp.round(value * (jnp.exp2(-power) * CODE)), -CODE, CODE)
    return codes.astype(jnp.int32), power.astype(jnp.int32)


POWERS = 32


def split_first(stage, row, n, x, y, keep_a, keep_b, send_a, send_b, pow_a, pow_b):
    rows, w = keep_a.shape[1] * 2, keep_a.shape[2]
    half, quarter = rows // 2, rows // 4

    def block(at, size, lanes):
        return stage[pl.ds(pl.multiple_of(row + at, quarter), size), lanes]

    left, right = pl.ds(0, w), pl.ds(w, w)
    keep_a[n] = block(x * half, half, left)
    keep_b[n] = jnp.concatenate([block(xx * half + y * quarter, quarter, right) for xx in range(2)], 0)
    gone = block((1 - x) * half, half, left)
    codes, power = coded(gone)
    at = pl.ds(pl.multiple_of(n * half, half), half)
    send_a[at, :] = codes.astype(jnp.int16)
    pow_a[pl.ds(n, 1), :] = power
    gone = jnp.concatenate(
        [block(xx * half + (1 - y) * quarter, quarter, right) for xx in range(2)], 0
    )
    codes, power = coded(gone)
    send_b[at, :] = codes.astype(jnp.int16)
    pow_b[pl.ds(n, 1), :] = power


def close_powers(n, half, sends, pows):
    for send, power in zip(sends, pows):
        send[pl.ds(n * half, POWERS), :] = power[...].astype(jnp.int16)


def first_shapes(n, rows, cols):
    keep = jax.ShapeDtypeStruct((n, rows // 2, cols // 2), f32)
    send = jax.ShapeDtypeStruct((n * rows // 2 + POWERS, cols // 2), jnp.int16)
    return [keep, keep, send, send]


def first_scratch(cols):
    return [pltpu.VMEM((POWERS, cols // 2), jnp.int32)] * 2


def kernel_grad_kernel(
    rows, cols, chans, part, x_at, g_at, staged, ids, cur, partner, outer, far, g_own, g_far, *refs
):
    step = pl.program_id(0)
    core = ids[0]
    size = rows * cols
    if staged:
        keep_a, keep_b, send_a, send_b, taps, grads, stage, pow_a, pow_b = refs
    else:
        out, taps, grads = refs

    @pl.when(step == 0)
    def _():
        own_at = 1 + rows * core
        far_at = 1 + rows * (1 - core)
        for r in range(rows):
            at = pl.ds(x_at + r * cols, cols)
            spread_taps(taps, own_at + r, cur[at, :], cols, chans)
            spread_taps(taps, far_at + r, partner[at, :], cols, chans)
        spread_taps(taps, (2 * rows + 1) * core, outer[...], cols, chans)
        spread_taps(taps, (2 * rows + 1) * (1 - core), far[...], cols, chans)
        for h in range(grads.shape[1] // part):
            lanes = pl.ds(pl.multiple_of((2 * h + core) * part, part), part)
            own_rows = pl.ds(pl.multiple_of(core * size, 16), size)
            far_rows = pl.ds(pl.multiple_of((1 - core) * size, 16), size)
            grads[own_rows, h * part : (h + 1) * part] = g_own[pl.ds(g_at, size), lanes]
            grads[far_rows, h * part : (h + 1) * part] = g_far[pl.ds(g_at, size), lanes]
        if staged:
            pow_a[...] = jnp.zeros(pow_a.shape, jnp.int32)
            pow_b[...] = jnp.zeros(pow_b.shape, jnp.int32)

    window = taps[pl.ds(pl.multiple_of(step * cols, 16), 2 * size), :]
    value = lax.dot_general(
        grads[...], window, (((0,), (0,)), ((), ())), preferred_element_type=f32
    )
    if not staged:
        for b in range(3):
            out[b] = value[:, b * chans : (b + 1) * chans]
        return
    sides = grads.shape[1] // part
    for b in range(3):
        stage[b] = value[:, b * chans : (b + 1) * chans]
    for b in range(3):
        for h in range(sides):
            n = (3 * step + b) * sides + h
            split_first(
                stage.at[b], h * part, n, ids[1], ids[2], keep_a, keep_b, send_a, send_b, pow_a, pow_b
            )

    @pl.when(step == 2)
    def _():
        close_powers(9 * sides, part // 2, (send_a, send_b), (pow_a, pow_b))


def kernel_grad(ids, cur, partner, outer, far, g_own, g_far, part, staged):
    cols, chans = outer.shape
    rows = 2
    size = rows * cols
    outs = g_own.shape[1] // 2
    x_at, g_at = cur.shape[0] - size, g_own.shape[0] - size
    scratch = [
        pltpu.VMEM(((2 * rows + 2) * cols, 3 * chans), bf16),
        pltpu.VMEM((2 * size, outs), bf16),
    ]
    if staged:
        shapes = first_shapes(9 * outs // part, part, chans)
        out_specs = [whole(shape.shape) for shape in shapes]
        scratch += [pltpu.VMEM((3, outs, chans), f32)] + first_scratch(chans)
    else:
        shapes = jax.ShapeDtypeStruct((9, outs, chans), f32)
        out_specs = pl.BlockSpec((3, outs, chans), lambda i: (i, 0, 0))
    return pl.pallas_call(
        lambda *refs: kernel_grad_kernel(rows, cols, chans, part, x_at, g_at, staged, *refs),
        grid=(3,),
        in_specs=[
            pl.BlockSpec(memory_space=pltpu.SMEM),
            whole(cur.shape),
            whole(cur.shape),
            whole((cols, chans)),
            pl.BlockSpec((cols, chans), lambda i: (0, 0)),
            whole(g_own.shape),
            whole(g_own.shape),
        ],
        out_specs=out_specs,
        out_shape=shapes,
        scratch_shapes=scratch,
        compiler_params=pltpu.CompilerParams(vmem_limit_bytes=VMEM_BYTES),
        cost_estimate=COST,
        name="kernel_grad",
    )(ids, cur, partner, outer, far, g_own, g_far)


def head_grad_kernel(staged, part, ids, mine, own, got, *refs):
    half = mine.shape[1]
    dims = (((0,), (0,)), ((), ()))
    value = lax.dot_general(mine[...], own[:, half:], dims, preferred_element_type=f32)
    value += lax.dot_general(got[:, :half], got[:, half:], dims, preferred_element_type=f32)
    if not staged:
        refs[0][...] = value
        return
    keep_a, keep_b, send_a, send_b, stage, pow_a, pow_b = refs
    stage[...] = value
    pow_a[...] = jnp.zeros(pow_a.shape, jnp.int32)
    pow_b[...] = jnp.zeros(pow_b.shape, jnp.int32)
    for n in range(half // part):
        split_first(stage, n * part, n, ids[1], ids[2], keep_a, keep_b, send_a, send_b, pow_a, pow_b)
    close_powers(half // part, part // 2, (send_a, send_b), (pow_a, pow_b))


def head_grad_call(ids, mine, own, got, part, staged):
    vmem = pl.BlockSpec(memory_space=pltpu.VMEM)
    half = mine.shape[1]
    chans = own.shape[1] - half
    shapes = [jax.ShapeDtypeStruct((half, chans), f32)]
    scratch = []
    if staged:
        shapes = first_shapes(half // part, part, chans)
        scratch = [pltpu.VMEM((half, chans), f32)] + first_scratch(chans)
    return pl.pallas_call(
        lambda *refs: head_grad_kernel(staged, part, *refs),
        in_specs=[pl.BlockSpec(memory_space=pltpu.SMEM)] + [vmem] * 3,
        out_specs=[vmem for _ in shapes],
        out_shape=shapes,
        scratch_shapes=scratch,
        compiler_params=pltpu.CompilerParams(vmem_limit_bytes=VMEM_BYTES),
        cost_estimate=COST,
        name="head_grad",
    )(ids, mine, own, got)


def scales_of(rows):
    return jnp.exp2(rows.astype(jnp.int32).astype(f32)) * (1.0 / CODE)


def second_kernel(ids, keep_a, keep_b, got_a, got_b, keep, send_a, send_b, step_a, step_b, pow_a, pow_b):
    count, rows, w = keep_a.shape
    half = rows // 2
    step_a[...] = scales_of(got_a[pl.ds(count * rows, POWERS), :])
    step_b[...] = scales_of(got_b[pl.ds(count * rows, POWERS), :])
    pow_a[...] = jnp.zeros(pow_a.shape, jnp.int32)
    pow_b[...] = jnp.zeros(pow_b.shape, jnp.int32)
    sides = (
        (keep_a, got_a, step_a, send_a, pow_a, ids[2], 0),
        (keep_b, got_b, step_b, send_b, pow_b, ids[1], w),
    )

    def body(n, carry):
        for held, got, step, send, power, bit, lane in sides:
            stays = pl.multiple_of(bit * half, half)
            goes = pl.multiple_of((1 - bit) * half, half)
            base = pl.multiple_of(n * rows, rows)

            def total(at):
                arrived = got[pl.ds(base + at, half), :].astype(jnp.int32).astype(f32)
                return held[n, pl.ds(at, half), :] + arrived * step[pl.ds(n, 1), :]

            keep[n, :, pl.ds(lane, w)] = total(stays)
            codes, top = coded(total(goes))
            send[pl.ds(pl.multiple_of(n * half, half), half), :] = codes.astype(jnp.int16)
            power[pl.ds(n, 1), :] = top
        return carry

    lax.fori_loop(0, count, body, 0)
    close_powers(count, half, (send_a, send_b), (pow_a, pow_b))


def second_call(ids, keep_a, keep_b, got_a, got_b):
    vmem = pl.BlockSpec(memory_space=pltpu.VMEM)
    count, rows, w = keep_a.shape
    send = jax.ShapeDtypeStruct((count * rows // 2 + POWERS, w), jnp.int16)
    return pl.pallas_call(
        second_kernel,
        in_specs=[pl.BlockSpec(memory_space=pltpu.SMEM)] + [vmem] * 4,
        out_specs=[vmem] * 3,
        out_shape=[jax.ShapeDtypeStruct((count, rows // 2, 2 * w), f32), send, send],
        scratch_shapes=[pltpu.VMEM((POWERS, w), f32)] * 2 + first_scratch(2 * w),
        compiler_params=pltpu.CompilerParams(vmem_limit_bytes=VMEM_BYTES),
        cost_estimate=LONG,
        name="sum_second",
    )(ids, keep_a, keep_b, got_a, got_b)


def third_kernel(counts, scales, *refs):
    pieces = len(counts)
    out, codes, step_a, step_b = refs[3 * pieces :]
    total = sum(counts)
    rows = refs[0].shape[1]
    w = refs[0].shape[2] // 2
    fine = rows // scales
    codes[:, pl.ds(total * fine, POWERS), :] = jnp.zeros((scales, POWERS, 2 * w), jnp.int32)
    base = 0
    for piece, count in enumerate(counts):
        keep, got_a, got_b = refs[3 * piece : 3 * piece + 3]
        step_a[...] = scales_of(got_a[pl.ds(count * rows, POWERS), :])
        step_b[...] = scales_of(got_b[pl.ds(count * rows, POWERS), :])

        def body(n, carry, keep=keep, got_a=got_a, got_b=got_b, base=base):
            at = pl.ds(pl.multiple_of(n * rows, rows), rows)
            arrived = jnp.concatenate(
                [
                    got[at, :].astype(jnp.int32).astype(f32) * step[pl.ds(n, 1), :]
                    for got, step in ((got_a, step_a), (got_b, step_b))
                ],
                1,
            )
            value = keep[n] + arrived
            for s in range(scales):
                code, power = coded(value[s * fine : (s + 1) * fine])
                codes[s, pl.ds(pl.multiple_of((base + n) * fine, fine), fine), :] = code
                codes[s, pl.ds(total * fine + base + n, 1), :] = power
            return carry

        lax.fori_loop(0, count, body, 0)
        base += count
    for s in range(scales):
        out[s] = codes[s].astype(jnp.int16)


def third_call(pieces, scales):
    vmem = pl.BlockSpec(memory_space=pltpu.VMEM)
    counts = [piece[0].shape[0] for piece in pieces]
    rows, cols = pieces[0][0].shape[1:]
    total = sum(counts) * rows // scales + POWERS
    total += -total % 16
    return pl.pallas_call(
        lambda *refs: third_kernel(counts, scales, *refs),
        in_specs=[vmem] * (3 * len(pieces)),
        out_specs=vmem,
        out_shape=jax.ShapeDtypeStruct((scales, total, cols), jnp.int16),
        scratch_shapes=[pltpu.VMEM((scales, total, cols), jnp.int32)]
        + [pltpu.VMEM((POWERS, cols // 2), f32)] * 2,
        compiler_params=pltpu.CompilerParams(vmem_limit_bytes=VMEM_BYTES),
        cost_estimate=COST,
        name="sum_third",
    )(*[ref for piece in pieces for ref in piece])


def route_kernel(devices, here, spans, block_of, *refs):
    inputs = refs[: len(spans)]
    out, blocks = refs[len(spans) : len(spans) + 2]
    values = refs[len(spans) + 2 :]
    lanes = 128
    fine, chans = blocks.shape[1:]
    groups = chans // lanes
    unit = groups * fine
    squares = jnp.zeros((fine, chans), f32)
    for got, value, runs in zip(inputs, values, spans):
        scales = got.shape[0]
        pieces = sum(run[2] for run in runs)
        for s in range(scales):
            value[s] = got[s].astype(jnp.int32).astype(f32)
        for piece, block, count in runs:

            def body(i, carry, value=value, piece=piece, block=block, pieces=pieces):
                n = piece + i
                total = jnp.zeros((fine, chans), f32)
                for s in range(value.shape[0]):
                    step = jnp.exp2(value[s, pl.ds(pieces * fine + n, 1), :]) * (1.0 / CODE)
                    total += value[s, pl.ds(pl.multiple_of(n * fine, fine), fine), :] * step
                blocks[block + i] = total
                return carry + total * total

            squares = lax.fori_loop(0, count, body, squares)
    squares = jnp.maximum(jnp.sum(jnp.sum(squares, 0, keepdims=True), 1, keepdims=True), 1e-37)
    sq_pow = jnp.floor(jnp.log2(squares))
    mant = squares * jnp.exp2(-sq_pow) * 8192.0
    mant_high = jnp.floor(mant)
    mant_low = jnp.floor((mant - mant_high) * 16384.0)
    row = lax.broadcasted_iota(jnp.int32, (16, lanes), 0)
    lane = lax.broadcasted_iota(jnp.int32, (16, lanes), 1)
    base = jnp.where(lane == 0, sq_pow, jnp.where(lane == 1, mant_high, mant_low)).astype(jnp.int32)
    base = jnp.where(row == here, base, 0)

    def send(d, carry):
        tail = base
        for k in range(here):
            b = block_of[here * d + k]
            value = blocks[jnp.maximum(b, 0)] * (b >= 0).astype(f32)
            value = jnp.concatenate(
                [value[:, g * lanes : (g + 1) * lanes] for g in range(groups)], 0
            )
            codes, power = coded(value)
            out[d, pl.ds(k * unit, unit), :] = codes.astype(jnp.int16)
            tail = jnp.where(row == k, power, tail)
        out[d, pl.ds(here * unit, 16), :] = tail.astype(jnp.int16)
        return carry

    lax.fori_loop(0, devices, send, 0, unroll=4)


def route_call(inputs, spans, block_of, devices, fine):
    here = block_of.shape[0] // devices
    chans = inputs[0].shape[2]
    rows = here * fine * chans // 128 + 16
    blocks = sum(run[2] for runs in spans for run in runs)
    vmem = pl.BlockSpec(memory_space=pltpu.VMEM)
    return pl.pallas_call(
        lambda *refs: route_kernel(devices, here, spans, *refs),
        in_specs=[pl.BlockSpec(memory_space=pltpu.SMEM)] + [vmem] * len(inputs),
        out_specs=vmem,
        out_shape=jax.ShapeDtypeStruct((devices, rows, 128), jnp.int16),
        scratch_shapes=[pltpu.VMEM((blocks, fine, chans), f32)]
        + [pltpu.VMEM(value.shape, f32) for value in inputs],
        compiler_params=pltpu.CompilerParams(vmem_limit_bytes=VMEM_BYTES),
        name="route",
    )(block_of, *inputs)


def dot_split(a, b, dims):
    dims = (dims, ((), ()))
    value = lax.dot_general(a[0], b[0], dims, preferred_element_type=f32)
    value += lax.dot_general(a[1], b[0], dims, preferred_element_type=f32)
    return value + lax.dot_general(a[0], b[1], dims, preferred_element_type=f32)


def update_kernel(
    starts, scalars, got, master, moment, second, left, right, master_new, moment_new, second_new, fresh, norm, grads, sums
):
    here, chans, half = master.shape
    lanes = 128
    groups = chans // lanes
    unit = (got.shape[1] - 16) // here
    fine = unit // groups
    for d, start in enumerate(starts):
        tail = got[d, pl.ds(here * unit, 16), :].astype(jnp.int32).astype(f32)
        sums[pl.ds(d, 1), :] = tail[here : here + 1]
        for k in range(here):
            value = got[d, pl.ds(k * unit, unit), :].astype(jnp.int32).astype(f32)
            value = value * (jnp.exp2(tail[k : k + 1]) * (1.0 / CODE))
            for g in range(groups):
                grads[k, pl.ds(start, fine), g * lanes : (g + 1) * lanes] = value[g * fine : (g + 1) * fine]
    rows = sums[...]
    lane = lax.broadcasted_iota(jnp.int32, rows.shape, 1)

    def column(index):
        return jnp.sum(jnp.where(lane == index, rows, 0.0), 1, keepdims=True)

    squares = (column(1) + column(2) * (1.0 / 16384.0)) * (1.0 / 8192.0) * jnp.exp2(column(0))
    squares = jnp.sum(squares, 0, keepdims=True) + scalars[0]
    grad_norm = jnp.sqrt(squares) / scalars[1]
    factor = clip_level / jnp.maximum(grad_norm, clip_level) / scalars[1]
    place = lax.broadcasted_iota(jnp.int32, (1, lanes), 1)
    norm[...] = jnp.where(place == 0, grad_norm, factor)
    for k in range(here):
        side = halves(left[k])
        other = halves(right[k])
        turned = dot_split(side, halves(grads[k]), ((0,), (1,)))
        turned = dot_split(halves(turned), other, ((1,), (0,))) * factor
        first = beta_one * moment[k] + (1.0 - beta_one) * turned
        spread = beta_two * second[k] + (1.0 - beta_two) * turned * turned
        moment_new[k] = first
        second_new[k] = spread
        ratio = (first / (1.0 - beta_one**STEP)) / (jnp.sqrt(spread / (1.0 - beta_two**STEP)) + adam_eps)
        back = dot_split(side, halves(ratio), ((1,), (0,)))
        back = dot_split(halves(back), other, ((1,), (1,)))
        value = master[k] - rate_matrix * (back + weight_decay * master[k])
        master_new[k] = value
        fresh[k] = value.astype(bf16)


def update_call(scalars, got, starts, master, moment, second, left, right):
    vmem = pl.BlockSpec(memory_space=pltpu.VMEM)
    here, chans, half = master.shape
    like = jax.ShapeDtypeStruct(master.shape, f32)
    return pl.pallas_call(
        lambda *refs: update_kernel(starts, *refs),
        in_specs=[pl.BlockSpec(memory_space=pltpu.SMEM)] + [vmem] * 6,
        out_specs=[vmem] * 5,
        out_shape=[
            like,
            like,
            like,
            jax.ShapeDtypeStruct(master.shape, bf16),
            jax.ShapeDtypeStruct((1, 128), f32),
        ],
        scratch_shapes=[
            pltpu.VMEM((here, half, chans), f32),
            pltpu.VMEM((len(starts), 128), f32),
        ],
        compiler_params=pltpu.CompilerParams(vmem_limit_bytes=VMEM_BYTES),
        name="update",
    )(scalars, got, master, moment, second, left, right)


def place_kernel(depth, taps, half, arrays, array, item, *refs):
    sources = refs[:arrays]
    conv, head, conv_store, head_store, in_sems, out_sems = refs[arrays:]
    blocks = array.shape[0]
    count = 2 * depth * taps

    def load(b, source):
        if b < count:
            target = conv_store.at[b // 2, :, pl.ds((b % 2) * half, half)]
        else:
            target = head_store.at[b - count]
        return pltpu.make_async_copy(source, target, in_sems.at[b])

    for b in range(blocks):
        for g in range(arrays):

            @pl.when(array[b] == g)
            def _(b=b, g=g):
                load(b, sources[g].at[item[b]]).start()

    stores = []
    for b in range(blocks):
        load(b, sources[0].at[0]).wait()
        if b >= count:
            stores.append(
                pltpu.make_async_copy(
                    head_store.at[b - count], head.at[b - count], out_sems.at[len(stores)]
                )
            )
            stores[-1].start()
        elif b % 2 == 1:
            tap = b // 2
            stores.append(
                pltpu.make_async_copy(
                    conv_store.at[tap], conv.at[tap // taps, tap % taps], out_sems.at[len(stores)]
                )
            )
            stores[-1].start()
    for store in stores:
        store.wait()


def place_blocks(sources, array, item, depth, taps):
    blocks = array.shape[0]
    chans, half = sources[0].shape[1:]
    heads = blocks - 2 * depth * taps
    anywhere = pl.BlockSpec(memory_space=pl.ANY)
    smem = pl.BlockSpec(memory_space=pltpu.SMEM)
    return pl.pallas_call(
        lambda *refs: place_kernel(depth, taps, half, len(sources), *refs),
        in_specs=[smem, smem] + [anywhere] * len(sources),
        out_specs=[anywhere, anywhere],
        out_shape=[
            jax.ShapeDtypeStruct((depth, taps, chans, 2 * half), bf16),
            jax.ShapeDtypeStruct((heads, chans, half), bf16),
        ],
        scratch_shapes=[
            pltpu.VMEM((depth * taps, chans, 2 * half), bf16),
            pltpu.VMEM((heads, chans, half), bf16),
            pltpu.SemaphoreType.DMA((blocks,)),
            pltpu.SemaphoreType.DMA((depth * taps + heads,)),
        ],
        compiler_params=pltpu.CompilerParams(vmem_limit_bytes=VMEM_BYTES),
        name="place_blocks",
    )(array, item, *sources)


def spread_slots(own, lay, z, beside):
    def line(value, pairs):
        return permute(
            value, [(lay.dev(a, i), lay.dev(b, i)) for a, b in pairs for i in range(lay.imgs)]
        )

    def over_x(value):
        return permute(value, lay.swap(2))

    def over_y(value):
        return permute(value, lay.swap(4))

    inner = (z == 1) | (z == 2)
    z_one = line(own, [(0, 1), (1, 0), (2, 3), (3, 2)])
    x_own = over_x(own)
    y_own = over_y(own)
    middle_own = line(own, [(1, 2), (2, 1)])
    z_one, x_own, y_own = lax.optimization_barrier((z_one, x_own, y_own))
    middle_one = line(z_one, [(1, 2), (2, 1)])
    xy_own = over_x(y_own)
    y_one = over_y(z_one)
    outer_own = line(middle_own, [(1, 0), (2, 3)])
    outer_one = line(middle_one, [(1, 0), (2, 3)])
    z_two = jnp.where(inner, middle_one, outer_own)
    x_one = over_x(z_one)
    y_two = over_y(after(z_two, *beside))
    x_two = over_x(z_two)
    z_three = jnp.where(inner, middle_own, outer_one)
    xy_one = over_y(x_one)
    y_three = over_y(z_three)
    x_three = over_x(z_three)
    xy_three = over_y(x_three)
    xy_two = over_x(y_two)
    bundles = [
        jnp.concatenate(v, 0)
        for v in (
            (own, z_one, x_own, y_own),
            (z_two, z_three, xy_own, x_one),
            (y_one, x_two, y_two, xy_one),
            (x_three, y_three, xy_two, xy_three),
        )
    ]
    return bundles + [permute(v, lay.swap(1)) for v in bundles]


PLACES = (0, 1, 4, 5, 3, 8, 10, 13, 2, 7, 9, 12, 6, 11, 14, 15)


def pick(value, index, axis):
    return lax.dynamic_index_in_dim(value, index, axis, keepdims=False)


class Sum:
    def __init__(self, made, ids, lay):
        self.keep, self.send = made[:2], made[2:]
        self.ids, self.lay = ids, lay

    def first(self):
        self.got = [permute(self.send[0], self.lay.swap(2)), permute(self.send[1], self.lay.swap(4))]

    def second(self, *wait):
        got = lax.optimization_barrier((*self.got, *wait))
        self.keep, *self.send = second_call(self.ids, *self.keep, *got[:2])
        self.got = [permute(self.send[0], self.lay.swap(4)), permute(self.send[1], self.lay.swap(2))]

    def third(self, *wait):
        got = lax.optimization_barrier((*self.got, *wait))
        return [self.keep, *got[:2]]


def soap_update(master, moment, second, left, right, grads):
    turned = jnp.einsum("sij,ski->sjk", left, grads, precision=highest)
    turned = jnp.einsum("sjk,skl->sjl", turned, right, precision=highest)
    moment = beta_one * moment + (1.0 - beta_one) * turned
    second = beta_two * second + (1.0 - beta_two) * turned * turned
    ratio = moment / (1.0 - beta_one**STEP) / (jnp.sqrt(second / (1.0 - beta_two**STEP)) + adam_eps)
    back = jnp.einsum("sij,sjk->sik", left, ratio, precision=highest)
    back = jnp.einsum("sik,slk->sil", back, right, precision=highest)
    return (master - rate_matrix * (back + weight_decay * master), moment, second)


def vector_update(params, moment, second, grads):
    moment = beta_one * moment + (1.0 - beta_one) * grads
    second = beta_two * second + (1.0 - beta_two) * grads * grads
    ratio = moment / (1.0 - beta_one**STEP) / (jnp.sqrt(second / (1.0 - beta_two**STEP)) + adam_eps)
    return (params - rate_vector * (ratio + weight_decay * params), moment, second)


def butterfly(value, lay):
    bit = 1
    while bit < lay.imgs:
        value = value + permute(value, lay.swap(bit))
        bit *= 2
    bit = 1
    while bit < lay.scales:
        value = value + permute(value, lay.scale_swap(bit))
        bit *= 2
    return value


def local(
    images,
    valid_mask,
    scale_cols,
    boxes,
    normal_targets,
    dense_targets,
    affine_scale,
    affine_shift,
    conv_bf16,
    head_bf16,
    vectors,
    vec_m,
    vec_v,
    master,
    slot_m,
    slot_v,
    basis_left,
    basis_right,
    owner_slot,
):
    held, width, chans = (images.shape[1], images.shape[2], images.shape[3])
    heads_count, head_width = (head_bf16.shape[0], head_bf16.shape[2])
    wide = heads_count * head_width
    depth, taps = (conv_bf16.shape[0], conv_bf16.shape[1])
    scales, imgs = lax.axis_size("scale"), lax.axis_size("img")
    lay = Layout(scales, imgs)
    rows = held // scales
    z = lax.axis_index("scale")
    img = lax.axis_index("img")
    group, core = img // 2, img % 2
    place = jnp.where(group % 2 == 0, z, scales - 1 - z)
    mine = 2 * (place % 2) + core

    widths = [width >> s for s in range(scales)]
    starts = []
    at = 0
    for w in widths:
        starts.append(at)
        at += w + GAP
    cols = at
    col_iota = jnp.arange(cols, dtype=jnp.int32)
    valid_col = jnp.zeros((cols,), jnp.bool_)
    for s in range(scales):
        valid_col |= (col_iota >= starts[s]) & (col_iota < starts[s] + scale_cols[s])
    col_mask = valid_col.astype(f32)[None, :, None]

    own = images[0]
    fine = [
        permute(own[rows * k : rows * (k + 1)], lay.rows_round(k, [0])) for k in range(scales)
    ]
    coarse = []
    for k in range(scales):
        piece = (k + z) % scales
        send = lax.dynamic_slice_in_dim(own[:, : widths[1]], piece * rows, rows, 0)
        coarse.append(permute(send, lay.rows_round(k, range(1, scales))))
    parts = [(fine[0] + fine[1]) + (fine[2] + fine[3])]
    for s in range(1, scales):
        got = 0.0
        for k in range(scales):
            got = got + jnp.where((mine - k) % scales == s, coarse[k][:, : widths[s]], 0)
        parts.append(got.astype(bf16))
    spread = []
    for s in range(scales):
        spread.append(parts[s])
        spread.append(jnp.zeros((rows, GAP, chans), bf16))
    x_zero = (jnp.concatenate(spread, 1) * col_mask.astype(bf16)).reshape(rows * cols, chans)

    valid_mask, boxes, normal_targets, scale_cols, *_ = lax.optimization_barrier(
        (valid_mask, boxes, normal_targets, scale_cols, *fine, *coarse)
    )

    mask_all = valid_mask.astype(f32)
    pixels = jnp.arange(held * width, dtype=jnp.int32)
    hits = jnp.sum((boxes[:, None] == pixels[None, :]).astype(f32), 0).reshape(held, width)
    packed = jnp.concatenate(
        [mask_all[None], (mask_all + box_weight * hits)[None], normal_targets], 0
    )
    packed_other = permute(packed, lay.swap(1))
    from_own = place // (scales // 2) == core
    packed = jnp.where(from_own, packed, packed_other)
    packed = lax.dynamic_slice_in_dim(packed, mine * rows, rows, 1).reshape(5, rows * width)
    valid, weight = packed[0][:, None], packed[1][:, None]
    normals = jnp.pad(packed[2:].T, ((0, 0), (0, 128 - 3)))
    tables = table_call(scale_cols, starts, widths, width, cols)
    gamma = vectors[:chans]
    bias = vectors[chans:]
    core_here = core.reshape(1)
    flat_mask = jnp.broadcast_to(col_mask, (rows, cols, 1)).reshape(rows * cols, 1)

    all_taps = conv_bf16.reshape(depth, 3, 3 * chans, chans)

    size = rows * cols

    def neighbours(value, facing):
        return permute(value, lay.swap(1)), permute(facing, lay.outward())

    def gain_of(depth_idx):
        return affine_scale[depth_idx].reshape(1, chans), affine_shift[depth_idx].reshape(1, chans)

    pre_shape = jax.ShapeDtypeStruct((size, chans), f32)
    buffer_shape = jax.ShapeDtypeStruct((size + cols, chans), bf16)
    grad_shape = jax.ShapeDtypeStruct((size, chans), bf16)
    facing_zero = lax.dynamic_slice_in_dim(x_zero, core * (rows - 1) * cols, cols, 0)
    partner_zero, outer_zero = neighbours(x_zero, facing_zero)
    arrived = []
    for r in range(2):
        send = lax.dynamic_slice_in_dim(
            dense_targets, ((r + z) % 2) * (held // 2), held // 2, 0
        )
        got = permute(after(send, (fine[1], outer_zero)[r]), lay.chip_round(r))
        arrived.append(got.reshape(2, rows * width, dense_targets.shape[2]))
    pre_zero, x_one, facing_one = conv_call(
        first_conv_kernel,
        core_here,
        x_zero,
        partner_zero,
        outer_zero,
        *gain_of(0),
        flat_mask,
        [],
        all_taps,
        0,
        [pre_shape, buffer_shape, jax.ShapeDtypeStruct((cols, chans), bf16)],
        False,
        "conv_rows",
    )
    partner_one, outer_one = neighbours(x_one, facing_one)
    give = jnp.stack([pick(got, 1 - core, 0) for got in arrived])
    arrived.append(permute(after(give, outer_one), lay.swap(1)))
    grad_one, facing_grad, grad_mine, grad_pack, grad_gamma, grad_bias, loss_parts = head_call(
        core_here,
        place.reshape(1),
        x_one,
        partner_one,
        outer_one,
        (*gain_of(1), flat_mask, gamma.reshape(1, chans), bias.reshape(1, wide)),
        (weight, valid, normals),
        head_bf16,
        arrived,
        tables,
        all_taps,
        1,
    )
    part = head_width // 2
    half = chans // 2
    staged = imgs == 8 and scales == 4
    x, y = (img // 2) % 2, img // 4
    ids = jnp.stack([core, x, y])
    grad_partner, grad_outer = neighbours(grad_one, facing_grad)
    pack_got = permute(grad_pack, lay.swap(1))
    conv_grad_one = kernel_grad(
        ids, x_one, partner_one, outer_one, grad_partner, grad_one, grad_partner, part, staged
    )
    if staged:
        early = Sum(conv_grad_one, ids, lay)
        early.first()
        pack_got = after(pack_got, *early.send)
    head_grad = head_grad_call(ids, grad_mine, grad_pack, pack_got, part, staged)
    if staged:
        middle = Sum(head_grad, ids, lay)
        middle.first()
        grad_outer = after(grad_outer, *middle.send)
    (grad_zero,) = conv_call(
        back_conv_kernel,
        core_here,
        grad_one,
        grad_partner,
        grad_outer,
        *gain_of(0),
        flat_mask,
        [pre_zero],
        all_taps,
        1,
        [grad_shape],
        True,
        "conv_back",
    )
    grad_zero_partner = permute(grad_zero, lay.swap(1))
    if staged:
        early.second(grad_zero)
        grad_zero_partner = after(grad_zero_partner, *early.send)
    conv_grad_zero = kernel_grad(
        ids,
        x_zero,
        partner_zero,
        outer_zero,
        partner_one,
        grad_zero,
        grad_zero_partner,
        part,
        staged,
    )
    if staged:
        late = Sum(conv_grad_zero, ids, lay)
        late.first()
    grad_gamma, grad_bias = grad_gamma.reshape(chans), grad_bias.reshape(wide)
    own_count = jnp.where(z == 0, jnp.sum(mask_all), 0.0).reshape(1)
    loss_parts = jnp.concatenate([loss_parts[0, :2], own_count])

    vec_rows = jnp.concatenate(
        [grad_gamma, grad_bias, loss_parts, jnp.zeros((-(chans + wide + 3) % 1024,), f32)]
    ).reshape(-1, 128)
    vec_sum = butterfly(vec_rows, lay).reshape(-1)
    totals = vec_sum[chans + wide : chans + wide + 2]
    count = vec_sum[chans + wide + 2]
    grad_vec = vec_sum[: chans + wide]
    vec_squares = jnp.sum(grad_vec * grad_vec)

    blocks_count = owner_slot.shape[0]
    slots_here = master.shape[0]
    slots = slots_here * scales * imgs
    slot_ids = jnp.arange(slots, dtype=jnp.int32)
    match = slot_ids[:, None] == owner_slot[None, :]
    block_of = jnp.sum(
        jnp.where(match, jnp.arange(blocks_count, dtype=jnp.int32)[None, :], 0), 1
    )
    owned_f = jnp.any(match, 1).astype(f32)

    if staged:
        early_line = third_call([early.third(*late.send)], scales)
        early_line = lax.all_to_all(early_line, "scale", 0, 0, tiled=True)
        middle.second(*late.send)
        late.second()
        late_line = third_call([late.third(), middle.third()], scales)
        late_line = lax.all_to_all(late_line, "scale", 0, 0, tiled=True)
        conv_pieces = 2 * taps
        payload = route_call(
            [early_line, late_line],
            [
                [(0, conv_pieces, conv_pieces)],
                [(0, 0, conv_pieces), (conv_pieces, 2 * conv_pieces, heads_count)],
            ],
            jnp.where(owned_f > 0, block_of, -1),
            scales * imgs,
            part // 4 // scales,
        )
        got = lax.all_to_all(payload, AXES, 0, 0, tiled=True)
        starts_here = [
            (i % 2) * (half // 2) + (i // 2 % 2) * (half // 4) + (i // 4) * (half // 8) + s * (half // 32)
            for s, i in lay.all_devices()
        ]
        master_new, slot_m_new, slot_v_new, fresh, norm = update_call(
            jnp.stack([vec_squares, count]),
            got,
            starts_here,
            master,
            slot_m,
            slot_v,
            basis_left,
            basis_right,
        )
        grad_norm, factor = norm[0, 0], norm[0, 1]
        vec_out = vector_update(vectors, vec_m, vec_v, grad_vec * factor)
        sources = spread_slots(fresh, lay, z, vec_out)
        owner = owner_slot // slots_here
        other_img = owner % imgs
        turn = other_img ^ img
        step = ((turn >> 1) & 1) * 8 + (turn >> 2) * 4 + ((owner // imgs) ^ z)
        place = jnp.sum(
            jnp.where(
                step[:, None] == jnp.arange(16, dtype=jnp.int32)[None, :],
                jnp.asarray(PLACES, jnp.int32)[None, :],
                0,
            ),
            1,
        )
        array = place // 4 + 4 * (turn & 1)
        item = (place % 4) * slots_here + owner_slot % slots_here
    else:
        parts = jnp.concatenate(
            [v.reshape(2 * taps, part, chans) for v in (conv_grad_zero, conv_grad_one)]
            + [head_grad[0].reshape(heads_count, part, chans)],
            0,
        )
        none = jnp.zeros_like(parts)
        blocks = jnp.concatenate(
            [jnp.where(core == 0, parts, none), jnp.where(core == 1, parts, none)], 1
        )
        by_slot = blocks[block_of] * owned_f[:, None, None]
        owned = lax.psum_scatter(by_slot, AXES, scatter_dimension=0, tiled=True)
        squares_sum = lax.psum(jnp.sum(owned * owned), AXES) + vec_squares

        grad_norm = jnp.sqrt(squares_sum) / count
        factor = clip_level / jnp.maximum(grad_norm, clip_level) / count
        master_new, slot_m_new, slot_v_new = soap_update(
            master, slot_m, slot_v, basis_left, basis_right, owned * factor
        )
        sources = [lax.all_gather(master_new.astype(bf16), AXES, axis=0, tiled=True)]
        array, item = jnp.zeros_like(owner_slot), owner_slot
        vec_out = vector_update(vectors, vec_m, vec_v, grad_vec * factor)
    vec_new, vec_m_new, vec_v_new = vec_out
    conv_copy, head_copy = place_blocks(sources, array, item, depth, taps)
    loss = jnp.stack([totals[0] / wide + totals[1], count])
    return (
        loss,
        grad_norm,
        vec_new,
        vec_m_new,
        vec_v_new,
        master_new,
        slot_m_new,
        slot_v_new,
        conv_copy,
        head_copy,
    )


def solution(mesh):
    in_specs = (
        P("scale", "img", None, None),
        P("img", None),
        P(),
        P("img"),
        P(None, "img", None),
        P("img", None, "scale"),
        P(),
        P(),
        P(),
        P(),
        P(),
        P(),
        P(),
        P(("scale", "img"), None, None),
        P(("scale", "img"), None, None),
        P(("scale", "img"), None, None),
        P(("scale", "img"), None, None),
        P(("scale", "img"), None, None),
        P(),
    )
    out_specs = (
        P(),
        P(),
        P(),
        P(),
        P(),
        P(("scale", "img"), None, None),
        P(("scale", "img"), None, None),
        P(("scale", "img"), None, None),
        P(),
        P(),
    )
    return jax.shard_map(local, mesh=mesh, in_specs=in_specs, out_specs=out_specs, check_vma=False)
```

```python
import jax
import jax.numpy as jnp
from jax import lax
from jax.experimental import pallas as pl
from jax.experimental.pallas import tpu as pltpu
from jax.sharding import PartitionSpec as P

STEP = 5

beta_one = 0.5
beta_two = 0.5
adam_eps = 1e-08
rate_matrix = 0.01
rate_vector = 0.2
weight_decay = 0.01
clip_level = 0.001
box_weight = 2.0
norm_eps = 1e-05
highest = lax.Precision.HIGHEST
bf16 = jnp.bfloat16
f32 = jnp.float32
AXES = ("scale", "img")
GAP = 16
CODE = 32767.0
CHUNK = 544
MIB = 2**20
COST = pl.CostEstimate(flops=5 * 10**9, bytes_accessed=10**6, transcendentals=0)
TINY = pl.CostEstimate(flops=1, bytes_accessed=1, transcendentals=0)
LONG = pl.CostEstimate(flops=10**11, bytes_accessed=10**6, transcendentals=0)


class Layout:
    def __init__(self, scales, imgs):
        self.scales = scales
        self.imgs = imgs

    def pos(self, group, scale):
        return scale if group % 2 == 0 else self.scales - 1 - scale

    def dev(self, scale, img):
        return scale * self.imgs + img

    def at(self, group, place, core):
        return self.dev(self.pos(group, place), 2 * group + core)

    def all_devices(self):
        return [(s, i) for s in range(self.scales) for i in range(self.imgs)]

    def swap(self, bit):
        return [(self.dev(s, i), self.dev(s, i ^ bit)) for s, i in self.all_devices()]

    def turn(self, step):
        return [
            (self.dev(s, i), self.dev((s + step) % self.scales, i)) for s, i in self.all_devices()
        ]

    def scale_swap(self, bit):
        return [(self.dev(s, i), self.dev(s ^ bit, i)) for s, i in self.all_devices()]

    def rows_round(self, shift, sources):
        pairs = []
        for s in sources:
            for i in range(self.imgs):
                group, core = i // 2, i % 2
                piece = (shift + s) % self.scales
                place = (self.scales // 2) * core + piece // 2
                pairs.append((self.dev(s, i), self.at(group, place, piece % 2)))
        return pairs

    def row_order(self):
        groups = self.imgs // 2
        return [
            self.at(j, place, c) for j in range(groups) for place in range(self.scales) for c in range(2)
        ]

    def outward(self):
        order = self.row_order()
        pairs = []
        for at in range(1, len(order) - 1, 2):
            pairs += [(order[at], order[at + 1]), (order[at + 1], order[at])]
        return pairs


def permute(value, pairs):
    return lax.ppermute(value, AXES, pairs)


def after(value, *others):
    return lax.optimization_barrier((value, *others))[0]


def table_kernel(starts, widths, width, cols_ref, up_high, up_low, down_high, down_low):
    def table(shape, coarse_axis):
        place = lax.broadcasted_iota(jnp.int32, shape, coarse_axis)
        fine = lax.broadcasted_iota(jnp.int32, shape, 1 - coarse_axis)
        total = jnp.zeros(shape, f32)
        bits = (2 * width).bit_length() - 1
        for s, (start, span) in enumerate(zip(starts, widths)):
            columns = cols_ref[s]
            numer = jnp.maximum((2 * fine + 1) * columns - width, 0)
            lower = lax.shift_right_logical(numer, bits)
            frac = (numer - lax.shift_left(lower, bits)).astype(f32) * (0.5 / width)
            upper = jnp.minimum(lower + 1, columns - 1)
            coarse = place - start
            inside = (coarse >= 0) & (coarse < span)
            part = jnp.where(coarse == lower, 1.0 - frac, 0.0) + jnp.where(coarse == upper, frac, 0.0)
            total += jnp.where(inside, part, 0.0)
        return halves(total)

    up_high[...], up_low[...] = table(up_high.shape, 1)
    down_high[...], down_low[...] = table(down_high.shape, 0)


def table_call(scale_cols, starts, widths, width, cols):
    vmem = pl.BlockSpec(memory_space=pltpu.VMEM)
    return pl.pallas_call(
        lambda *refs: table_kernel(starts, widths, width, *refs),
        in_specs=[pl.BlockSpec(memory_space=pltpu.SMEM)],
        out_specs=[vmem] * 4,
        out_shape=[jax.ShapeDtypeStruct((width, cols), bf16)] * 2
        + [jax.ShapeDtypeStruct((cols, width), bf16)] * 2,
        cost_estimate=TINY,
        name="tables",
    )(scale_cols)


def halves(value):
    high = value.astype(bf16)
    return high, (value - high.astype(f32)).astype(bf16)


def whole(shape):
    return pl.BlockSpec(shape, lambda *_: (0,) * len(shape))


def spread_taps(store, at, row, cols, chans):
    base = pl.multiple_of(at * cols, 16)
    value = row.astype(f32)
    store[pl.ds(base, cols), pl.ds(0, chans)] = pltpu.roll(value, 1, 0).astype(bf16)
    store[pl.ds(base, cols), pl.ds(chans, chans)] = row
    store[pl.ds(base, cols), pl.ds(2 * chans, chans)] = pltpu.roll(value, cols - 1, 0).astype(bf16)


def load_taps(rows, cols, chans, core, cur, partner, outer, taps):
    for r in range(rows):
        spread_taps(taps, r + 1, cur[pl.ds(r * cols, cols), :], cols, chans)
    outside = (rows + 1) * core
    spread_taps(taps, outside, outer[...], cols, chans)
    inside = pl.multiple_of((rows - 1) * core * cols, 16)
    spread_taps(taps, rows + 1 - outside, partner[pl.ds(inside, cols), :], cols, chans)


def fetch(source, layer, target, sems):
    copies = [pltpu.make_async_copy(source.at[layer, a], target.at[a], sems.at[a]) for a in range(3)]
    for copy in copies:
        copy.start()
    return copies


def conv_into(pre, taps, weights, copies, cols):
    size = pre.shape[0]
    for a in range(3):
        copies[a].wait()
        value = jnp.dot(taps[pl.ds(a * cols, size), :], weights[a], preferred_element_type=f32)
        if a == 0:
            pre[...] = value
        else:
            pre[...] += value


def gelu_slope(u):
    root = 0.7978845608028654
    bend = 0.044715
    th = jnp.tanh(root * (u + bend * u * u * u))
    return 0.5 * (1.0 + th) + 0.5 * u * (1.0 - th * th) * root * (1.0 + 3.0 * bend * u * u)


def face(buffer, facing, core, rows, cols):
    at = pl.multiple_of(cols + core * (rows - 1) * cols, 16)
    facing[...] = buffer[pl.ds(at, cols), :]


def first_conv_kernel(
    rows, cols, chans, layer, core_ref, cur, partner, outer, gain, shift, mask, w_hbm, pre, out, facing, taps, w, sems
):
    copies = fetch(w_hbm, layer, w, sems)
    load_taps(rows, cols, chans, core_ref[0], cur, partner, outer, taps)
    out[pl.ds(0, cols), :] = outer[...]
    conv_into(pre, taps, w, copies, cols)

    def body(i, carry):
        at = pl.ds(pl.multiple_of(i * CHUNK, 16), CHUNK)
        u = pre[at, :] * gain[...] + shift[...]
        to = pl.ds(pl.multiple_of(cols + i * CHUNK, 16), CHUNK)
        out[to, :] = (jax.nn.gelu(u) * mask[at, :]).astype(bf16)
        return carry

    lax.fori_loop(0, rows * cols // CHUNK, body, 0)
    face(out, facing, core_ref[0], rows, cols)


def back_conv_kernel(
    rows, cols, chans, layer, core_ref, cur, partner, outer, gain, shift, mask, pre_in, w_hbm, out, taps, w, sems, acc
):
    copies = fetch(w_hbm, layer, w, sems)
    size = rows * cols
    cur = cur.at[pl.ds(cols, size)]
    partner = partner.at[pl.ds(cols, size)]
    load_taps(rows, cols, chans, core_ref[0], cur, partner, outer, taps)
    for a in range(3):
        copies[2 - a].wait()
        value = 0.0
        for b in range(3):
            value += lax.dot_general(
                taps[pl.ds(a * cols, size), b * chans : (b + 1) * chans],
                w[2 - a, (2 - b) * chans : (3 - b) * chans, :],
                (((1,), (1,)), ((), ())),
                preferred_element_type=f32,
            )
        if a == 0:
            acc[...] = value
        else:
            acc[...] += value

    def body(i, carry):
        at = pl.ds(pl.multiple_of(i * CHUNK, 16), CHUNK)
        u = pre_in[at, :] * gain[...] + shift[...]
        out[at, :] = (acc[at, :] * mask[at, :] * gelu_slope(u) * gain[...]).astype(bf16)
        return carry

    lax.fori_loop(0, size // CHUNK, body, 0)


def conv_call(kernel, core, cur, partner, outer, gain, shift, mask, more, weights, layer, shapes, acc, name):
    cols, chans = outer.shape
    rows = 2
    size = rows * cols
    scratch = [
        pltpu.VMEM(((rows + 2) * cols, 3 * chans), bf16),
        pltpu.VMEM((3, 3 * chans, chans), bf16),
        pltpu.SemaphoreType.DMA((3,)),
    ]
    if acc:
        scratch.append(pltpu.VMEM((size, chans), f32))
    vmem = pl.BlockSpec(memory_space=pltpu.VMEM)
    return pl.pallas_call(
        lambda *refs: kernel(rows, cols, chans, layer, *refs),
        in_specs=[pl.BlockSpec(memory_space=pltpu.SMEM)]
        + [vmem] * (6 + len(more))
        + [pl.BlockSpec(memory_space=pl.ANY)],
        out_specs=[vmem for _ in shapes],
        out_shape=shapes,
        scratch_shapes=scratch,
        compiler_params=pltpu.CompilerParams(vmem_limit_bytes=(30 if acc else 30) * MIB),
        cost_estimate=COST if acc else TINY,
        name=name,
    )(core, cur, partner, outer, gain, shift, mask, *more, weights)


def head_kernel(
    rows,
    cols,
    width,
    scales,
    layer,
    core_ref,
    cur,
    partner,
    outer,
    gain,
    shift,
    mask,
    gamma,
    bias,
    weight,
    valid,
    normals,
    heads_hbm,
    target_hbm,
    up_high_hbm,
    up_low_hbm,
    down_high_hbm,
    down_low_hbm,
    w_hbm,
    out,
    facing,
    mine,
    pack,
    dgamma,
    dbias,
    sums,
    taps,
    w,
    sems,
    pre,
    y_ref,
    tapped,
    raised_high,
    raised_low,
    dj_low,
    back,
    target,
    heads,
    target_in,
    up_high,
    up_low,
    down_high,
    down_low,
    more_sems,
):
    chans = outer.shape[1]
    size = rows * cols
    core = core_ref[0]
    copies = fetch(w_hbm, layer, w, sems)
    pairs = (
        (up_high_hbm, up_high),
        (up_low_hbm, up_low),
        (target_hbm, target_in),
        (heads_hbm, heads),
        (down_high_hbm, down_high),
        (down_low_hbm, down_low),
    )
    loads = [pltpu.make_async_copy(a, b, more_sems.at[i]) for i, (a, b) in enumerate(pairs)]
    for load in loads:
        load.start()
    cur = cur.at[pl.ds(cols, size)]
    partner = partner.at[pl.ds(cols, size)]
    load_taps(rows, cols, chans, core, cur, partner, outer, taps)
    out[pl.ds(0, cols), :] = outer[...]
    conv_into(pre, taps, w, copies, cols)

    def forward(i, carry):
        at = pl.ds(0, size)
        u = pre[at, :] * gain[...] + shift[...]
        y = jax.nn.gelu(u) * mask[at, :]
        y_ref[at, :] = y
        scale = lax.rsqrt(jnp.mean(y * y, -1, keepdims=True) + norm_eps)
        tapped[at, :] = (gamma[...] * y * scale).astype(bf16)
        return carry

    forward(0, 0)
    for load in loads:
        load.wait()
    part = target_in.shape[2]
    for s in range(scales):
        target[:, s * part : (s + 1) * part] = target_in[s]

    half_wide = mine.shape[1]
    for r in range(rows):
        line = tapped[pl.ds(r * cols, cols), :]
        value = jnp.dot(up_high[...], line, preferred_element_type=f32)
        value += jnp.dot(up_low[...], line, preferred_element_type=f32)
        high = value.astype(bf16)
        raised_high[pl.ds(r * width, width), :] = high
        pack[pl.ds(r * width, width), pl.ds(half_wide, chans)] = high
        raised_low[pl.ds(r * width, width), :] = (value - high.astype(f32)).astype(bf16)

    step = heads.shape[2]
    wide = heads.shape[0] * step
    dense = jnp.zeros((1, step), f32)
    normal = jnp.zeros((1, 1), f32)
    for t in range(wide // step):
        joined = jnp.dot(raised_high[...], heads[t], preferred_element_type=f32)
        joined += jnp.dot(raised_low[...], heads[t], preferred_element_type=f32)
        joined += float(scales) * bias[:, t * step : (t + 1) * step]
        diff = joined - target[:, t * step : (t + 1) * step].astype(f32)
        pulled = weight[...] * diff
        dense += jnp.sum(pulled * diff, 0, keepdims=True)
        grad = pulled * (1.0 / wide)
        if t == 0:
            lane = lax.broadcasted_iota(jnp.int32, (joined.shape[0], 128), 1)
            n = jnp.where(lane < 3, joined[:, :128], 0.0)
            other = normals[...]
            inner = jnp.sum(n * other, -1, keepdims=True)
            own_sq = jnp.sum(n * n, -1, keepdims=True) + 1.0
            other_sq = jnp.sum(other * other, -1, keepdims=True) + 1.0
            root = lax.rsqrt(own_sq * other_sq)
            normal += jnp.sum(valid[...] * (1.0 - inner * root), 0, keepdims=True)
            turn = valid[...] * root * (inner / own_sq * n - other)
            grad = jnp.concatenate([grad[:, :128] + turn, grad[:, 128:]], 1)
        dbias[:, t * step : (t + 1) * step] = float(scales) * jnp.sum(grad, 0, keepdims=True)
        dj_low[:, t * step : (t + 1) * step] = grad.astype(bf16)
        half = step // 2
        first, second = grad[:, :half], grad[:, half:]
        mine[:, t * half : (t + 1) * half] = jnp.where(core == 0, first, second).astype(bf16)
        pack[:, t * half : (t + 1) * half] = jnp.where(core == 0, second, first).astype(bf16)
    lane = lax.broadcasted_iota(jnp.int32, (1, 128), 1)
    total = 0.5 * jnp.sum(dense, 1, keepdims=True)
    sums[...] = jnp.where(lane == 0, total, jnp.where(lane == 1, normal, 0.0))

    draised = 0.0
    for t in range(heads.shape[0]):
        draised += lax.dot_general(
            dj_low[:, t * step : (t + 1) * step],
            heads[t],
            (((1,), (1,)), ((), ())),
            preferred_element_type=f32,
        )
    for r in range(rows):
        part = draised[r * width : (r + 1) * width]
        high = part.astype(bf16)
        low = (part - high.astype(f32)).astype(bf16)
        value = jnp.dot(down_high[...], high, preferred_element_type=f32)
        value += jnp.dot(down_low[...], high, preferred_element_type=f32)
        value += jnp.dot(down_high[...], low, preferred_element_type=f32)
        back[pl.ds(r * cols, cols), :] = value

    def backward(i, carry):
        at = pl.ds(0, size)
        y = y_ref[at, :]
        dt = back[at, :]
        scale = lax.rsqrt(jnp.mean(y * y, -1, keepdims=True) + norm_eps)
        dty = dt * y
        pull = jnp.mean(gamma[...] * dty, -1, keepdims=True)
        dy = gamma[...] * dt * scale - y * (scale * scale * scale * pull)
        u = pre[at, :] * gain[...] + shift[...]
        to = pl.ds(cols, size)
        out[to, :] = (dy * mask[at, :] * gelu_slope(u) * gain[...]).astype(bf16)
        return carry + jnp.sum(dty * scale, 0, keepdims=True)

    dgamma[...] = backward(0, jnp.zeros((1, chans), f32))
    face(out, facing, core, rows, cols)


def head_call(core, cur, partner, outer, vectors, pixel, heads, target, tables, weights, layer):
    cols, chans = outer.shape
    rows = 2
    size = rows * cols
    width = tables[0].shape[0]
    wide = heads.shape[0] * heads.shape[2]
    pixels = rows * width
    scales = target.shape[0]
    vmem = pl.BlockSpec(memory_space=pltpu.VMEM)
    anywhere = pl.BlockSpec(memory_space=pl.ANY)
    shapes = [
        jax.ShapeDtypeStruct((size + cols, chans), bf16),
        jax.ShapeDtypeStruct((cols, chans), bf16),
        jax.ShapeDtypeStruct((pixels, wide // 2), bf16),
        jax.ShapeDtypeStruct((pixels, wide // 2 + chans), bf16),
        jax.ShapeDtypeStruct((1, chans), f32),
        jax.ShapeDtypeStruct((1, wide), f32),
        jax.ShapeDtypeStruct((1, 128), f32),
    ]
    return pl.pallas_call(
        lambda *refs: head_kernel(rows, cols, width, scales, layer, *refs),
        in_specs=[pl.BlockSpec(memory_space=pltpu.SMEM)] + [vmem] * 11 + [anywhere] * 7,
        out_specs=[vmem for _ in shapes],
        out_shape=shapes,
        scratch_shapes=[
            pltpu.VMEM(((rows + 2) * cols, 3 * chans), bf16),
            pltpu.VMEM((3, 3 * chans, chans), bf16),
            pltpu.SemaphoreType.DMA((3,)),
            pltpu.VMEM((size, chans), f32),
            pltpu.VMEM((size, chans), f32),
            pltpu.VMEM((size, chans), bf16),
            pltpu.VMEM((pixels, chans), bf16),
            pltpu.VMEM((pixels, chans), bf16),
            pltpu.VMEM((pixels, wide), bf16),
            pltpu.VMEM((size, chans), f32),
            pltpu.VMEM((pixels, wide), bf16),
            pltpu.VMEM(heads.shape, bf16),
            pltpu.VMEM(target.shape, bf16),
        ]
        + [pltpu.VMEM(table.shape, bf16) for table in tables]
        + [pltpu.SemaphoreType.DMA((6,))],
        compiler_params=pltpu.CompilerParams(vmem_limit_bytes=56 * MIB),
        cost_estimate=COST,
        name="head_rows",
    )(core, cur, partner, outer, *vectors, *pixel, heads, target, *tables, weights)


def coded(value):
    top = jnp.max(jnp.abs(value), 0, keepdims=True)
    power = jnp.clip(jnp.ceil(jnp.log2(top)), -100.0, 110.0)
    codes = jnp.clip(jnp.round(value * (jnp.exp2(-power) * CODE)), -CODE, CODE)
    return codes.astype(jnp.int32), power.astype(jnp.int32)


POWERS = 32


def split_first(stage, row, n, x, y, keep_a, keep_b, send_a, send_b, pow_a, pow_b):
    rows, w = keep_a.shape[1] * 2, keep_a.shape[2]
    half, quarter = rows // 2, rows // 4

    def block(at, size, lanes):
        return stage[pl.ds(pl.multiple_of(row + at, quarter), size), lanes]

    left, right = pl.ds(0, w), pl.ds(w, w)
    keep_a[n] = block(x * half, half, left)
    keep_b[n] = jnp.concatenate([block(xx * half + y * quarter, quarter, right) for xx in range(2)], 0)
    gone = block((1 - x) * half, half, left)
    codes, power = coded(gone)
    at = pl.ds(pl.multiple_of(n * half, half), half)
    send_a[at, :] = codes.astype(jnp.int16)
    pow_a[pl.ds(n, 1), :] = power
    gone = jnp.concatenate(
        [block(xx * half + (1 - y) * quarter, quarter, right) for xx in range(2)], 0
    )
    codes, power = coded(gone)
    send_b[at, :] = codes.astype(jnp.int16)
    pow_b[pl.ds(n, 1), :] = power


def close_powers(n, half, sends, pows):
    for send, power in zip(sends, pows):
        send[pl.ds(n * half, POWERS), :] = power[...].astype(jnp.int16)


def first_shapes(n, rows, cols):
    keep = jax.ShapeDtypeStruct((n, rows // 2, cols // 2), f32)
    send = jax.ShapeDtypeStruct((n * rows // 2 + POWERS, cols // 2), jnp.int16)
    return [keep, keep, send, send]


def first_scratch(cols):
    return [pltpu.VMEM((POWERS, cols // 2), jnp.int32)] * 2


def kernel_grad_kernel(
    rows, cols, chans, part, x_at, g_at, staged, ids, cur, partner, outer, far, g_own, g_far, *refs
):
    step = pl.program_id(0)
    core = ids[0]
    size = rows * cols
    if staged:
        keep_a, keep_b, send_a, send_b, taps, grads, stage, pow_a, pow_b = refs
    else:
        out, taps, grads = refs

    @pl.when(step == 0)
    def _():
        own_at = 1 + rows * core
        far_at = 1 + rows * (1 - core)
        for r in range(rows):
            at = pl.ds(x_at + r * cols, cols)
            spread_taps(taps, own_at + r, cur[at, :], cols, chans)
            spread_taps(taps, far_at + r, partner[at, :], cols, chans)
        spread_taps(taps, (2 * rows + 1) * core, outer[...], cols, chans)
        spread_taps(taps, (2 * rows + 1) * (1 - core), far[...], cols, chans)
        for h in range(grads.shape[1] // part):
            lanes = pl.ds(pl.multiple_of((2 * h + core) * part, part), part)
            own_rows = pl.ds(pl.multiple_of(core * size, 16), size)
            far_rows = pl.ds(pl.multiple_of((1 - core) * size, 16), size)
            grads[own_rows, h * part : (h + 1) * part] = g_own[pl.ds(g_at, size), lanes]
            grads[far_rows, h * part : (h + 1) * part] = g_far[pl.ds(g_at, size), lanes]
        if staged:
            pow_a[...] = jnp.zeros(pow_a.shape, jnp.int32)
            pow_b[...] = jnp.zeros(pow_b.shape, jnp.int32)

    window = taps[pl.ds(pl.multiple_of(step * cols, 16), 2 * size), :]
    value = lax.dot_general(
        grads[...], window, (((0,), (0,)), ((), ())), preferred_element_type=f32
    )
    if not staged:
        for b in range(3):
            out[b] = value[:, b * chans : (b + 1) * chans]
        return
    sides = grads.shape[1] // part
    for b in range(3):
        stage[b] = value[:, b * chans : (b + 1) * chans]
    for b in range(3):
        for h in range(sides):
            n = (3 * step + b) * sides + h
            split_first(
                stage.at[b], h * part, n, ids[1], ids[2], keep_a, keep_b, send_a, send_b, pow_a, pow_b
            )

    @pl.when(step == 2)
    def _():
        close_powers(9 * sides, part // 2, (send_a, send_b), (pow_a, pow_b))


def kernel_grad(ids, cur, partner, outer, far, g_own, g_far, part, staged):
    cols, chans = outer.shape
    rows = 2
    size = rows * cols
    outs = g_own.shape[1] // 2
    x_at, g_at = cur.shape[0] - size, g_own.shape[0] - size
    scratch = [
        pltpu.VMEM(((2 * rows + 2) * cols, 3 * chans), bf16),
        pltpu.VMEM((2 * size, outs), bf16),
    ]
    if staged:
        shapes = first_shapes(9 * outs // part, part, chans)
        out_specs = [whole(shape.shape) for shape in shapes]
        scratch += [pltpu.VMEM((3, outs, chans), f32)] + first_scratch(chans)
    else:
        shapes = jax.ShapeDtypeStruct((9, outs, chans), f32)
        out_specs = pl.BlockSpec((3, outs, chans), lambda i: (i, 0, 0))
    return pl.pallas_call(
        lambda *refs: kernel_grad_kernel(rows, cols, chans, part, x_at, g_at, staged, *refs),
        grid=(3,),
        in_specs=[
            pl.BlockSpec(memory_space=pltpu.SMEM),
            whole(cur.shape),
            whole(cur.shape),
            whole((cols, chans)),
            pl.BlockSpec((cols, chans), lambda i: (0, 0)),
            whole(g_own.shape),
            whole(g_own.shape),
        ],
        out_specs=out_specs,
        out_shape=shapes,
        scratch_shapes=scratch,
        compiler_params=pltpu.CompilerParams(vmem_limit_bytes=(56 if g_at else 36) * MIB),
        cost_estimate=COST,
        name="kernel_grad",
    )(ids, cur, partner, outer, far, g_own, g_far)


def head_grad_kernel(staged, part, ids, mine, own, got, *refs):
    half = mine.shape[1]
    dims = (((0,), (0,)), ((), ()))
    value = lax.dot_general(mine[...], own[:, half:], dims, preferred_element_type=f32)
    value += lax.dot_general(got[:, :half], got[:, half:], dims, preferred_element_type=f32)
    if not staged:
        refs[0][...] = value
        return
    keep_a, keep_b, send_a, send_b, stage, pow_a, pow_b = refs
    stage[...] = value
    pow_a[...] = jnp.zeros(pow_a.shape, jnp.int32)
    pow_b[...] = jnp.zeros(pow_b.shape, jnp.int32)
    for n in range(half // part):
        split_first(stage, n * part, n, ids[1], ids[2], keep_a, keep_b, send_a, send_b, pow_a, pow_b)
    close_powers(half // part, part // 2, (send_a, send_b), (pow_a, pow_b))


def head_grad_call(ids, mine, own, got, part, staged):
    vmem = pl.BlockSpec(memory_space=pltpu.VMEM)
    half = mine.shape[1]
    chans = own.shape[1] - half
    shapes = [jax.ShapeDtypeStruct((half, chans), f32)]
    scratch = []
    if staged:
        shapes = first_shapes(half // part, part, chans)
        scratch = [pltpu.VMEM((half, chans), f32)] + first_scratch(chans)
    return pl.pallas_call(
        lambda *refs: head_grad_kernel(staged, part, *refs),
        in_specs=[pl.BlockSpec(memory_space=pltpu.SMEM)] + [vmem] * 3,
        out_specs=[vmem for _ in shapes],
        out_shape=shapes,
        scratch_shapes=scratch,
        compiler_params=pltpu.CompilerParams(vmem_limit_bytes=16 * MIB),
        cost_estimate=COST,
        name="head_grad",
    )(ids, mine, own, got)


def scales_of(rows):
    return jnp.exp2(rows.astype(jnp.int32).astype(f32)) * (1.0 / CODE)


def second_kernel(ids, keep_a, keep_b, got_a, got_b, keep, send_a, send_b, step_a, step_b, pow_a, pow_b):
    count, rows, w = keep_a.shape
    half = rows // 2
    step_a[...] = scales_of(got_a[pl.ds(count * rows, POWERS), :])
    step_b[...] = scales_of(got_b[pl.ds(count * rows, POWERS), :])
    pow_a[...] = jnp.zeros(pow_a.shape, jnp.int32)
    pow_b[...] = jnp.zeros(pow_b.shape, jnp.int32)
    sides = (
        (keep_a, got_a, step_a, send_a, pow_a, ids[2], 0),
        (keep_b, got_b, step_b, send_b, pow_b, ids[1], w),
    )

    def body(n, carry):
        for held, got, step, send, power, bit, lane in sides:
            stays = pl.multiple_of(bit * half, half)
            goes = pl.multiple_of((1 - bit) * half, half)
            base = pl.multiple_of(n * rows, rows)

            def total(at):
                arrived = got[pl.ds(base + at, half), :].astype(jnp.int32).astype(f32)
                return held[n, pl.ds(at, half), :] + arrived * step[pl.ds(n, 1), :]

            keep[n, :, pl.ds(lane, w)] = total(stays)
            codes, top = coded(total(goes))
            send[pl.ds(pl.multiple_of(n * half, half), half), :] = codes.astype(jnp.int16)
            power[pl.ds(n, 1), :] = top
        return carry

    lax.fori_loop(0, count, body, 0)
    close_powers(count, half, (send_a, send_b), (pow_a, pow_b))


def second_call(ids, keep_a, keep_b, got_a, got_b):
    vmem = pl.BlockSpec(memory_space=pltpu.VMEM)
    count, rows, w = keep_a.shape
    send = jax.ShapeDtypeStruct((count * rows // 2 + POWERS, w), jnp.int16)
    return pl.pallas_call(
        second_kernel,
        in_specs=[pl.BlockSpec(memory_space=pltpu.SMEM)] + [vmem] * 4,
        out_specs=[vmem] * 3,
        out_shape=[jax.ShapeDtypeStruct((count, rows // 2, 2 * w), f32), send, send],
        scratch_shapes=[pltpu.VMEM((POWERS, w), f32)] * 2 + first_scratch(2 * w),
        compiler_params=pltpu.CompilerParams(vmem_limit_bytes=16 * MIB),
        cost_estimate=LONG,
        name="sum_second",
    )(ids, keep_a, keep_b, got_a, got_b)


def third_kernel(counts, scales, *refs):
    pieces = len(counts)
    out, codes, step_a, step_b = refs[3 * pieces :]
    total = sum(counts)
    rows = refs[0].shape[1]
    w = refs[0].shape[2] // 2
    fine = rows // scales
    codes[:, pl.ds(total * fine, POWERS), :] = jnp.zeros((scales, POWERS, 2 * w), jnp.int32)
    base = 0
    for piece, count in enumerate(counts):
        keep, got_a, got_b = refs[3 * piece : 3 * piece + 3]
        step_a[...] = scales_of(got_a[pl.ds(count * rows, POWERS), :])
        step_b[...] = scales_of(got_b[pl.ds(count * rows, POWERS), :])

        def body(n, carry, keep=keep, got_a=got_a, got_b=got_b, base=base):
            at = pl.ds(pl.multiple_of(n * rows, rows), rows)
            arrived = jnp.concatenate(
                [
                    got[at, :].astype(jnp.int32).astype(f32) * step[pl.ds(n, 1), :]
                    for got, step in ((got_a, step_a), (got_b, step_b))
                ],
                1,
            )
            value = keep[n] + arrived
            for s in range(scales):
                code, power = coded(value[s * fine : (s + 1) * fine])
                codes[s, pl.ds(pl.multiple_of((base + n) * fine, fine), fine), :] = code
                codes[s, pl.ds(total * fine + base + n, 1), :] = power
            return carry

        lax.fori_loop(0, count, body, 0)
        base += count
    for s in range(scales):
        out[s] = codes[s].astype(jnp.int16)


def third_call(pieces, scales):
    vmem = pl.BlockSpec(memory_space=pltpu.VMEM)
    counts = [piece[0].shape[0] for piece in pieces]
    rows, cols = pieces[0][0].shape[1:]
    total = sum(counts) * rows // scales + POWERS
    total += -total % 16
    return pl.pallas_call(
        lambda *refs: third_kernel(counts, scales, *refs),
        in_specs=[vmem] * (3 * len(pieces)),
        out_specs=vmem,
        out_shape=jax.ShapeDtypeStruct((scales, total, cols), jnp.int16),
        scratch_shapes=[pltpu.VMEM((scales, total, cols), jnp.int32)]
        + [pltpu.VMEM((POWERS, cols // 2), f32)] * 2,
        compiler_params=pltpu.CompilerParams(vmem_limit_bytes=16 * MIB),
        cost_estimate=COST,
        name="sum_third",
    )(*[ref for piece in pieces for ref in piece])


def route_kernel(devices, here, spans, block_of, *refs):
    inputs = refs[: len(spans)]
    out, blocks = refs[len(spans) : len(spans) + 2]
    values = refs[len(spans) + 2 :]
    lanes = 128
    fine, chans = blocks.shape[1:]
    groups = chans // lanes
    unit = groups * fine
    squares = jnp.zeros((fine, chans), f32)
    for got, value, runs in zip(inputs, values, spans):
        scales = got.shape[0]
        pieces = sum(run[2] for run in runs)
        for s in range(scales):
            value[s] = got[s].astype(jnp.int32).astype(f32)
        for piece, block, count in runs:

            def body(i, carry, value=value, piece=piece, block=block, pieces=pieces):
                n = piece + i
                total = jnp.zeros((fine, chans), f32)
                for s in range(value.shape[0]):
                    step = jnp.exp2(value[s, pl.ds(pieces * fine + n, 1), :]) * (1.0 / CODE)
                    total += value[s, pl.ds(pl.multiple_of(n * fine, fine), fine), :] * step
                blocks[block + i] = total
                return carry + total * total

            squares = lax.fori_loop(0, count, body, squares)
    squares = jnp.maximum(jnp.sum(jnp.sum(squares, 0, keepdims=True), 1, keepdims=True), 1e-37)
    sq_pow = jnp.floor(jnp.log2(squares))
    mant = squares * jnp.exp2(-sq_pow) * 8192.0
    mant_high = jnp.floor(mant)
    mant_low = jnp.floor((mant - mant_high) * 16384.0)
    row = lax.broadcasted_iota(jnp.int32, (16, lanes), 0)
    lane = lax.broadcasted_iota(jnp.int32, (16, lanes), 1)
    base = jnp.where(lane == 0, sq_pow, jnp.where(lane == 1, mant_high, mant_low)).astype(jnp.int32)
    base = jnp.where(row == here, base, 0)

    def send(d, carry):
        tail = base
        for k in range(here):
            b = block_of[here * d + k]
            value = blocks[jnp.maximum(b, 0)] * (b >= 0).astype(f32)
            value = jnp.concatenate(
                [value[:, g * lanes : (g + 1) * lanes] for g in range(groups)], 0
            )
            codes, power = coded(value)
            out[d, pl.ds(k * unit, unit), :] = codes.astype(jnp.int16)
            tail = jnp.where(row == k, power, tail)
        out[d, pl.ds(here * unit, 16), :] = tail.astype(jnp.int16)
        return carry

    lax.fori_loop(0, devices, send, 0, unroll=4)


def route_call(inputs, spans, block_of, devices, fine):
    here = block_of.shape[0] // devices
    chans = inputs[0].shape[2]
    rows = here * fine * chans // 128 + 16
    blocks = sum(run[2] for runs in spans for run in runs)
    vmem = pl.BlockSpec(memory_space=pltpu.VMEM)
    return pl.pallas_call(
        lambda *refs: route_kernel(devices, here, spans, *refs),
        in_specs=[pl.BlockSpec(memory_space=pltpu.SMEM)] + [vmem] * len(inputs),
        out_specs=vmem,
        out_shape=jax.ShapeDtypeStruct((devices, rows, 128), jnp.int16),
        scratch_shapes=[pltpu.VMEM((blocks, fine, chans), f32)]
        + [pltpu.VMEM(value.shape, f32) for value in inputs],
        compiler_params=pltpu.CompilerParams(vmem_limit_bytes=16 * MIB),
        name="route",
    )(block_of, *inputs)


def dot_split(a, b, dims):
    dims = (dims, ((), ()))
    value = lax.dot_general(a[0], b[0], dims, preferred_element_type=f32)
    value += lax.dot_general(a[1], b[0], dims, preferred_element_type=f32)
    return value + lax.dot_general(a[0], b[1], dims, preferred_element_type=f32)


def update_kernel(
    starts, scalars, got, master, moment, second, left, right, master_new, moment_new, second_new, fresh, norm, grads, sums
):
    here, chans, half = master.shape
    lanes = 128
    groups = chans // lanes
    unit = (got.shape[1] - 16) // here
    fine = unit // groups
    for d, start in enumerate(starts):
        tail = got[d, pl.ds(here * unit, 16), :].astype(jnp.int32).astype(f32)
        sums[pl.ds(d, 1), :] = tail[here : here + 1]
        for k in range(here):
            value = got[d, pl.ds(k * unit, unit), :].astype(jnp.int32).astype(f32)
            value = value * (jnp.exp2(tail[k : k + 1]) * (1.0 / CODE))
            for g in range(groups):
                grads[k, pl.ds(start, fine), g * lanes : (g + 1) * lanes] = value[g * fine : (g + 1) * fine]
    rows = sums[...]
    lane = lax.broadcasted_iota(jnp.int32, rows.shape, 1)

    def column(index):
        return jnp.sum(jnp.where(lane == index, rows, 0.0), 1, keepdims=True)

    squares = (column(1) + column(2) * (1.0 / 16384.0)) * (1.0 / 8192.0) * jnp.exp2(column(0))
    squares = jnp.sum(squares, 0, keepdims=True) + scalars[0]
    grad_norm = jnp.sqrt(squares) / scalars[1]
    factor = clip_level / jnp.maximum(grad_norm, clip_level) / scalars[1]
    place = lax.broadcasted_iota(jnp.int32, (1, lanes), 1)
    norm[...] = jnp.where(place == 0, grad_norm, factor)
    for k in range(here):
        side = halves(left[k])
        other = halves(right[k])
        turned = dot_split(side, halves(grads[k]), ((0,), (1,)))
        turned = dot_split(halves(turned), other, ((1,), (0,))) * factor
        first = beta_one * moment[k] + (1.0 - beta_one) * turned
        spread = beta_two * second[k] + (1.0 - beta_two) * turned * turned
        moment_new[k] = first
        second_new[k] = spread
        ratio = (first / (1.0 - beta_one**STEP)) / (jnp.sqrt(spread / (1.0 - beta_two**STEP)) + adam_eps)
        back = dot_split(side, halves(ratio), ((1,), (0,)))
        back = dot_split(halves(back), other, ((1,), (1,)))
        value = master[k] - rate_matrix * (back + weight_decay * master[k])
        master_new[k] = value
        fresh[k] = value.astype(bf16)


def update_call(scalars, got, starts, master, moment, second, left, right):
    vmem = pl.BlockSpec(memory_space=pltpu.VMEM)
    here, chans, half = master.shape
    like = jax.ShapeDtypeStruct(master.shape, f32)
    return pl.pallas_call(
        lambda *refs: update_kernel(starts, *refs),
        in_specs=[pl.BlockSpec(memory_space=pltpu.SMEM)] + [vmem] * 6,
        out_specs=[vmem] * 5,
        out_shape=[
            like,
            like,
            like,
            jax.ShapeDtypeStruct(master.shape, bf16),
            jax.ShapeDtypeStruct((1, 128), f32),
        ],
        scratch_shapes=[
            pltpu.VMEM((here, half, chans), f32),
            pltpu.VMEM((len(starts), 128), f32),
        ],
        compiler_params=pltpu.CompilerParams(vmem_limit_bytes=56 * MIB),
        name="update",
    )(scalars, got, master, moment, second, left, right)


def place_kernel(depth, taps, half, arrays, array, item, *refs):
    sources = refs[:arrays]
    conv, head, sems = refs[arrays:]
    blocks = array.shape[0]
    count = 2 * depth * taps

    def save(b, source):
        if b < count:
            tap = b // 2
            target = conv.at[tap // taps, tap % taps, :, pl.ds((b % 2) * half, half)]
        else:
            target = head.at[b - count]
        return pltpu.make_async_copy(source, target, sems.at[b])

    for b in range(blocks):
        for g in range(arrays):

            @pl.when(array[b] == g)
            def _(b=b, g=g):
                save(b, sources[g].at[item[b]]).start()

    for b in range(blocks):
        save(b, sources[0].at[0]).wait()


def place_blocks(sources, array, item, depth, taps):
    blocks = array.shape[0]
    chans, half = sources[0].shape[1:]
    heads = blocks - 2 * depth * taps
    anywhere = pl.BlockSpec(memory_space=pl.ANY)
    vmem = pl.BlockSpec(memory_space=pltpu.VMEM)
    smem = pl.BlockSpec(memory_space=pltpu.SMEM)
    size = sum(source.size for source in sources) * 2
    return pl.pallas_call(
        lambda *refs: place_kernel(depth, taps, half, len(sources), *refs),
        in_specs=[smem, smem] + [vmem] * len(sources),
        out_specs=[anywhere, anywhere],
        out_shape=[
            jax.ShapeDtypeStruct((depth, taps, chans, 2 * half), bf16),
            jax.ShapeDtypeStruct((heads, chans, half), bf16),
        ],
        scratch_shapes=[pltpu.SemaphoreType.DMA((blocks,))],
        compiler_params=pltpu.CompilerParams(vmem_limit_bytes=size + 4 * MIB),
        name="place_blocks",
    )(array, item, *sources)


def spread_slots(own, lay, z, beside):
    def line(value, pairs):
        return permute(
            value, [(lay.dev(a, i), lay.dev(b, i)) for a, b in pairs for i in range(lay.imgs)]
        )

    def over_x(value):
        return permute(value, lay.swap(2))

    def over_y(value):
        return permute(value, lay.swap(4))

    inner = (z == 1) | (z == 2)
    z_one = line(own, [(0, 1), (1, 0), (2, 3), (3, 2)])
    x_own = over_x(own)
    y_own = over_y(own)
    middle_own = line(own, [(1, 2), (2, 1)])
    z_one, x_own, y_own = lax.optimization_barrier((z_one, x_own, y_own))
    x_one = over_x(z_one)
    y_one = over_y(z_one)
    middle_one = line(z_one, [(1, 2), (2, 1)])
    outer_own = line(middle_own, [(1, 0), (2, 3)])
    xy_own = over_x(y_own)
    z_two = jnp.where(inner, middle_one, outer_own)
    y_two = over_y(after(z_two, *beside))
    outer_one = line(middle_one, [(1, 0), (2, 3)])
    x_two = over_x(after(z_two, x_one))
    xy_one = over_y(after(x_one, y_one))
    z_three = jnp.where(inner, middle_own, outer_one)
    x_three = over_x(after(z_three, xy_own))
    y_three = over_y(after(z_three, y_two))
    xy_two = over_x(after(y_two, x_two))
    xy_three = over_y(after(x_three, xy_one))
    bundles = [
        jnp.concatenate(v, 0)
        for v in (
            (own, z_one, x_own, y_own),
            (z_two, z_three, xy_own, x_one, y_one),
            (x_two, y_two, xy_one, x_three, y_three),
            (xy_two, xy_three),
        )
    ]
    return bundles + [permute(v, lay.swap(1)) for v in bundles]


PLACES = (0, 1, 8, 9, 3, 12, 17, 20, 2, 11, 16, 19, 10, 18, 24, 25)


def pick(value, index, axis):
    return lax.dynamic_index_in_dim(value, index, axis, keepdims=False)


class Sum:
    def __init__(self, made, ids, lay):
        self.keep, self.send = made[:2], made[2:]
        self.ids, self.lay = ids, lay

    def first(self):
        self.got = [permute(self.send[0], self.lay.swap(2)), permute(self.send[1], self.lay.swap(4))]

    def second(self, *wait):
        got = lax.optimization_barrier((*self.got, *wait))
        self.keep, *self.send = second_call(self.ids, *self.keep, *got[:2])
        self.got = [permute(self.send[0], self.lay.swap(4)), permute(self.send[1], self.lay.swap(2))]

    def third(self, *wait):
        got = lax.optimization_barrier((*self.got, *wait))
        return [self.keep, *got[:2]]


def soap_update(master, moment, second, left, right, grads):
    turned = jnp.einsum("sij,ski->sjk", left, grads, precision=highest)
    turned = jnp.einsum("sjk,skl->sjl", turned, right, precision=highest)
    moment = beta_one * moment + (1.0 - beta_one) * turned
    second = beta_two * second + (1.0 - beta_two) * turned * turned
    ratio = moment / (1.0 - beta_one**STEP) / (jnp.sqrt(second / (1.0 - beta_two**STEP)) + adam_eps)
    back = jnp.einsum("sij,sjk->sik", left, ratio, precision=highest)
    back = jnp.einsum("sik,slk->sil", back, right, precision=highest)
    return (master - rate_matrix * (back + weight_decay * master), moment, second)


def vector_update(params, moment, second, grads):
    moment = beta_one * moment + (1.0 - beta_one) * grads
    second = beta_two * second + (1.0 - beta_two) * grads * grads
    ratio = moment / (1.0 - beta_one**STEP) / (jnp.sqrt(second / (1.0 - beta_two**STEP)) + adam_eps)
    return (params - rate_vector * (ratio + weight_decay * params), moment, second)


def butterfly(value, lay):
    bit = 1
    while bit < lay.imgs:
        value = value + permute(value, lay.swap(bit))
        bit *= 2
    bit = 1
    while bit < lay.scales:
        value = value + permute(value, lay.scale_swap(bit))
        bit *= 2
    return value


def local(
    images,
    valid_mask,
    scale_cols,
    boxes,
    normal_targets,
    dense_targets,
    affine_scale,
    affine_shift,
    conv_bf16,
    head_bf16,
    vectors,
    vec_m,
    vec_v,
    master,
    slot_m,
    slot_v,
    basis_left,
    basis_right,
    owner_slot,
):
    held, width, chans = (images.shape[1], images.shape[2], images.shape[3])
    heads_count, head_width = (head_bf16.shape[0], head_bf16.shape[2])
    wide = heads_count * head_width
    depth, taps = (conv_bf16.shape[0], conv_bf16.shape[1])
    scales, imgs = lax.axis_size("scale"), lax.axis_size("img")
    lay = Layout(scales, imgs)
    rows = held // scales
    z = lax.axis_index("scale")
    img = lax.axis_index("img")
    group, core = img // 2, img % 2
    place = jnp.where(group % 2 == 0, z, scales - 1 - z)
    mine = 2 * (place % 2) + core

    widths = [width >> s for s in range(scales)]
    starts = []
    at = 0
    for w in widths:
        starts.append(at)
        at += w + GAP
    cols = at
    col_iota = jnp.arange(cols, dtype=jnp.int32)
    valid_col = jnp.zeros((cols,), jnp.bool_)
    for s in range(scales):
        valid_col |= (col_iota >= starts[s]) & (col_iota < starts[s] + scale_cols[s])
    col_mask = valid_col.astype(f32)[None, :, None]

    own = images[0]
    fine = [
        permute(own[rows * k : rows * (k + 1)], lay.rows_round(k, [0])) for k in range(scales)
    ]
    coarse = []
    for k in range(scales):
        piece = (k + z) % scales
        send = lax.dynamic_slice_in_dim(own[:, : widths[1]], piece * rows, rows, 0)
        coarse.append(permute(send, lay.rows_round(k, range(1, scales))))
    target_rows = after(dense_targets, fine[-1]).reshape(held // (2 * rows), 2, rows, width, dense_targets.shape[2])
    kept_rows = pick(target_rows, core, 1)
    traded = permute(pick(target_rows, 1 - core, 1), lay.swap(1))
    lower = jnp.where(core == 0, kept_rows, traded)
    upper = jnp.where(core == 0, traded, kept_rows)
    ordered = jnp.concatenate([lower, upper], 0)
    ordered = jnp.where(group % 2 == 0, ordered, ordered[::-1])

    parts = [(fine[0] + fine[1]) + (fine[2] + fine[3])]
    for s in range(1, scales):
        got = 0.0
        for k in range(scales):
            got = got + jnp.where((mine - k) % scales == s, coarse[k][:, : widths[s]], 0)
        parts.append(got.astype(bf16))
    spread = []
    for s in range(scales):
        spread.append(parts[s])
        spread.append(jnp.zeros((rows, GAP, chans), bf16))
    x_zero = (jnp.concatenate(spread, 1) * col_mask.astype(bf16)).reshape(rows * cols, chans)

    valid_mask, boxes, normal_targets, scale_cols, *_ = lax.optimization_barrier(
        (valid_mask, boxes, normal_targets, scale_cols, *fine, *coarse)
    )

    mask_all = valid_mask.astype(f32)
    pixels = jnp.arange(held * width, dtype=jnp.int32)
    hits = jnp.sum((boxes[:, None] == pixels[None, :]).astype(f32), 0).reshape(held, width)
    packed = jnp.concatenate(
        [mask_all[None], (mask_all + box_weight * hits)[None], normal_targets], 0
    )
    packed_other = permute(packed, lay.swap(1))
    from_own = place // (scales // 2) == core
    packed = jnp.where(from_own, packed, packed_other)
    packed = lax.dynamic_slice_in_dim(packed, mine * rows, rows, 1).reshape(5, rows * width)
    valid, weight = packed[0][:, None], packed[1][:, None]
    normals = jnp.pad(packed[2:].T, ((0, 0), (0, 128 - 3)))
    tables = table_call(scale_cols, starts, widths, width, cols)
    gamma = vectors[:chans]
    bias = vectors[chans:]
    core_here = core.reshape(1)
    flat_mask = jnp.broadcast_to(col_mask, (rows, cols, 1)).reshape(rows * cols, 1)

    all_taps = conv_bf16.reshape(depth, 3, 3 * chans, chans)

    size = rows * cols

    def neighbours(value, facing):
        return permute(value, lay.swap(1)), permute(facing, lay.outward())

    def gain_of(depth_idx):
        return affine_scale[depth_idx].reshape(1, chans), affine_shift[depth_idx].reshape(1, chans)

    pre_shape = jax.ShapeDtypeStruct((size, chans), f32)
    buffer_shape = jax.ShapeDtypeStruct((size + cols, chans), bf16)
    grad_shape = jax.ShapeDtypeStruct((size, chans), bf16)
    facing_zero = lax.dynamic_slice_in_dim(x_zero, core * (rows - 1) * cols, cols, 0)
    partner_zero, outer_zero = neighbours(x_zero, facing_zero)
    arrived = lax.all_to_all(after(ordered, outer_zero), "scale", 0, 0, tiled=True)
    arrived = arrived.reshape(scales, rows * width, dense_targets.shape[2])
    pre_zero, x_one, facing_one = conv_call(
        first_conv_kernel,
        core_here,
        x_zero,
        partner_zero,
        outer_zero,
        *gain_of(0),
        flat_mask,
        [],
        all_taps,
        0,
        [pre_shape, buffer_shape, jax.ShapeDtypeStruct((cols, chans), bf16)],
        False,
        "conv_rows",
    )
    partner_one, outer_one = neighbours(x_one, facing_one)
    grad_one, facing_grad, grad_mine, grad_pack, grad_gamma, grad_bias, loss_parts = head_call(
        core_here,
        x_one,
        partner_one,
        outer_one,
        (*gain_of(1), flat_mask, gamma.reshape(1, chans), bias.reshape(1, wide)),
        (weight, valid, normals),
        head_bf16,
        arrived,
        tables,
        all_taps,
        1,
    )
    part = head_width // 2
    half = chans // 2
    staged = imgs == 8 and scales == 4
    x, y = (img // 2) % 2, img // 4
    ids = jnp.stack([core, x, y])
    grad_partner, grad_outer = neighbours(grad_one, facing_grad)
    pack_got = permute(grad_pack, lay.swap(1))
    conv_grad_one = kernel_grad(
        ids, x_one, partner_one, outer_one, grad_partner, grad_one, grad_partner, part, staged
    )
    if staged:
        early = Sum(conv_grad_one, ids, lay)
        early.first()
        pack_got = after(pack_got, *early.send)
    head_grad = head_grad_call(ids, grad_mine, grad_pack, pack_got, part, staged)
    if staged:
        middle = Sum(head_grad, ids, lay)
        middle.first()
        grad_outer = after(grad_outer, *middle.send)
    (grad_zero,) = conv_call(
        back_conv_kernel,
        core_here,
        grad_one,
        grad_partner,
        grad_outer,
        *gain_of(0),
        flat_mask,
        [pre_zero],
        all_taps,
        1,
        [grad_shape],
        True,
        "conv_back",
    )
    grad_zero_partner = permute(grad_zero, lay.swap(1))
    if staged:
        early.second(grad_zero)
        grad_zero_partner = after(grad_zero_partner, *early.send)
    conv_grad_zero = kernel_grad(
        ids,
        x_zero,
        partner_zero,
        outer_zero,
        partner_one,
        grad_zero,
        grad_zero_partner,
        part,
        staged,
    )
    if staged:
        late = Sum(conv_grad_zero, ids, lay)
        late.first()
    grad_gamma, grad_bias = grad_gamma.reshape(chans), grad_bias.reshape(wide)
    own_count = jnp.where(z == 0, jnp.sum(mask_all), 0.0).reshape(1)
    loss_parts = jnp.concatenate([loss_parts[0, :2], own_count])

    vec_rows = jnp.concatenate(
        [grad_gamma, grad_bias, loss_parts, jnp.zeros((-(chans + wide + 3) % 1024,), f32)]
    ).reshape(-1, 128)
    vec_sum = butterfly(vec_rows, lay).reshape(-1)
    totals = vec_sum[chans + wide : chans + wide + 2]
    count = vec_sum[chans + wide + 2]
    grad_vec = vec_sum[: chans + wide]
    vec_squares = jnp.sum(grad_vec * grad_vec)

    blocks_count = owner_slot.shape[0]
    slots_here = master.shape[0]
    slots = slots_here * scales * imgs
    slot_ids = jnp.arange(slots, dtype=jnp.int32)
    match = slot_ids[:, None] == owner_slot[None, :]
    block_of = jnp.sum(
        jnp.where(match, jnp.arange(blocks_count, dtype=jnp.int32)[None, :], 0), 1
    )
    owned_f = jnp.any(match, 1).astype(f32)

    if staged:
        early_line = third_call([early.third(*late.send)], scales)
        early_line = lax.all_to_all(early_line, "scale", 0, 0, tiled=True)
        middle.second(*late.send)
        late.second()
        late_line = third_call([late.third(), middle.third()], scales)
        late_line = lax.all_to_all(late_line, "scale", 0, 0, tiled=True)
        conv_pieces = 2 * taps
        payload = route_call(
            [early_line, late_line],
            [
                [(0, conv_pieces, conv_pieces)],
                [(0, 0, conv_pieces), (conv_pieces, 2 * conv_pieces, heads_count)],
            ],
            jnp.where(owned_f > 0, block_of, -1),
            scales * imgs,
            part // 4 // scales,
        )
        got = lax.all_to_all(payload, AXES, 0, 0, tiled=True)
        starts_here = [
            (i % 2) * (half // 2) + (i // 2 % 2) * (half // 4) + (i // 4) * (half // 8) + s * (half // 32)
            for s, i in lay.all_devices()
        ]
        master_new, slot_m_new, slot_v_new, fresh, norm = update_call(
            jnp.stack([vec_squares, count]),
            got,
            starts_here,
            master,
            slot_m,
            slot_v,
            basis_left,
            basis_right,
        )
        grad_norm, factor = norm[0, 0], norm[0, 1]
        vec_out = vector_update(vectors, vec_m, vec_v, grad_vec * factor)
        sources = spread_slots(fresh, lay, z, vec_out)
        owner = owner_slot // slots_here
        other_img = owner % imgs
        turn = other_img ^ img
        step = ((turn >> 1) & 1) * 8 + (turn >> 2) * 4 + ((owner // imgs) ^ z)
        place = jnp.sum(
            jnp.where(
                step[:, None] == jnp.arange(16, dtype=jnp.int32)[None, :],
                jnp.asarray(PLACES, jnp.int32)[None, :],
                0,
            ),
            1,
        )
        array = place // 8 + 4 * (turn & 1)
        item = (place % 8) * slots_here + owner_slot % slots_here
    else:
        parts = jnp.concatenate(
            [v.reshape(2 * taps, part, chans) for v in (conv_grad_zero, conv_grad_one)]
            + [head_grad[0].reshape(heads_count, part, chans)],
            0,
        )
        none = jnp.zeros_like(parts)
        blocks = jnp.concatenate(
            [jnp.where(core == 0, parts, none), jnp.where(core == 1, parts, none)], 1
        )
        by_slot = blocks[block_of] * owned_f[:, None, None]
        owned = lax.psum_scatter(by_slot, AXES, scatter_dimension=0, tiled=True)
        squares_sum = lax.psum(jnp.sum(owned * owned), AXES) + vec_squares

        grad_norm = jnp.sqrt(squares_sum) / count
        factor = clip_level / jnp.maximum(grad_norm, clip_level) / count
        master_new, slot_m_new, slot_v_new = soap_update(
            master, slot_m, slot_v, basis_left, basis_right, owned * factor
        )
        sources = [lax.all_gather(master_new.astype(bf16), AXES, axis=0, tiled=True)]
        array, item = jnp.zeros_like(owner_slot), owner_slot
        vec_out = vector_update(vectors, vec_m, vec_v, grad_vec * factor)
    vec_new, vec_m_new, vec_v_new = vec_out
    conv_copy, head_copy = place_blocks(sources, array, item, depth, taps)
    loss = jnp.stack([totals[0] / wide + totals[1], count])
    return (
        loss,
        grad_norm,
        vec_new,
        vec_m_new,
        vec_v_new,
        master_new,
        slot_m_new,
        slot_v_new,
        conv_copy,
        head_copy,
    )


def solution(mesh):
    in_specs = (
        P("scale", "img", None, None),
        P("img", None),
        P(),
        P("img"),
        P(None, "img", None),
        P("img", None, "scale"),
        P(),
        P(),
        P(),
        P(),
        P(),
        P(),
        P(),
        P(("scale", "img"), None, None),
        P(("scale", "img"), None, None),
        P(("scale", "img"), None, None),
        P(("scale", "img"), None, None),
        P(("scale", "img"), None, None),
        P(),
    )
    out_specs = (
        P(),
        P(),
        P(),
        P(),
        P(),
        P(("scale", "img"), None, None),
        P(("scale", "img"), None, None),
        P(("scale", "img"), None, None),
        P(),
        P(),
    )
    return jax.shard_map(local, mesh=mesh, in_specs=in_specs, out_specs=out_specs, check_vma=False)
```

```python
import jax
import jax.numpy as jnp
from jax import lax
from jax.experimental import pallas as pl
from jax.experimental.pallas import tpu as pltpu
from jax.sharding import PartitionSpec as P

STEP = 5

beta_one = 0.5
beta_two = 0.5
adam_eps = 1e-08
rate_matrix = 0.01
rate_vector = 0.2
weight_decay = 0.01
clip_level = 0.001
box_weight = 2.0
norm_eps = 1e-05
highest = lax.Precision.HIGHEST
bf16 = jnp.bfloat16
f32 = jnp.float32
AXES = ("scale", "img")
GAP = 16
CODE = 32767.0
CHUNK = 544
MIB = 2**20
COST = pl.CostEstimate(flops=5 * 10**9, bytes_accessed=10**6, transcendentals=0)
TINY = pl.CostEstimate(flops=1, bytes_accessed=1, transcendentals=0)
LONG = pl.CostEstimate(flops=10**11, bytes_accessed=10**6, transcendentals=0)


class Layout:
    def __init__(self, scales, imgs):
        self.scales = scales
        self.imgs = imgs

    def pos(self, group, scale):
        return scale if group % 2 == 0 else self.scales - 1 - scale

    def dev(self, scale, img):
        return scale * self.imgs + img

    def at(self, group, place, core):
        return self.dev(self.pos(group, place), 2 * group + core)

    def all_devices(self):
        return [(s, i) for s in range(self.scales) for i in range(self.imgs)]

    def swap(self, bit):
        return [(self.dev(s, i), self.dev(s, i ^ bit)) for s, i in self.all_devices()]

    def turn(self, step):
        return [
            (self.dev(s, i), self.dev((s + step) % self.scales, i)) for s, i in self.all_devices()
        ]

    def scale_swap(self, bit):
        return [(self.dev(s, i), self.dev(s ^ bit, i)) for s, i in self.all_devices()]

    def rows_round(self, shift, sources):
        pairs = []
        for s in sources:
            for i in range(self.imgs):
                group, core = i // 2, i % 2
                piece = (shift + s) % self.scales
                place = (self.scales // 2) * core + piece // 2
                pairs.append((self.dev(s, i), self.at(group, place, piece % 2)))
        return pairs

    def row_order(self):
        groups = self.imgs // 2
        return [
            self.at(j, place, c) for j in range(groups) for place in range(self.scales) for c in range(2)
        ]

    def outward(self):
        order = self.row_order()
        pairs = []
        for at in range(1, len(order) - 1, 2):
            pairs += [(order[at], order[at + 1]), (order[at + 1], order[at])]
        return pairs


def permute(value, pairs):
    return lax.ppermute(value, AXES, pairs)


def after(value, *others):
    return lax.optimization_barrier((value, *others))[0]


def table_kernel(starts, widths, width, cols_ref, up_high, up_low, down_high, down_low):
    def table(shape, coarse_axis):
        place = lax.broadcasted_iota(jnp.int32, shape, coarse_axis)
        fine = lax.broadcasted_iota(jnp.int32, shape, 1 - coarse_axis)
        total = jnp.zeros(shape, f32)
        bits = (2 * width).bit_length() - 1
        for s, (start, span) in enumerate(zip(starts, widths)):
            columns = cols_ref[s]
            numer = jnp.maximum((2 * fine + 1) * columns - width, 0)
            lower = lax.shift_right_logical(numer, bits)
            frac = (numer - lax.shift_left(lower, bits)).astype(f32) * (0.5 / width)
            upper = jnp.minimum(lower + 1, columns - 1)
            coarse = place - start
            inside = (coarse >= 0) & (coarse < span)
            part = jnp.where(coarse == lower, 1.0 - frac, 0.0) + jnp.where(coarse == upper, frac, 0.0)
            total += jnp.where(inside, part, 0.0)
        return halves(total)

    up_high[...], up_low[...] = table(up_high.shape, 1)
    down_high[...], down_low[...] = table(down_high.shape, 0)


def table_call(scale_cols, starts, widths, width, cols):
    vmem = pl.BlockSpec(memory_space=pltpu.VMEM)
    return pl.pallas_call(
        lambda *refs: table_kernel(starts, widths, width, *refs),
        in_specs=[pl.BlockSpec(memory_space=pltpu.SMEM)],
        out_specs=[vmem] * 4,
        out_shape=[jax.ShapeDtypeStruct((width, cols), bf16)] * 2
        + [jax.ShapeDtypeStruct((cols, width), bf16)] * 2,
        cost_estimate=TINY,
        name="tables",
    )(scale_cols)


def halves(value):
    high = value.astype(bf16)
    return high, (value - high.astype(f32)).astype(bf16)


def whole(shape):
    return pl.BlockSpec(shape, lambda *_: (0,) * len(shape))


def spread_taps(store, at, row, cols, chans):
    base = pl.multiple_of(at * cols, 16)
    value = row.astype(f32)
    store[pl.ds(base, cols), pl.ds(0, chans)] = pltpu.roll(value, 1, 0).astype(bf16)
    store[pl.ds(base, cols), pl.ds(chans, chans)] = row
    store[pl.ds(base, cols), pl.ds(2 * chans, chans)] = pltpu.roll(value, cols - 1, 0).astype(bf16)


def load_taps(rows, cols, chans, core, cur, partner, outer, taps):
    for r in range(rows):
        spread_taps(taps, r + 1, cur[pl.ds(r * cols, cols), :], cols, chans)
    outside = (rows + 1) * core
    spread_taps(taps, outside, outer[...], cols, chans)
    inside = pl.multiple_of((rows - 1) * core * cols, 16)
    spread_taps(taps, rows + 1 - outside, partner[pl.ds(inside, cols), :], cols, chans)


def fetch(source, layer, target, sems):
    copies = [pltpu.make_async_copy(source.at[layer, a], target.at[a], sems.at[a]) for a in range(3)]
    for copy in copies:
        copy.start()
    return copies


def conv_into(pre, taps, weights, copies, cols):
    size = pre.shape[0]
    for a in range(3):
        copies[a].wait()
        value = jnp.dot(taps[pl.ds(a * cols, size), :], weights[a], preferred_element_type=f32)
        if a == 0:
            pre[...] = value
        else:
            pre[...] += value


def gelu_slope(u):
    root = 0.7978845608028654
    bend = 0.044715
    th = jnp.tanh(root * (u + bend * u * u * u))
    return 0.5 * (1.0 + th) + 0.5 * u * (1.0 - th * th) * root * (1.0 + 3.0 * bend * u * u)


def face(buffer, facing, core, rows, cols):
    at = pl.multiple_of(cols + core * (rows - 1) * cols, 16)
    facing[...] = buffer[pl.ds(at, cols), :]


def first_conv_kernel(
    rows, cols, chans, layer, core_ref, cur, partner, outer, gain, shift, mask, w_hbm, pre, out, facing, taps, w, sems
):
    copies = fetch(w_hbm, layer, w, sems)
    load_taps(rows, cols, chans, core_ref[0], cur, partner, outer, taps)
    out[pl.ds(0, cols), :] = outer[...]
    conv_into(pre, taps, w, copies, cols)

    def body(i, carry):
        at = pl.ds(pl.multiple_of(i * CHUNK, 16), CHUNK)
        u = pre[at, :] * gain[...] + shift[...]
        to = pl.ds(pl.multiple_of(cols + i * CHUNK, 16), CHUNK)
        out[to, :] = (jax.nn.gelu(u) * mask[at, :]).astype(bf16)
        return carry

    lax.fori_loop(0, rows * cols // CHUNK, body, 0)
    face(out, facing, core_ref[0], rows, cols)


def back_conv_kernel(
    rows, cols, chans, layer, core_ref, cur, partner, outer, gain, shift, mask, pre_in, w_hbm, out, taps, w, sems, acc
):
    copies = fetch(w_hbm, layer, w, sems)
    size = rows * cols
    cur = cur.at[pl.ds(cols, size)]
    partner = partner.at[pl.ds(cols, size)]
    load_taps(rows, cols, chans, core_ref[0], cur, partner, outer, taps)
    for a in range(3):
        copies[2 - a].wait()
        value = 0.0
        for b in range(3):
            value += lax.dot_general(
                taps[pl.ds(a * cols, size), b * chans : (b + 1) * chans],
                w[2 - a, (2 - b) * chans : (3 - b) * chans, :],
                (((1,), (1,)), ((), ())),
                preferred_element_type=f32,
            )
        if a == 0:
            acc[...] = value
        else:
            acc[...] += value

    def body(i, carry):
        at = pl.ds(pl.multiple_of(i * CHUNK, 16), CHUNK)
        u = pre_in[at, :] * gain[...] + shift[...]
        out[at, :] = (acc[at, :] * mask[at, :] * gelu_slope(u) * gain[...]).astype(bf16)
        return carry

    lax.fori_loop(0, size // CHUNK, body, 0)


def conv_call(kernel, core, cur, partner, outer, gain, shift, mask, more, weights, layer, shapes, acc, name):
    cols, chans = outer.shape
    rows = 2
    size = rows * cols
    scratch = [
        pltpu.VMEM(((rows + 2) * cols, 3 * chans), bf16),
        pltpu.VMEM((3, 3 * chans, chans), bf16),
        pltpu.SemaphoreType.DMA((3,)),
    ]
    if acc:
        scratch.append(pltpu.VMEM((size, chans), f32))
    vmem = pl.BlockSpec(memory_space=pltpu.VMEM)
    return pl.pallas_call(
        lambda *refs: kernel(rows, cols, chans, layer, *refs),
        in_specs=[pl.BlockSpec(memory_space=pltpu.SMEM)]
        + [vmem] * (6 + len(more))
        + [pl.BlockSpec(memory_space=pl.ANY)],
        out_specs=[vmem for _ in shapes],
        out_shape=shapes,
        scratch_shapes=scratch,
        compiler_params=pltpu.CompilerParams(vmem_limit_bytes=(30 if acc else 30) * MIB),
        cost_estimate=COST if acc else TINY,
        name=name,
    )(core, cur, partner, outer, gain, shift, mask, *more, weights)


def head_kernel(
    rows,
    cols,
    width,
    scales,
    layer,
    core_ref,
    cur,
    partner,
    outer,
    gain,
    shift,
    mask,
    gamma,
    bias,
    weight,
    valid,
    normals,
    heads_hbm,
    target_hbm,
    up_high_hbm,
    up_low_hbm,
    down_high_hbm,
    down_low_hbm,
    w_hbm,
    out,
    facing,
    mine,
    pack,
    dgamma,
    dbias,
    sums,
    taps,
    w,
    sems,
    pre,
    y_ref,
    tapped,
    raised_high,
    raised_low,
    dj_low,
    back,
    target,
    heads,
    target_in,
    up_high,
    up_low,
    down_high,
    down_low,
    more_sems,
):
    chans = outer.shape[1]
    size = rows * cols
    core = core_ref[0]
    copies = fetch(w_hbm, layer, w, sems)
    pairs = (
        (up_high_hbm, up_high),
        (up_low_hbm, up_low),
        (target_hbm, target_in),
        (heads_hbm, heads),
        (down_high_hbm, down_high),
        (down_low_hbm, down_low),
    )
    loads = [pltpu.make_async_copy(a, b, more_sems.at[i]) for i, (a, b) in enumerate(pairs)]
    for load in loads:
        load.start()
    cur = cur.at[pl.ds(cols, size)]
    partner = partner.at[pl.ds(cols, size)]
    load_taps(rows, cols, chans, core, cur, partner, outer, taps)
    out[pl.ds(0, cols), :] = outer[...]
    conv_into(pre, taps, w, copies, cols)

    def forward(i, carry):
        at = pl.ds(0, size)
        u = pre[at, :] * gain[...] + shift[...]
        y = jax.nn.gelu(u) * mask[at, :]
        y_ref[at, :] = y
        scale = lax.rsqrt(jnp.mean(y * y, -1, keepdims=True) + norm_eps)
        tapped[at, :] = (gamma[...] * y * scale).astype(bf16)
        return carry

    forward(0, 0)
    for load in loads:
        load.wait()
    part = target_in.shape[2]
    for s in range(scales):
        target[:, s * part : (s + 1) * part] = target_in[s]

    half_wide = mine.shape[1]
    for r in range(rows):
        line = tapped[pl.ds(r * cols, cols), :]
        value = jnp.dot(up_high[...], line, preferred_element_type=f32)
        value += jnp.dot(up_low[...], line, preferred_element_type=f32)
        high = value.astype(bf16)
        raised_high[pl.ds(r * width, width), :] = high
        pack[pl.ds(r * width, width), pl.ds(half_wide, chans)] = high
        raised_low[pl.ds(r * width, width), :] = (value - high.astype(f32)).astype(bf16)

    step = heads.shape[2]
    wide = heads.shape[0] * step
    dense = jnp.zeros((1, step), f32)
    normal = jnp.zeros((1, 1), f32)
    for t in range(wide // step):
        joined = jnp.dot(raised_high[...], heads[t], preferred_element_type=f32)
        joined += jnp.dot(raised_low[...], heads[t], preferred_element_type=f32)
        joined += float(scales) * bias[:, t * step : (t + 1) * step]
        diff = joined - target[:, t * step : (t + 1) * step].astype(f32)
        pulled = weight[...] * diff
        dense += jnp.sum(pulled * diff, 0, keepdims=True)
        grad = pulled * (1.0 / wide)
        if t == 0:
            lane = lax.broadcasted_iota(jnp.int32, (joined.shape[0], 128), 1)
            n = jnp.where(lane < 3, joined[:, :128], 0.0)
            other = normals[...]
            inner = jnp.sum(n * other, -1, keepdims=True)
            own_sq = jnp.sum(n * n, -1, keepdims=True) + 1.0
            other_sq = jnp.sum(other * other, -1, keepdims=True) + 1.0
            root = lax.rsqrt(own_sq * other_sq)
            normal += jnp.sum(valid[...] * (1.0 - inner * root), 0, keepdims=True)
            turn = valid[...] * root * (inner / own_sq * n - other)
            grad = jnp.concatenate([grad[:, :128] + turn, grad[:, 128:]], 1)
        dbias[:, t * step : (t + 1) * step] = float(scales) * jnp.sum(grad, 0, keepdims=True)
        dj_low[:, t * step : (t + 1) * step] = grad.astype(bf16)
        half = step // 2
        first, second = grad[:, :half], grad[:, half:]
        mine[:, t * half : (t + 1) * half] = jnp.where(core == 0, first, second).astype(bf16)
        pack[:, t * half : (t + 1) * half] = jnp.where(core == 0, second, first).astype(bf16)
    lane = lax.broadcasted_iota(jnp.int32, (1, 128), 1)
    total = 0.5 * jnp.sum(dense, 1, keepdims=True)
    sums[...] = jnp.where(lane == 0, total, jnp.where(lane == 1, normal, 0.0))

    draised = 0.0
    for t in range(heads.shape[0]):
        draised += lax.dot_general(
            dj_low[:, t * step : (t + 1) * step],
            heads[t],
            (((1,), (1,)), ((), ())),
            preferred_element_type=f32,
        )
    for r in range(rows):
        part = draised[r * width : (r + 1) * width]
        high = part.astype(bf16)
        low = (part - high.astype(f32)).astype(bf16)
        value = jnp.dot(down_high[...], high, preferred_element_type=f32)
        value += jnp.dot(down_low[...], high, preferred_element_type=f32)
        value += jnp.dot(down_high[...], low, preferred_element_type=f32)
        back[pl.ds(r * cols, cols), :] = value

    def backward(i, carry):
        at = pl.ds(0, size)
        y = y_ref[at, :]
        dt = back[at, :]
        scale = lax.rsqrt(jnp.mean(y * y, -1, keepdims=True) + norm_eps)
        dty = dt * y
        pull = jnp.mean(gamma[...] * dty, -1, keepdims=True)
        dy = gamma[...] * dt * scale - y * (scale * scale * scale * pull)
        u = pre[at, :] * gain[...] + shift[...]
        to = pl.ds(cols, size)
        out[to, :] = (dy * mask[at, :] * gelu_slope(u) * gain[...]).astype(bf16)
        return carry + jnp.sum(dty * scale, 0, keepdims=True)

    dgamma[...] = backward(0, jnp.zeros((1, chans), f32))
    face(out, facing, core, rows, cols)


def head_call(core, cur, partner, outer, vectors, pixel, heads, target, tables, weights, layer):
    cols, chans = outer.shape
    rows = 2
    size = rows * cols
    width = tables[0].shape[0]
    wide = heads.shape[0] * heads.shape[2]
    pixels = rows * width
    scales = target.shape[0]
    vmem = pl.BlockSpec(memory_space=pltpu.VMEM)
    anywhere = pl.BlockSpec(memory_space=pl.ANY)
    shapes = [
        jax.ShapeDtypeStruct((size + cols, chans), bf16),
        jax.ShapeDtypeStruct((cols, chans), bf16),
        jax.ShapeDtypeStruct((pixels, wide // 2), bf16),
        jax.ShapeDtypeStruct((pixels, wide // 2 + chans), bf16),
        jax.ShapeDtypeStruct((1, chans), f32),
        jax.ShapeDtypeStruct((1, wide), f32),
        jax.ShapeDtypeStruct((1, 128), f32),
    ]
    return pl.pallas_call(
        lambda *refs: head_kernel(rows, cols, width, scales, layer, *refs),
        in_specs=[pl.BlockSpec(memory_space=pltpu.SMEM)] + [vmem] * 11 + [anywhere] * 7,
        out_specs=[vmem for _ in shapes],
        out_shape=shapes,
        scratch_shapes=[
            pltpu.VMEM(((rows + 2) * cols, 3 * chans), bf16),
            pltpu.VMEM((3, 3 * chans, chans), bf16),
            pltpu.SemaphoreType.DMA((3,)),
            pltpu.VMEM((size, chans), f32),
            pltpu.VMEM((size, chans), f32),
            pltpu.VMEM((size, chans), bf16),
            pltpu.VMEM((pixels, chans), bf16),
            pltpu.VMEM((pixels, chans), bf16),
            pltpu.VMEM((pixels, wide), bf16),
            pltpu.VMEM((size, chans), f32),
            pltpu.VMEM((pixels, wide), bf16),
            pltpu.VMEM(heads.shape, bf16),
            pltpu.VMEM(target.shape, bf16),
        ]
        + [pltpu.VMEM(table.shape, bf16) for table in tables]
        + [pltpu.SemaphoreType.DMA((6,))],
        compiler_params=pltpu.CompilerParams(vmem_limit_bytes=56 * MIB),
        cost_estimate=COST,
        name="head_rows",
    )(core, cur, partner, outer, *vectors, *pixel, heads, target, *tables, weights)


def coded(value):
    top = jnp.max(jnp.abs(value), 0, keepdims=True)
    power = jnp.clip(jnp.ceil(jnp.log2(top)), -100.0, 110.0)
    codes = jnp.clip(jnp.round(value * (jnp.exp2(-power) * CODE)), -CODE, CODE)
    return codes.astype(jnp.int32), power.astype(jnp.int32)


def coded_wide(value):
    top = jnp.max(jnp.abs(value), 0, keepdims=True)
    lanes = top.shape[1] // 4
    top = jnp.maximum(
        jnp.maximum(top[:, :lanes], top[:, lanes : 2 * lanes]),
        jnp.maximum(top[:, 2 * lanes : 3 * lanes], top[:, 3 * lanes :]),
    )
    power = jnp.clip(jnp.ceil(jnp.log2(top)), -100.0, 110.0)
    step = jnp.concatenate([jnp.exp2(-power) * CODE] * 4, 1)
    codes = jnp.clip(jnp.round(value * step), -CODE, CODE)
    return codes.astype(jnp.int32), power.astype(jnp.int32)


def power_place(n):
    return n // 4, slice(n % 4 * 128, n % 4 * 128 + 128)


POWERS = 32


def split_first(stage, row, n, x, y, keep_a, keep_b, send_a, send_b, pow_a, pow_b):
    rows, w = keep_a.shape[1] * 2, keep_a.shape[2]
    half, quarter = rows // 2, rows // 4

    def block(at, size, lanes):
        return stage[pl.ds(pl.multiple_of(row + at, quarter), size), lanes]

    left, right = pl.ds(0, w), pl.ds(w, w)
    keep_a[n] = block(x * half, half, left)
    keep_b[n] = jnp.concatenate([block(xx * half + y * quarter, quarter, right) for xx in range(2)], 0)
    gone = block((1 - x) * half, half, left)
    codes, power = coded(gone)
    at = pl.ds(pl.multiple_of(n * half, half), half)
    send_a[at, :] = codes.astype(jnp.int16)
    pow_a[pl.ds(n, 1), :] = power
    gone = jnp.concatenate(
        [block(xx * half + (1 - y) * quarter, quarter, right) for xx in range(2)], 0
    )
    codes, power = coded(gone)
    send_b[at, :] = codes.astype(jnp.int16)
    pow_b[pl.ds(n, 1), :] = power


def close_powers(n, half, sends, pows):
    for send, power in zip(sends, pows):
        send[pl.ds(n * half, POWERS), :] = power[...].astype(jnp.int16)


def first_shapes(n, rows, cols):
    keep = jax.ShapeDtypeStruct((n, rows // 2, cols // 2), f32)
    send = jax.ShapeDtypeStruct((n * rows // 2 + POWERS, cols // 2), jnp.int16)
    return [keep, keep, send, send]


def first_scratch(cols):
    return [pltpu.VMEM((POWERS, cols // 2), jnp.int32)] * 2


def kernel_grad_kernel(
    rows, cols, chans, part, x_at, g_at, staged, ids, cur, partner, outer, far, g_own, g_far, *refs
):
    step = pl.program_id(0)
    core = ids[0]
    size = rows * cols
    if staged:
        keep_a, keep_b, send_a, send_b, taps, grads, stage, pow_a, pow_b = refs
    else:
        out, taps, grads = refs

    @pl.when(step == 0)
    def _():
        own_at = 1 + rows * core
        far_at = 1 + rows * (1 - core)
        for r in range(rows):
            at = pl.ds(x_at + r * cols, cols)
            spread_taps(taps, own_at + r, cur[at, :], cols, chans)
            spread_taps(taps, far_at + r, partner[at, :], cols, chans)
        spread_taps(taps, (2 * rows + 1) * core, outer[...], cols, chans)
        spread_taps(taps, (2 * rows + 1) * (1 - core), far[...], cols, chans)
        for h in range(grads.shape[1] // part):
            lanes = pl.ds(pl.multiple_of((2 * h + core) * part, part), part)
            own_rows = pl.ds(pl.multiple_of(core * size, 16), size)
            far_rows = pl.ds(pl.multiple_of((1 - core) * size, 16), size)
            grads[own_rows, h * part : (h + 1) * part] = g_own[pl.ds(g_at, size), lanes]
            grads[far_rows, h * part : (h + 1) * part] = g_far[pl.ds(g_at, size), lanes]
        if staged:
            pow_a[...] = jnp.zeros(pow_a.shape, jnp.int32)
            pow_b[...] = jnp.zeros(pow_b.shape, jnp.int32)

    window = taps[pl.ds(pl.multiple_of(step * cols, 16), 2 * size), :]
    value = lax.dot_general(
        grads[...], window, (((0,), (0,)), ((), ())), preferred_element_type=f32
    )
    if not staged:
        for b in range(3):
            out[b] = value[:, b * chans : (b + 1) * chans]
        return
    sides = grads.shape[1] // part
    for b in range(3):
        stage[b] = value[:, b * chans : (b + 1) * chans]
    for b in range(3):
        for h in range(sides):
            n = (3 * step + b) * sides + h
            split_first(
                stage.at[b], h * part, n, ids[1], ids[2], keep_a, keep_b, send_a, send_b, pow_a, pow_b
            )

    @pl.when(step == 2)
    def _():
        close_powers(9 * sides, part // 2, (send_a, send_b), (pow_a, pow_b))


def kernel_grad(ids, cur, partner, outer, far, g_own, g_far, part, staged):
    cols, chans = outer.shape
    rows = 2
    size = rows * cols
    outs = g_own.shape[1] // 2
    x_at, g_at = cur.shape[0] - size, g_own.shape[0] - size
    scratch = [
        pltpu.VMEM(((2 * rows + 2) * cols, 3 * chans), bf16),
        pltpu.VMEM((2 * size, outs), bf16),
    ]
    if staged:
        shapes = first_shapes(9 * outs // part, part, chans)
        out_specs = [whole(shape.shape) for shape in shapes]
        scratch += [pltpu.VMEM((3, outs, chans), f32)] + first_scratch(chans)
    else:
        shapes = jax.ShapeDtypeStruct((9, outs, chans), f32)
        out_specs = pl.BlockSpec((3, outs, chans), lambda i: (i, 0, 0))
    return pl.pallas_call(
        lambda *refs: kernel_grad_kernel(rows, cols, chans, part, x_at, g_at, staged, *refs),
        grid=(3,),
        in_specs=[
            pl.BlockSpec(memory_space=pltpu.SMEM),
            whole(cur.shape),
            whole(cur.shape),
            whole((cols, chans)),
            pl.BlockSpec((cols, chans), lambda i: (0, 0)),
            whole(g_own.shape),
            whole(g_own.shape),
        ],
        out_specs=out_specs,
        out_shape=shapes,
        scratch_shapes=scratch,
        compiler_params=pltpu.CompilerParams(vmem_limit_bytes=(56 if g_at else 36) * MIB),
        cost_estimate=COST,
        name="kernel_grad",
    )(ids, cur, partner, outer, far, g_own, g_far)


def head_grad_kernel(staged, part, ids, mine, own, got, *refs):
    half = mine.shape[1]
    dims = (((0,), (0,)), ((), ()))
    value = lax.dot_general(mine[...], own[:, half:], dims, preferred_element_type=f32)
    value += lax.dot_general(got[:, :half], got[:, half:], dims, preferred_element_type=f32)
    if not staged:
        refs[0][...] = value
        return
    keep_a, keep_b, send_a, send_b, stage, pow_a, pow_b = refs
    stage[...] = value
    pow_a[...] = jnp.zeros(pow_a.shape, jnp.int32)
    pow_b[...] = jnp.zeros(pow_b.shape, jnp.int32)
    for n in range(half // part):
        split_first(stage, n * part, n, ids[1], ids[2], keep_a, keep_b, send_a, send_b, pow_a, pow_b)
    close_powers(half // part, part // 2, (send_a, send_b), (pow_a, pow_b))


def head_grad_call(ids, mine, own, got, part, staged):
    vmem = pl.BlockSpec(memory_space=pltpu.VMEM)
    half = mine.shape[1]
    chans = own.shape[1] - half
    shapes = [jax.ShapeDtypeStruct((half, chans), f32)]
    scratch = []
    if staged:
        shapes = first_shapes(half // part, part, chans)
        scratch = [pltpu.VMEM((half, chans), f32)] + first_scratch(chans)
    return pl.pallas_call(
        lambda *refs: head_grad_kernel(staged, part, *refs),
        in_specs=[pl.BlockSpec(memory_space=pltpu.SMEM)] + [vmem] * 3,
        out_specs=[vmem for _ in shapes],
        out_shape=shapes,
        scratch_shapes=scratch,
        compiler_params=pltpu.CompilerParams(vmem_limit_bytes=16 * MIB),
        cost_estimate=COST,
        name="head_grad",
    )(ids, mine, own, got)


def scales_of(rows):
    return jnp.exp2(rows.astype(jnp.int32).astype(f32)) * (1.0 / CODE)


def second_kernel(ids, keep_a, keep_b, got_a, got_b, keep, send_a, send_b, step_a, step_b, pow_a, pow_b):
    count, rows, w = keep_a.shape
    half = rows // 2
    step_a[...] = scales_of(got_a[pl.ds(count * rows, POWERS), :])
    step_b[...] = scales_of(got_b[pl.ds(count * rows, POWERS), :])
    pow_a[...] = jnp.zeros(pow_a.shape, jnp.int32)
    pow_b[...] = jnp.zeros(pow_b.shape, jnp.int32)
    sides = (
        (keep_a, got_a, step_a, send_a, pow_a, ids[2], 0),
        (keep_b, got_b, step_b, send_b, pow_b, ids[1], w),
    )

    def body(n, carry):
        for held, got, step, send, power, bit, lane in sides:
            stays = pl.multiple_of(bit * half, half)
            goes = pl.multiple_of((1 - bit) * half, half)
            base = pl.multiple_of(n * rows, rows)

            def total(at):
                arrived = got[pl.ds(base + at, half), :].astype(jnp.int32).astype(f32)
                return held[n, pl.ds(at, half), :] + arrived * step[pl.ds(n, 1), :]

            keep[n, :, pl.ds(lane, w)] = total(stays)
            codes, top = coded(total(goes))
            send[pl.ds(pl.multiple_of(n * half, half), half), :] = codes.astype(jnp.int16)
            power[pl.ds(n, 1), :] = top
        return carry

    lax.fori_loop(0, count, body, 0)
    close_powers(count, half, (send_a, send_b), (pow_a, pow_b))


def second_call(ids, keep_a, keep_b, got_a, got_b):
    vmem = pl.BlockSpec(memory_space=pltpu.VMEM)
    count, rows, w = keep_a.shape
    send = jax.ShapeDtypeStruct((count * rows // 2 + POWERS, w), jnp.int16)
    return pl.pallas_call(
        second_kernel,
        in_specs=[pl.BlockSpec(memory_space=pltpu.SMEM)] + [vmem] * 4,
        out_specs=[vmem] * 3,
        out_shape=[jax.ShapeDtypeStruct((count, rows // 2, 2 * w), f32), send, send],
        scratch_shapes=[pltpu.VMEM((POWERS, w), f32)] * 2 + first_scratch(2 * w),
        compiler_params=pltpu.CompilerParams(vmem_limit_bytes=16 * MIB),
        cost_estimate=LONG,
        name="sum_second",
    )(ids, keep_a, keep_b, got_a, got_b)


def third_kernel(counts, scales, *refs):
    pieces = len(counts)
    out, codes, step_a, step_b, powers = refs[3 * pieces :]
    total = sum(counts)
    rows = refs[0].shape[1]
    w = refs[0].shape[2] // 2
    fine = rows // scales
    tail = codes.shape[1] - total * fine
    codes[:, pl.ds(total * fine, tail), :] = jnp.zeros((scales, tail, 2 * w), jnp.int32)
    base = 0
    for piece, count in enumerate(counts):
        keep, got_a, got_b = refs[3 * piece : 3 * piece + 3]
        step_a[...] = scales_of(got_a[pl.ds(count * rows, POWERS), :])
        step_b[...] = scales_of(got_b[pl.ds(count * rows, POWERS), :])

        def body(n, carry, keep=keep, got_a=got_a, got_b=got_b, base=base):
            at = pl.ds(pl.multiple_of(n * rows, rows), rows)
            arrived = jnp.concatenate(
                [
                    got[at, :].astype(jnp.int32).astype(f32) * step[pl.ds(n, 1), :]
                    for got, step in ((got_a, step_a), (got_b, step_b))
                ],
                1,
            )
            value = keep[n] + arrived
            for s in range(scales):
                code, power = coded_wide(value[s * fine : (s + 1) * fine])
                codes[s, pl.ds(pl.multiple_of((base + n) * fine, fine), fine), :] = code
                powers[s, pl.ds(base + n, 1), :] = power
            return carry

        lax.fori_loop(0, count, body, 0)
        base += count
    for s in range(scales):
        for n in range(total):
            row, lanes = power_place(n)
            codes[s, total * fine + row : total * fine + row + 1, lanes] = powers[s, n : n + 1, :]
        out[s] = codes[s].astype(jnp.int16)


def third_call(pieces, scales):
    vmem = pl.BlockSpec(memory_space=pltpu.VMEM)
    counts = [piece[0].shape[0] for piece in pieces]
    rows, cols = pieces[0][0].shape[1:]
    total = sum(counts) * rows // scales + -(-sum(counts) // 4)
    total += -total % 16
    return pl.pallas_call(
        lambda *refs: third_kernel(counts, scales, *refs),
        in_specs=[vmem] * (3 * len(pieces)),
        out_specs=vmem,
        out_shape=jax.ShapeDtypeStruct((scales, total, cols), jnp.int16),
        scratch_shapes=[pltpu.VMEM((scales, total, cols), jnp.int32)]
        + [pltpu.VMEM((POWERS, cols // 2), f32)] * 2
        + [pltpu.VMEM((scales, POWERS, cols // 4), jnp.int32)],
        compiler_params=pltpu.CompilerParams(vmem_limit_bytes=(56 if len(pieces) == 1 else 16) * MIB),
        cost_estimate=COST,
        name="sum_third",
    )(*[ref for piece in pieces for ref in piece])


def route_kernel(devices, here, spans, block_of, *refs):
    inputs = refs[: len(spans)]
    out, blocks, steps = refs[len(spans) : len(spans) + 3]
    values = refs[len(spans) + 3 :]
    lanes = 128
    fine, chans = blocks.shape[1:]
    groups = chans // lanes
    unit = groups * fine
    squares = jnp.zeros((fine, chans), f32)
    for got, value, runs in zip(inputs, values, spans):
        scales = got.shape[0]
        pieces = sum(run[2] for run in runs)
        for s in range(scales):
            value[s] = got[s].astype(jnp.int32).astype(f32)
            for n in range(pieces):
                line, place = power_place(n)
                power = value[s, pieces * fine + line : pieces * fine + line + 1, place]
                steps[s, n : n + 1, :] = jnp.exp2(power) * (1.0 / CODE)
        for piece, block, count in runs:

            def body(i, carry, value=value, piece=piece, block=block, pieces=pieces):
                n = piece + i
                total = jnp.zeros((fine, chans), f32)
                for s in range(value.shape[0]):
                    step = jnp.concatenate([steps[s, pl.ds(n, 1), :]] * 4, 1)
                    total += value[s, pl.ds(pl.multiple_of(n * fine, fine), fine), :] * step
                blocks[block + i] = total
                return carry + total * total

            squares = lax.fori_loop(0, count, body, squares)
    squares = jnp.maximum(jnp.sum(jnp.sum(squares, 0, keepdims=True), 1, keepdims=True), 1e-37)
    sq_pow = jnp.floor(jnp.log2(squares))
    mant = squares * jnp.exp2(-sq_pow) * 8192.0
    mant_high = jnp.floor(mant)
    mant_low = jnp.floor((mant - mant_high) * 16384.0)
    row = lax.broadcasted_iota(jnp.int32, (16, lanes), 0)
    lane = lax.broadcasted_iota(jnp.int32, (16, lanes), 1)
    base = jnp.where(lane == 0, sq_pow, jnp.where(lane == 1, mant_high, mant_low)).astype(jnp.int32)
    base = jnp.where(row == here, base, 0)

    def send(d, carry):
        tail = base
        for k in range(here):
            b = block_of[here * d + k]
            value = blocks[jnp.maximum(b, 0)] * (b >= 0).astype(f32)
            value = jnp.concatenate(
                [value[:, g * lanes : (g + 1) * lanes] for g in range(groups)], 0
            )
            codes, power = coded(value)
            out[d, pl.ds(k * unit, unit), :] = codes.astype(jnp.int16)
            tail = jnp.where(row == k, power, tail)
        out[d, pl.ds(here * unit, 16), :] = tail.astype(jnp.int16)
        return carry

    lax.fori_loop(0, devices, send, 0, unroll=4)


def route_call(inputs, spans, block_of, devices, fine):
    here = block_of.shape[0] // devices
    chans = inputs[0].shape[2]
    rows = here * fine * chans // 128 + 16
    blocks = sum(run[2] for runs in spans for run in runs)
    vmem = pl.BlockSpec(memory_space=pltpu.VMEM)
    return pl.pallas_call(
        lambda *refs: route_kernel(devices, here, spans, *refs),
        in_specs=[pl.BlockSpec(memory_space=pltpu.SMEM)] + [vmem] * len(inputs),
        out_specs=vmem,
        out_shape=jax.ShapeDtypeStruct((devices, rows, 128), jnp.int16),
        scratch_shapes=[
            pltpu.VMEM((blocks, fine, chans), f32),
            pltpu.VMEM((inputs[0].shape[0], POWERS, chans // 4), f32),
        ]
        + [pltpu.VMEM(value.shape, f32) for value in inputs],
        compiler_params=pltpu.CompilerParams(vmem_limit_bytes=16 * MIB),
        name="route",
    )(block_of, *inputs)


def dot_split(a, b, dims):
    dims = (dims, ((), ()))
    value = lax.dot_general(a[0], b[0], dims, preferred_element_type=f32)
    value += lax.dot_general(a[1], b[0], dims, preferred_element_type=f32)
    return value + lax.dot_general(a[0], b[1], dims, preferred_element_type=f32)


def update_kernel(
    starts, scalars, got, master, moment, second, left, right, master_new, moment_new, second_new, fresh, norm, grads, sums
):
    here, chans, half = master.shape
    lanes = 128
    groups = chans // lanes
    unit = (got.shape[1] - 16) // here
    fine = unit // groups
    for d, start in enumerate(starts):
        tail = got[d, pl.ds(here * unit, 16), :].astype(jnp.int32).astype(f32)
        sums[pl.ds(d, 1), :] = tail[here : here + 1]
        for k in range(here):
            value = got[d, pl.ds(k * unit, unit), :].astype(jnp.int32).astype(f32)
            value = value * (jnp.exp2(tail[k : k + 1]) * (1.0 / CODE))
            for g in range(groups):
                grads[k, pl.ds(start, fine), g * lanes : (g + 1) * lanes] = value[g * fine : (g + 1) * fine]
    rows = sums[...]
    lane = lax.broadcasted_iota(jnp.int32, rows.shape, 1)

    def column(index):
        return jnp.sum(jnp.where(lane == index, rows, 0.0), 1, keepdims=True)

    squares = (column(1) + column(2) * (1.0 / 16384.0)) * (1.0 / 8192.0) * jnp.exp2(column(0))
    squares = jnp.sum(squares, 0, keepdims=True) + scalars[0]
    grad_norm = jnp.sqrt(squares) / scalars[1]
    factor = clip_level / jnp.maximum(grad_norm, clip_level) / scalars[1]
    place = lax.broadcasted_iota(jnp.int32, (1, lanes), 1)
    norm[...] = jnp.where(place == 0, grad_norm, factor)
    for k in range(here):
        side = halves(left[k])
        other = halves(right[k])
        turned = dot_split(side, halves(grads[k]), ((0,), (1,)))
        turned = dot_split(halves(turned), other, ((1,), (0,))) * factor
        first = beta_one * moment[k] + (1.0 - beta_one) * turned
        spread = beta_two * second[k] + (1.0 - beta_two) * turned * turned
        moment_new[k] = first
        second_new[k] = spread
        ratio = (first / (1.0 - beta_one**STEP)) / (jnp.sqrt(spread / (1.0 - beta_two**STEP)) + adam_eps)
        back = dot_split(side, halves(ratio), ((1,), (0,)))
        back = dot_split(halves(back), other, ((1,), (1,)))
        value = master[k] - rate_matrix * (back + weight_decay * master[k])
        master_new[k] = value
        fresh[k] = value.astype(bf16)


def update_call(scalars, got, starts, master, moment, second, left, right):
    vmem = pl.BlockSpec(memory_space=pltpu.VMEM)
    here, chans, half = master.shape
    like = jax.ShapeDtypeStruct(master.shape, f32)
    return pl.pallas_call(
        lambda *refs: update_kernel(starts, *refs),
        in_specs=[pl.BlockSpec(memory_space=pltpu.SMEM)] + [vmem] * 6,
        out_specs=[vmem] * 5,
        out_shape=[
            like,
            like,
            like,
            jax.ShapeDtypeStruct(master.shape, bf16),
            jax.ShapeDtypeStruct((1, 128), f32),
        ],
        scratch_shapes=[
            pltpu.VMEM((here, half, chans), f32),
            pltpu.VMEM((len(starts), 128), f32),
        ],
        compiler_params=pltpu.CompilerParams(vmem_limit_bytes=56 * MIB),
        name="update",
    )(scalars, got, master, moment, second, left, right)


def place_kernel(depth, taps, half, arrays, array, item, *refs):
    sources = refs[:arrays]
    conv, head, sems = refs[arrays:]
    blocks = array.shape[0]
    count = 2 * depth * taps

    def save(b, source):
        if b < count:
            tap = b // 2
            target = conv.at[tap // taps, tap % taps, :, pl.ds((b % 2) * half, half)]
        else:
            target = head.at[b - count]
        return pltpu.make_async_copy(source, target, sems.at[b])

    for b in range(blocks):
        for g in range(arrays):

            @pl.when(array[b] == g)
            def _(b=b, g=g):
                save(b, sources[g].at[item[b]]).start()

    for b in range(blocks):
        save(b, sources[0].at[0]).wait()


def place_blocks(sources, array, item, depth, taps):
    blocks = array.shape[0]
    chans, half = sources[0].shape[1:]
    heads = blocks - 2 * depth * taps
    anywhere = pl.BlockSpec(memory_space=pl.ANY)
    vmem = pl.BlockSpec(memory_space=pltpu.VMEM)
    smem = pl.BlockSpec(memory_space=pltpu.SMEM)
    size = sum(source.size for source in sources) * 2
    return pl.pallas_call(
        lambda *refs: place_kernel(depth, taps, half, len(sources), *refs),
        in_specs=[smem, smem] + [vmem] * len(sources),
        out_specs=[anywhere, anywhere],
        out_shape=[
            jax.ShapeDtypeStruct((depth, taps, chans, 2 * half), bf16),
            jax.ShapeDtypeStruct((heads, chans, half), bf16),
        ],
        scratch_shapes=[pltpu.SemaphoreType.DMA((blocks,))],
        compiler_params=pltpu.CompilerParams(vmem_limit_bytes=size + 4 * MIB),
        name="place_blocks",
    )(array, item, *sources)


def spread_slots(own, lay, z, beside):
    def line(value, pairs):
        return permute(
            value, [(lay.dev(a, i), lay.dev(b, i)) for a, b in pairs for i in range(lay.imgs)]
        )

    def over_x(value):
        return permute(value, lay.swap(2))

    def over_y(value):
        return permute(value, lay.swap(4))

    inner = (z == 1) | (z == 2)
    z_one = line(own, [(0, 1), (1, 0), (2, 3), (3, 2)])
    x_own = over_x(own)
    y_own = over_y(own)
    middle_own = line(own, [(1, 2), (2, 1)])
    z_one, x_own, y_own = lax.optimization_barrier((z_one, x_own, y_own))
    x_one = over_x(z_one)
    y_one = over_y(z_one)
    middle_one = line(z_one, [(1, 2), (2, 1)])
    outer_own = line(middle_own, [(1, 0), (2, 3)])
    xy_own = over_x(y_own)
    z_two = jnp.where(inner, middle_one, outer_own)
    y_two = over_y(after(z_two, *beside))
    outer_one = line(middle_one, [(1, 0), (2, 3)])
    x_two = over_x(after(z_two, x_one))
    xy_one = over_y(after(x_one, y_one))
    z_three = jnp.where(inner, middle_own, outer_one)
    x_three = over_x(after(z_three, xy_own))
    y_three = over_y(after(z_three, y_two))
    xy_two = over_x(after(y_two, x_two))
    xy_three = over_y(after(x_three, xy_one))
    bundles = [
        jnp.concatenate(v, 0)
        for v in (
            (own, z_one, x_own, y_own),
            (z_two, z_three, xy_own, x_one, y_one),
            (x_two, y_two, xy_one, x_three, y_three),
            (xy_two, xy_three),
        )
    ]
    return bundles + [permute(v, lay.swap(1)) for v in bundles]


PLACES = (0, 1, 8, 9, 3, 12, 17, 20, 2, 11, 16, 19, 10, 18, 24, 25)


def pick(value, index, axis):
    return lax.dynamic_index_in_dim(value, index, axis, keepdims=False)


class Sum:
    def __init__(self, made, ids, lay):
        self.keep, self.send = made[:2], made[2:]
        self.ids, self.lay = ids, lay

    def first(self):
        self.got = [permute(self.send[0], self.lay.swap(2)), permute(self.send[1], self.lay.swap(4))]

    def second(self, *wait):
        got = lax.optimization_barrier((*self.got, *wait))
        self.keep, *self.send = second_call(self.ids, *self.keep, *got[:2])
        self.got = [permute(self.send[0], self.lay.swap(4)), permute(self.send[1], self.lay.swap(2))]

    def third(self, *wait):
        got = lax.optimization_barrier((*self.got, *wait))
        return [self.keep, *got[:2]]


def soap_update(master, moment, second, left, right, grads):
    turned = jnp.einsum("sij,ski->sjk", left, grads, precision=highest)
    turned = jnp.einsum("sjk,skl->sjl", turned, right, precision=highest)
    moment = beta_one * moment + (1.0 - beta_one) * turned
    second = beta_two * second + (1.0 - beta_two) * turned * turned
    ratio = moment / (1.0 - beta_one**STEP) / (jnp.sqrt(second / (1.0 - beta_two**STEP)) + adam_eps)
    back = jnp.einsum("sij,sjk->sik", left, ratio, precision=highest)
    back = jnp.einsum("sik,slk->sil", back, right, precision=highest)
    return (master - rate_matrix * (back + weight_decay * master), moment, second)


def vector_update(params, moment, second, grads):
    moment = beta_one * moment + (1.0 - beta_one) * grads
    second = beta_two * second + (1.0 - beta_two) * grads * grads
    ratio = moment / (1.0 - beta_one**STEP) / (jnp.sqrt(second / (1.0 - beta_two**STEP)) + adam_eps)
    return (params - rate_vector * (ratio + weight_decay * params), moment, second)


def butterfly(value, lay):
    bit = 1
    while bit < lay.imgs:
        value = value + permute(value, lay.swap(bit))
        bit *= 2
    bit = 1
    while bit < lay.scales:
        value = value + permute(value, lay.scale_swap(bit))
        bit *= 2
    return value


def local(
    images,
    valid_mask,
    scale_cols,
    boxes,
    normal_targets,
    dense_targets,
    affine_scale,
    affine_shift,
    conv_bf16,
    head_bf16,
    vectors,
    vec_m,
    vec_v,
    master,
    slot_m,
    slot_v,
    basis_left,
    basis_right,
    owner_slot,
):
    held, width, chans = (images.shape[1], images.shape[2], images.shape[3])
    heads_count, head_width = (head_bf16.shape[0], head_bf16.shape[2])
    wide = heads_count * head_width
    depth, taps = (conv_bf16.shape[0], conv_bf16.shape[1])
    scales, imgs = lax.axis_size("scale"), lax.axis_size("img")
    lay = Layout(scales, imgs)
    rows = held // scales
    z = lax.axis_index("scale")
    img = lax.axis_index("img")
    group, core = img // 2, img % 2
    place = jnp.where(group % 2 == 0, z, scales - 1 - z)
    mine = 2 * (place % 2) + core

    widths = [width >> s for s in range(scales)]
    starts = []
    at = 0
    for w in widths:
        starts.append(at)
        at += w + GAP
    cols = at
    col_iota = jnp.arange(cols, dtype=jnp.int32)
    valid_col = jnp.zeros((cols,), jnp.bool_)
    for s in range(scales):
        valid_col |= (col_iota >= starts[s]) & (col_iota < starts[s] + scale_cols[s])
    col_mask = valid_col.astype(f32)[None, :, None]

    own = images[0]
    fine = [
        permute(own[rows * k : rows * (k + 1)], lay.rows_round(k, [0])) for k in range(scales)
    ]
    coarse = []
    for k in range(scales):
        piece = (k + z) % scales
        send = lax.dynamic_slice_in_dim(own[:, : widths[1]], piece * rows, rows, 0)
        coarse.append(permute(send, lay.rows_round(k, range(1, scales))))
    target_rows = after(dense_targets, fine[-1]).reshape(held // (2 * rows), 2, rows, width, dense_targets.shape[2])
    kept_rows = pick(target_rows, core, 1)
    traded = permute(pick(target_rows, 1 - core, 1), lay.swap(1))
    lower = jnp.where(core == 0, kept_rows, traded)
    upper = jnp.where(core == 0, traded, kept_rows)
    ordered = jnp.concatenate([lower, upper], 0)
    ordered = jnp.where(group % 2 == 0, ordered, ordered[::-1])

    parts = [(fine[0] + fine[1]) + (fine[2] + fine[3])]
    for s in range(1, scales):
        got = 0.0
        for k in range(scales):
            got = got + jnp.where((mine - k) % scales == s, coarse[k][:, : widths[s]], 0)
        parts.append(got.astype(bf16))
    spread = []
    for s in range(scales):
        spread.append(parts[s])
        spread.append(jnp.zeros((rows, GAP, chans), bf16))
    x_zero = (jnp.concatenate(spread, 1) * col_mask.astype(bf16)).reshape(rows * cols, chans)

    valid_mask, boxes, normal_targets, scale_cols, *_ = lax.optimization_barrier(
        (valid_mask, boxes, normal_targets, scale_cols, *fine, *coarse)
    )

    mask_all = valid_mask.astype(f32)
    pixels = jnp.arange(held * width, dtype=jnp.int32)
    hits = jnp.sum((boxes[:, None] == pixels[None, :]).astype(f32), 0).reshape(held, width)
    packed = jnp.concatenate(
        [mask_all[None], (mask_all + box_weight * hits)[None], normal_targets], 0
    )
    packed_other = permute(packed, lay.swap(1))
    from_own = place // (scales // 2) == core
    packed = jnp.where(from_own, packed, packed_other)
    packed = lax.dynamic_slice_in_dim(packed, mine * rows, rows, 1).reshape(5, rows * width)
    valid, weight = packed[0][:, None], packed[1][:, None]
    normals = jnp.pad(packed[2:].T, ((0, 0), (0, 128 - 3)))
    tables = table_call(scale_cols, starts, widths, width, cols)
    gamma = vectors[:chans]
    bias = vectors[chans:]
    core_here = core.reshape(1)
    flat_mask = jnp.broadcast_to(col_mask, (rows, cols, 1)).reshape(rows * cols, 1)

    all_taps = conv_bf16.reshape(depth, 3, 3 * chans, chans)

    size = rows * cols

    def neighbours(value, facing):
        return permute(value, lay.swap(1)), permute(facing, lay.outward())

    def gain_of(depth_idx):
        return affine_scale[depth_idx].reshape(1, chans), affine_shift[depth_idx].reshape(1, chans)

    pre_shape = jax.ShapeDtypeStruct((size, chans), f32)
    buffer_shape = jax.ShapeDtypeStruct((size + cols, chans), bf16)
    grad_shape = jax.ShapeDtypeStruct((size, chans), bf16)
    facing_zero = lax.dynamic_slice_in_dim(x_zero, core * (rows - 1) * cols, cols, 0)
    partner_zero, outer_zero = neighbours(x_zero, facing_zero)
    arrived = lax.all_to_all(after(ordered, outer_zero), "scale", 0, 0, tiled=True)
    arrived = arrived.reshape(scales, rows * width, dense_targets.shape[2])
    pre_zero, x_one, facing_one = conv_call(
        first_conv_kernel,
        core_here,
        x_zero,
        partner_zero,
        outer_zero,
        *gain_of(0),
        flat_mask,
        [],
        all_taps,
        0,
        [pre_shape, buffer_shape, jax.ShapeDtypeStruct((cols, chans), bf16)],
        False,
        "conv_rows",
    )
    partner_one, outer_one = neighbours(x_one, facing_one)
    grad_one, facing_grad, grad_mine, grad_pack, grad_gamma, grad_bias, loss_parts = head_call(
        core_here,
        x_one,
        partner_one,
        outer_one,
        (*gain_of(1), flat_mask, gamma.reshape(1, chans), bias.reshape(1, wide)),
        (weight, valid, normals),
        head_bf16,
        arrived,
        tables,
        all_taps,
        1,
    )
    part = head_width // 2
    half = chans // 2
    staged = imgs == 8 and scales == 4
    x, y = (img // 2) % 2, img // 4
    ids = jnp.stack([core, x, y])
    grad_partner, grad_outer = neighbours(grad_one, facing_grad)
    pack_got = permute(grad_pack, lay.swap(1))
    conv_grad_one = kernel_grad(
        ids, x_one, partner_one, outer_one, grad_partner, grad_one, grad_partner, part, staged
    )
    if staged:
        early = Sum(conv_grad_one, ids, lay)
        early.first()
        pack_got = after(pack_got, *early.send)
    head_grad = head_grad_call(ids, grad_mine, grad_pack, pack_got, part, staged)
    if staged:
        middle = Sum(head_grad, ids, lay)
        middle.first()
        grad_outer = after(grad_outer, *middle.send)
    (grad_zero,) = conv_call(
        back_conv_kernel,
        core_here,
        grad_one,
        grad_partner,
        grad_outer,
        *gain_of(0),
        flat_mask,
        [pre_zero],
        all_taps,
        1,
        [grad_shape],
        True,
        "conv_back",
    )
    grad_zero_partner = permute(grad_zero, lay.swap(1))
    if staged:
        early.second(grad_zero)
        grad_zero_partner = after(grad_zero_partner, *early.send)
    conv_grad_zero = kernel_grad(
        ids,
        x_zero,
        partner_zero,
        outer_zero,
        partner_one,
        grad_zero,
        grad_zero_partner,
        part,
        staged,
    )
    if staged:
        late = Sum(conv_grad_zero, ids, lay)
        late.first()
    grad_gamma, grad_bias = grad_gamma.reshape(chans), grad_bias.reshape(wide)
    own_count = jnp.where(z == 0, jnp.sum(mask_all), 0.0).reshape(1)
    loss_parts = jnp.concatenate([loss_parts[0, :2], own_count])

    vec_rows = jnp.concatenate(
        [grad_gamma, grad_bias, loss_parts, jnp.zeros((-(chans + wide + 3) % 1024,), f32)]
    ).reshape(-1, 128)
    vec_sum = butterfly(vec_rows, lay).reshape(-1)
    totals = vec_sum[chans + wide : chans + wide + 2]
    count = vec_sum[chans + wide + 2]
    grad_vec = vec_sum[: chans + wide]
    vec_squares = jnp.sum(grad_vec * grad_vec)

    blocks_count = owner_slot.shape[0]
    slots_here = master.shape[0]
    slots = slots_here * scales * imgs
    slot_ids = jnp.arange(slots, dtype=jnp.int32)
    match = slot_ids[:, None] == owner_slot[None, :]
    block_of = jnp.sum(
        jnp.where(match, jnp.arange(blocks_count, dtype=jnp.int32)[None, :], 0), 1
    )
    owned_f = jnp.any(match, 1).astype(f32)

    if staged:
        early_line = third_call([early.third(*late.send)], scales)
        early_line = lax.all_to_all(early_line, "scale", 0, 0, tiled=True)
        middle.second(*late.send)
        late.second(*middle.send)
        late_line = third_call([late.third(), middle.third()], scales)
        late_line = lax.all_to_all(late_line, "scale", 0, 0, tiled=True)
        conv_pieces = 2 * taps
        payload = route_call(
            [early_line, late_line],
            [
                [(0, conv_pieces, conv_pieces)],
                [(0, 0, conv_pieces), (conv_pieces, 2 * conv_pieces, heads_count)],
            ],
            jnp.where(owned_f > 0, block_of, -1),
            scales * imgs,
            part // 4 // scales,
        )
        got = lax.all_to_all(payload, AXES, 0, 0, tiled=True)
        starts_here = [
            (i % 2) * (half // 2) + (i // 2 % 2) * (half // 4) + (i // 4) * (half // 8) + s * (half // 32)
            for s, i in lay.all_devices()
        ]
        master_new, slot_m_new, slot_v_new, fresh, norm = update_call(
            jnp.stack([vec_squares, count]),
            got,
            starts_here,
            master,
            slot_m,
            slot_v,
            basis_left,
            basis_right,
        )
        grad_norm, factor = norm[0, 0], norm[0, 1]
        vec_out = vector_update(vectors, vec_m, vec_v, grad_vec * factor)
        sources = spread_slots(fresh, lay, z, vec_out)
        owner = owner_slot // slots_here
        other_img = owner % imgs
        turn = other_img ^ img
        step = ((turn >> 1) & 1) * 8 + (turn >> 2) * 4 + ((owner // imgs) ^ z)
        place = jnp.sum(
            jnp.where(
                step[:, None] == jnp.arange(16, dtype=jnp.int32)[None, :],
                jnp.asarray(PLACES, jnp.int32)[None, :],
                0,
            ),
            1,
        )
        array = place // 8 + 4 * (turn & 1)
        item = (place % 8) * slots_here + owner_slot % slots_here
    else:
        parts = jnp.concatenate(
            [v.reshape(2 * taps, part, chans) for v in (conv_grad_zero, conv_grad_one)]
            + [head_grad[0].reshape(heads_count, part, chans)],
            0,
        )
        none = jnp.zeros_like(parts)
        blocks = jnp.concatenate(
            [jnp.where(core == 0, parts, none), jnp.where(core == 1, parts, none)], 1
        )
        by_slot = blocks[block_of] * owned_f[:, None, None]
        owned = lax.psum_scatter(by_slot, AXES, scatter_dimension=0, tiled=True)
        squares_sum = lax.psum(jnp.sum(owned * owned), AXES) + vec_squares

        grad_norm = jnp.sqrt(squares_sum) / count
        factor = clip_level / jnp.maximum(grad_norm, clip_level) / count
        master_new, slot_m_new, slot_v_new = soap_update(
            master, slot_m, slot_v, basis_left, basis_right, owned * factor
        )
        sources = [lax.all_gather(master_new.astype(bf16), AXES, axis=0, tiled=True)]
        array, item = jnp.zeros_like(owner_slot), owner_slot
        vec_out = vector_update(vectors, vec_m, vec_v, grad_vec * factor)
    vec_new, vec_m_new, vec_v_new = vec_out
    conv_copy, head_copy = place_blocks(sources, array, item, depth, taps)
    loss = jnp.stack([totals[0] / wide + totals[1], count])
    return (
        loss,
        grad_norm,
        vec_new,
        vec_m_new,
        vec_v_new,
        master_new,
        slot_m_new,
        slot_v_new,
        conv_copy,
        head_copy,
    )


def solution(mesh):
    in_specs = (
        P("scale", "img", None, None),
        P("img", None),
        P(),
        P("img"),
        P(None, "img", None),
        P("img", None, "scale"),
        P(),
        P(),
        P(),
        P(),
        P(),
        P(),
        P(),
        P(("scale", "img"), None, None),
        P(("scale", "img"), None, None),
        P(("scale", "img"), None, None),
        P(("scale", "img"), None, None),
        P(("scale", "img"), None, None),
        P(),
    )
    out_specs = (
        P(),
        P(),
        P(),
        P(),
        P(),
        P(("scale", "img"), None, None),
        P(("scale", "img"), None, None),
        P(("scale", "img"), None, None),
        P(),
        P(),
    )
    return jax.shard_map(local, mesh=mesh, in_specs=in_specs, out_specs=out_specs, check_vma=False)
```

```python
import jax
import jax.numpy as jnp
from jax import lax
from jax.experimental import pallas as pl
from jax.experimental.pallas import tpu as pltpu
from jax.sharding import PartitionSpec as P

STEP = 5

beta_one = 0.5
beta_two = 0.5
adam_eps = 1e-08
rate_matrix = 0.01
rate_vector = 0.2
weight_decay = 0.01
clip_level = 0.001
box_weight = 2.0
norm_eps = 1e-05
highest = lax.Precision.HIGHEST
bf16 = jnp.bfloat16
f32 = jnp.float32
AXES = ("scale", "img")
GAP = 16
CODE = 32767.0
CHUNK = 544
MIB = 2**20
COST = pl.CostEstimate(flops=5 * 10**9, bytes_accessed=10**6, transcendentals=0)
TINY = pl.CostEstimate(flops=1, bytes_accessed=1, transcendentals=0)
LONG = pl.CostEstimate(flops=10**11, bytes_accessed=10**6, transcendentals=0)


class Layout:
    def __init__(self, scales, imgs):
        self.scales = scales
        self.imgs = imgs

    def pos(self, group, scale):
        return scale if group % 2 == 0 else self.scales - 1 - scale

    def dev(self, scale, img):
        return scale * self.imgs + img

    def at(self, group, place, core):
        return self.dev(self.pos(group, place), 2 * group + core)

    def all_devices(self):
        return [(s, i) for s in range(self.scales) for i in range(self.imgs)]

    def swap(self, bit):
        return [(self.dev(s, i), self.dev(s, i ^ bit)) for s, i in self.all_devices()]

    def turn(self, step):
        return [
            (self.dev(s, i), self.dev((s + step) % self.scales, i)) for s, i in self.all_devices()
        ]

    def scale_swap(self, bit):
        return [(self.dev(s, i), self.dev(s ^ bit, i)) for s, i in self.all_devices()]

    def rows_round(self, shift, sources):
        pairs = []
        for s in sources:
            for i in range(self.imgs):
                group, core = i // 2, i % 2
                piece = (shift + s) % self.scales
                place = (self.scales // 2) * core + piece // 2
                pairs.append((self.dev(s, i), self.at(group, place, piece % 2)))
        return pairs

    def row_order(self):
        groups = self.imgs // 2
        return [
            self.at(j, place, c) for j in range(groups) for place in range(self.scales) for c in range(2)
        ]

    def outward(self):
        order = self.row_order()
        pairs = []
        for at in range(1, len(order) - 1, 2):
            pairs += [(order[at], order[at + 1]), (order[at + 1], order[at])]
        return pairs


def permute(value, pairs):
    return lax.ppermute(value, AXES, pairs)


def after(value, *others):
    return lax.optimization_barrier((value, *others))[0]


def table_kernel(starts, widths, width, cols_ref, up_high, up_low, down_high, down_low):
    def table(shape, coarse_axis):
        place = lax.broadcasted_iota(jnp.int32, shape, coarse_axis)
        fine = lax.broadcasted_iota(jnp.int32, shape, 1 - coarse_axis)
        total = jnp.zeros(shape, f32)
        bits = (2 * width).bit_length() - 1
        for s, (start, span) in enumerate(zip(starts, widths)):
            columns = cols_ref[s]
            numer = jnp.maximum((2 * fine + 1) * columns - width, 0)
            lower = lax.shift_right_logical(numer, bits)
            frac = (numer - lax.shift_left(lower, bits)).astype(f32) * (0.5 / width)
            upper = jnp.minimum(lower + 1, columns - 1)
            coarse = place - start
            inside = (coarse >= 0) & (coarse < span)
            part = jnp.where(coarse == lower, 1.0 - frac, 0.0) + jnp.where(coarse == upper, frac, 0.0)
            total += jnp.where(inside, part, 0.0)
        return halves(total)

    up_high[...], up_low[...] = table(up_high.shape, 1)
    down_high[...], down_low[...] = table(down_high.shape, 0)


def table_call(scale_cols, starts, widths, width, cols):
    vmem = pl.BlockSpec(memory_space=pltpu.VMEM)
    return pl.pallas_call(
        lambda *refs: table_kernel(starts, widths, width, *refs),
        in_specs=[pl.BlockSpec(memory_space=pltpu.SMEM)],
        out_specs=[vmem] * 4,
        out_shape=[jax.ShapeDtypeStruct((width, cols), bf16)] * 2
        + [jax.ShapeDtypeStruct((cols, width), bf16)] * 2,
        cost_estimate=TINY,
        name="tables",
    )(scale_cols)


def halves(value):
    high = value.astype(bf16)
    return high, (value - high.astype(f32)).astype(bf16)


def whole(shape):
    return pl.BlockSpec(shape, lambda *_: (0,) * len(shape))


def spread_taps(store, at, row, cols, chans):
    base = pl.multiple_of(at * cols, 16)
    value = row.astype(f32)
    store[pl.ds(base, cols), pl.ds(0, chans)] = pltpu.roll(value, 1, 0).astype(bf16)
    store[pl.ds(base, cols), pl.ds(chans, chans)] = row
    store[pl.ds(base, cols), pl.ds(2 * chans, chans)] = pltpu.roll(value, cols - 1, 0).astype(bf16)


def load_taps(rows, cols, chans, core, cur, partner, outer, taps):
    for r in range(rows):
        spread_taps(taps, r + 1, cur[pl.ds(r * cols, cols), :], cols, chans)
    outside = (rows + 1) * core
    spread_taps(taps, outside, outer[...], cols, chans)
    inside = pl.multiple_of((rows - 1) * core * cols, 16)
    spread_taps(taps, rows + 1 - outside, partner[pl.ds(inside, cols), :], cols, chans)


def fetch(source, layer, target, sems):
    copies = [pltpu.make_async_copy(source.at[layer, a], target.at[a], sems.at[a]) for a in range(3)]
    for copy in copies:
        copy.start()
    return copies


def conv_into(pre, taps, weights, copies, cols):
    size = pre.shape[0]
    for a in range(3):
        copies[a].wait()
        value = jnp.dot(taps[pl.ds(a * cols, size), :], weights[a], preferred_element_type=f32)
        if a == 0:
            pre[...] = value
        else:
            pre[...] += value


def gelu_slope(u):
    root = 0.7978845608028654
    bend = 0.044715
    th = jnp.tanh(root * (u + bend * u * u * u))
    return 0.5 * (1.0 + th) + 0.5 * u * (1.0 - th * th) * root * (1.0 + 3.0 * bend * u * u)


def face(buffer, facing, core, rows, cols):
    at = pl.multiple_of(cols + core * (rows - 1) * cols, 16)
    facing[...] = buffer[pl.ds(at, cols), :]


def first_conv_kernel(
    rows, cols, chans, layer, core_ref, cur, partner, outer, gain, shift, mask, w_hbm, pre, out, facing, taps, w, sems
):
    copies = fetch(w_hbm, layer, w, sems)
    load_taps(rows, cols, chans, core_ref[0], cur, partner, outer, taps)
    out[pl.ds(0, cols), :] = outer[...]
    conv_into(pre, taps, w, copies, cols)

    def body(i, carry):
        at = pl.ds(pl.multiple_of(i * CHUNK, 16), CHUNK)
        u = pre[at, :] * gain[...] + shift[...]
        to = pl.ds(pl.multiple_of(cols + i * CHUNK, 16), CHUNK)
        out[to, :] = (jax.nn.gelu(u) * mask[at, :]).astype(bf16)
        return carry

    lax.fori_loop(0, rows * cols // CHUNK, body, 0)
    face(out, facing, core_ref[0], rows, cols)


def back_conv_kernel(
    rows, cols, chans, layer, core_ref, cur, partner, outer, gain, shift, mask, pre_in, w_hbm, out, taps, w, sems, acc
):
    copies = fetch(w_hbm, layer, w, sems)
    size = rows * cols
    cur = cur.at[pl.ds(cols, size)]
    partner = partner.at[pl.ds(cols, size)]
    load_taps(rows, cols, chans, core_ref[0], cur, partner, outer, taps)
    for a in range(3):
        copies[2 - a].wait()
        value = 0.0
        for b in range(3):
            value += lax.dot_general(
                taps[pl.ds(a * cols, size), b * chans : (b + 1) * chans],
                w[2 - a, (2 - b) * chans : (3 - b) * chans, :],
                (((1,), (1,)), ((), ())),
                preferred_element_type=f32,
            )
        if a == 0:
            acc[...] = value
        else:
            acc[...] += value

    def body(i, carry):
        at = pl.ds(pl.multiple_of(i * CHUNK, 16), CHUNK)
        u = pre_in[at, :] * gain[...] + shift[...]
        out[at, :] = (acc[at, :] * mask[at, :] * gelu_slope(u) * gain[...]).astype(bf16)
        return carry

    lax.fori_loop(0, size // CHUNK, body, 0)


def conv_call(kernel, core, cur, partner, outer, gain, shift, mask, more, weights, layer, shapes, acc, name):
    cols, chans = outer.shape
    rows = 2
    size = rows * cols
    scratch = [
        pltpu.VMEM(((rows + 2) * cols, 3 * chans), bf16),
        pltpu.VMEM((3, 3 * chans, chans), bf16),
        pltpu.SemaphoreType.DMA((3,)),
    ]
    if acc:
        scratch.append(pltpu.VMEM((size, chans), f32))
    vmem = pl.BlockSpec(memory_space=pltpu.VMEM)
    return pl.pallas_call(
        lambda *refs: kernel(rows, cols, chans, layer, *refs),
        in_specs=[pl.BlockSpec(memory_space=pltpu.SMEM)]
        + [vmem] * (6 + len(more))
        + [pl.BlockSpec(memory_space=pl.ANY)],
        out_specs=[vmem for _ in shapes],
        out_shape=shapes,
        scratch_shapes=scratch,
        compiler_params=pltpu.CompilerParams(vmem_limit_bytes=(30 if acc else 30) * MIB),
        cost_estimate=COST if acc else TINY,
        name=name,
    )(core, cur, partner, outer, gain, shift, mask, *more, weights)


def head_kernel(
    rows,
    cols,
    width,
    scales,
    layer,
    core_ref,
    cur,
    partner,
    outer,
    gain,
    shift,
    mask,
    gamma,
    bias,
    weight,
    valid,
    normals,
    heads_hbm,
    target_hbm,
    up_high_hbm,
    up_low_hbm,
    down_high_hbm,
    down_low_hbm,
    w_hbm,
    out,
    facing,
    mine,
    pack,
    dgamma,
    dbias,
    sums,
    taps,
    w,
    sems,
    pre,
    y_ref,
    tapped,
    raised_high,
    raised_low,
    dj_low,
    back,
    target,
    heads,
    target_in,
    up_high,
    up_low,
    down_high,
    down_low,
    more_sems,
):
    chans = outer.shape[1]
    size = rows * cols
    core = core_ref[0]
    copies = fetch(w_hbm, layer, w, sems)
    pairs = (
        (up_high_hbm, up_high),
        (up_low_hbm, up_low),
        (target_hbm, target_in),
        (heads_hbm, heads),
        (down_high_hbm, down_high),
        (down_low_hbm, down_low),
    )
    loads = [pltpu.make_async_copy(a, b, more_sems.at[i]) for i, (a, b) in enumerate(pairs)]
    for load in loads:
        load.start()
    cur = cur.at[pl.ds(cols, size)]
    partner = partner.at[pl.ds(cols, size)]
    load_taps(rows, cols, chans, core, cur, partner, outer, taps)
    out[pl.ds(0, cols), :] = outer[...]
    conv_into(pre, taps, w, copies, cols)

    def forward(i, carry):
        at = pl.ds(0, size)
        u = pre[at, :] * gain[...] + shift[...]
        y = jax.nn.gelu(u) * mask[at, :]
        y_ref[at, :] = y
        scale = lax.rsqrt(jnp.mean(y * y, -1, keepdims=True) + norm_eps)
        tapped[at, :] = (gamma[...] * y * scale).astype(bf16)
        return carry

    forward(0, 0)
    for load in loads:
        load.wait()
    part = target_in.shape[2]
    for s in range(scales):
        target[:, s * part : (s + 1) * part] = target_in[s]

    half_wide = mine.shape[1]
    for r in range(rows):
        line = tapped[pl.ds(r * cols, cols), :]
        value = jnp.dot(up_high[...], line, preferred_element_type=f32)
        value += jnp.dot(up_low[...], line, preferred_element_type=f32)
        high = value.astype(bf16)
        raised_high[pl.ds(r * width, width), :] = high
        pack[pl.ds(r * width, width), pl.ds(half_wide, chans)] = high
        raised_low[pl.ds(r * width, width), :] = (value - high.astype(f32)).astype(bf16)

    step = heads.shape[2]
    wide = heads.shape[0] * step
    dense = jnp.zeros((1, step), f32)
    normal = jnp.zeros((1, 1), f32)
    for t in range(wide // step):
        joined = jnp.dot(raised_high[...], heads[t], preferred_element_type=f32)
        joined += jnp.dot(raised_low[...], heads[t], preferred_element_type=f32)
        joined += float(scales) * bias[:, t * step : (t + 1) * step]
        diff = joined - target[:, t * step : (t + 1) * step].astype(f32)
        pulled = weight[...] * diff
        dense += jnp.sum(pulled * diff, 0, keepdims=True)
        grad = pulled * (1.0 / wide)
        if t == 0:
            lane = lax.broadcasted_iota(jnp.int32, (joined.shape[0], 128), 1)
            n = jnp.where(lane < 3, joined[:, :128], 0.0)
            other = normals[...]
            inner = jnp.sum(n * other, -1, keepdims=True)
            own_sq = jnp.sum(n * n, -1, keepdims=True) + 1.0
            other_sq = jnp.sum(other * other, -1, keepdims=True) + 1.0
            root = lax.rsqrt(own_sq * other_sq)
            normal += jnp.sum(valid[...] * (1.0 - inner * root), 0, keepdims=True)
            turn = valid[...] * root * (inner / own_sq * n - other)
            grad = jnp.concatenate([grad[:, :128] + turn, grad[:, 128:]], 1)
        dbias[:, t * step : (t + 1) * step] = float(scales) * jnp.sum(grad, 0, keepdims=True)
        dj_low[:, t * step : (t + 1) * step] = grad.astype(bf16)
        half = step // 2
        first, second = grad[:, :half], grad[:, half:]
        mine[:, t * half : (t + 1) * half] = jnp.where(core == 0, first, second).astype(bf16)
        pack[:, t * half : (t + 1) * half] = jnp.where(core == 0, second, first).astype(bf16)
    lane = lax.broadcasted_iota(jnp.int32, (1, 128), 1)
    total = 0.5 * jnp.sum(dense, 1, keepdims=True)
    sums[...] = jnp.where(lane == 0, total, jnp.where(lane == 1, normal, 0.0))

    draised = 0.0
    for t in range(heads.shape[0]):
        draised += lax.dot_general(
            dj_low[:, t * step : (t + 1) * step],
            heads[t],
            (((1,), (1,)), ((), ())),
            preferred_element_type=f32,
        )
    for r in range(rows):
        part = draised[r * width : (r + 1) * width]
        high = part.astype(bf16)
        low = (part - high.astype(f32)).astype(bf16)
        value = jnp.dot(down_high[...], high, preferred_element_type=f32)
        value += jnp.dot(down_low[...], high, preferred_element_type=f32)
        value += jnp.dot(down_high[...], low, preferred_element_type=f32)
        back[pl.ds(r * cols, cols), :] = value

    def backward(i, carry):
        at = pl.ds(0, size)
        y = y_ref[at, :]
        dt = back[at, :]
        scale = lax.rsqrt(jnp.mean(y * y, -1, keepdims=True) + norm_eps)
        dty = dt * y
        pull = jnp.mean(gamma[...] * dty, -1, keepdims=True)
        dy = gamma[...] * dt * scale - y * (scale * scale * scale * pull)
        u = pre[at, :] * gain[...] + shift[...]
        to = pl.ds(cols, size)
        out[to, :] = (dy * mask[at, :] * gelu_slope(u) * gain[...]).astype(bf16)
        return carry + jnp.sum(dty * scale, 0, keepdims=True)

    dgamma[...] = backward(0, jnp.zeros((1, chans), f32))
    face(out, facing, core, rows, cols)


def head_call(core, cur, partner, outer, vectors, pixel, heads, target, tables, weights, layer):
    cols, chans = outer.shape
    rows = 2
    size = rows * cols
    width = tables[0].shape[0]
    wide = heads.shape[0] * heads.shape[2]
    pixels = rows * width
    scales = target.shape[0]
    vmem = pl.BlockSpec(memory_space=pltpu.VMEM)
    anywhere = pl.BlockSpec(memory_space=pl.ANY)
    shapes = [
        jax.ShapeDtypeStruct((size + cols, chans), bf16),
        jax.ShapeDtypeStruct((cols, chans), bf16),
        jax.ShapeDtypeStruct((pixels, wide // 2), bf16),
        jax.ShapeDtypeStruct((pixels, wide // 2 + chans), bf16),
        jax.ShapeDtypeStruct((1, chans), f32),
        jax.ShapeDtypeStruct((1, wide), f32),
        jax.ShapeDtypeStruct((1, 128), f32),
    ]
    return pl.pallas_call(
        lambda *refs: head_kernel(rows, cols, width, scales, layer, *refs),
        in_specs=[pl.BlockSpec(memory_space=pltpu.SMEM)] + [vmem] * 11 + [anywhere] * 7,
        out_specs=[vmem for _ in shapes],
        out_shape=shapes,
        scratch_shapes=[
            pltpu.VMEM(((rows + 2) * cols, 3 * chans), bf16),
            pltpu.VMEM((3, 3 * chans, chans), bf16),
            pltpu.SemaphoreType.DMA((3,)),
            pltpu.VMEM((size, chans), f32),
            pltpu.VMEM((size, chans), f32),
            pltpu.VMEM((size, chans), bf16),
            pltpu.VMEM((pixels, chans), bf16),
            pltpu.VMEM((pixels, chans), bf16),
            pltpu.VMEM((pixels, wide), bf16),
            pltpu.VMEM((size, chans), f32),
            pltpu.VMEM((pixels, wide), bf16),
            pltpu.VMEM(heads.shape, bf16),
            pltpu.VMEM(target.shape, bf16),
        ]
        + [pltpu.VMEM(table.shape, bf16) for table in tables]
        + [pltpu.SemaphoreType.DMA((6,))],
        compiler_params=pltpu.CompilerParams(vmem_limit_bytes=56 * MIB),
        cost_estimate=COST,
        name="head_rows",
    )(core, cur, partner, outer, *vectors, *pixel, heads, target, *tables, weights)


def coded(value):
    top = jnp.max(jnp.abs(value), 0, keepdims=True)
    power = jnp.clip(jnp.ceil(jnp.log2(top)), -100.0, 110.0)
    codes = jnp.clip(jnp.round(value * (jnp.exp2(-power) * CODE)), -CODE, CODE)
    return codes.astype(jnp.int32), power.astype(jnp.int32)


def coded_wide(value):
    top = jnp.max(jnp.abs(value), 0, keepdims=True)
    lanes = top.shape[1] // 4
    top = jnp.maximum(
        jnp.maximum(top[:, :lanes], top[:, lanes : 2 * lanes]),
        jnp.maximum(top[:, 2 * lanes : 3 * lanes], top[:, 3 * lanes :]),
    )
    power = jnp.clip(jnp.ceil(jnp.log2(top)), -100.0, 110.0)
    step = jnp.concatenate([jnp.exp2(-power) * CODE] * 4, 1)
    codes = jnp.clip(jnp.round(value * step), -CODE, CODE)
    return codes.astype(jnp.int32), power.astype(jnp.int32)


def power_place(n):
    return n // 4, slice(n % 4 * 128, n % 4 * 128 + 128)


POWERS = 32


def split_first(stage, row, n, x, y, keep_a, keep_b, send_a, send_b, pow_a, pow_b):
    rows, w = keep_a.shape[1] * 2, keep_a.shape[2]
    half, quarter = rows // 2, rows // 4

    def block(at, size, lanes):
        return stage[pl.ds(pl.multiple_of(row + at, quarter), size), lanes]

    left, right = pl.ds(0, w), pl.ds(w, w)
    keep_a[n] = block(x * half, half, left)
    keep_b[n] = jnp.concatenate([block(xx * half + y * quarter, quarter, right) for xx in range(2)], 0)
    gone = block((1 - x) * half, half, left)
    codes, power = coded(gone)
    at = pl.ds(pl.multiple_of(n * half, half), half)
    send_a[at, :] = codes.astype(jnp.int16)
    pow_a[pl.ds(n, 1), :] = power
    gone = jnp.concatenate(
        [block(xx * half + (1 - y) * quarter, quarter, right) for xx in range(2)], 0
    )
    codes, power = coded(gone)
    send_b[at, :] = codes.astype(jnp.int16)
    pow_b[pl.ds(n, 1), :] = power


def close_powers(n, half, sends, pows):
    for send, power in zip(sends, pows):
        send[pl.ds(n * half, POWERS), :] = power[...].astype(jnp.int16)


def first_shapes(n, rows, cols):
    keep = jax.ShapeDtypeStruct((n, rows // 2, cols // 2), f32)
    send = jax.ShapeDtypeStruct((n * rows // 2 + POWERS, cols // 2), jnp.int16)
    return [keep, keep, send, send]


def first_scratch(cols):
    return [pltpu.VMEM((POWERS, cols // 2), jnp.int32)] * 2


def kernel_grad_kernel(
    rows, cols, chans, part, x_at, g_at, staged, ids, cur, partner, outer, far, g_own, g_far, *refs
):
    step = pl.program_id(0)
    core = ids[0]
    size = rows * cols
    if staged:
        keep_a, keep_b, send_a, send_b, taps, grads, stage, pow_a, pow_b = refs
    else:
        out, taps, grads = refs

    @pl.when(step == 0)
    def _():
        own_at = 1 + rows * core
        far_at = 1 + rows * (1 - core)
        for r in range(rows):
            at = pl.ds(x_at + r * cols, cols)
            spread_taps(taps, own_at + r, cur[at, :], cols, chans)
            spread_taps(taps, far_at + r, partner[at, :], cols, chans)
        spread_taps(taps, (2 * rows + 1) * core, outer[...], cols, chans)
        spread_taps(taps, (2 * rows + 1) * (1 - core), far[...], cols, chans)
        for h in range(grads.shape[1] // part):
            lanes = pl.ds(pl.multiple_of((2 * h + core) * part, part), part)
            own_rows = pl.ds(pl.multiple_of(core * size, 16), size)
            far_rows = pl.ds(pl.multiple_of((1 - core) * size, 16), size)
            grads[own_rows, h * part : (h + 1) * part] = g_own[pl.ds(g_at, size), lanes]
            grads[far_rows, h * part : (h + 1) * part] = g_far[pl.ds(g_at, size), lanes]
        if staged:
            pow_a[...] = jnp.zeros(pow_a.shape, jnp.int32)
            pow_b[...] = jnp.zeros(pow_b.shape, jnp.int32)

    window = taps[pl.ds(pl.multiple_of(step * cols, 16), 2 * size), :]
    value = lax.dot_general(
        grads[...], window, (((0,), (0,)), ((), ())), preferred_element_type=f32
    )
    if not staged:
        for b in range(3):
            out[b] = value[:, b * chans : (b + 1) * chans]
        return
    sides = grads.shape[1] // part
    for b in range(3):
        stage[b] = value[:, b * chans : (b + 1) * chans]
    for b in range(3):
        for h in range(sides):
            n = (3 * step + b) * sides + h
            split_first(
                stage.at[b], h * part, n, ids[1], ids[2], keep_a, keep_b, send_a, send_b, pow_a, pow_b
            )

    @pl.when(step == 2)
    def _():
        close_powers(9 * sides, part // 2, (send_a, send_b), (pow_a, pow_b))


def kernel_grad(ids, cur, partner, outer, far, g_own, g_far, part, staged):
    cols, chans = outer.shape
    rows = 2
    size = rows * cols
    outs = g_own.shape[1] // 2
    x_at, g_at = cur.shape[0] - size, g_own.shape[0] - size
    scratch = [
        pltpu.VMEM(((2 * rows + 2) * cols, 3 * chans), bf16),
        pltpu.VMEM((2 * size, outs), bf16),
    ]
    if staged:
        shapes = first_shapes(9 * outs // part, part, chans)
        out_specs = [whole(shape.shape) for shape in shapes]
        scratch += [pltpu.VMEM((3, outs, chans), f32)] + first_scratch(chans)
    else:
        shapes = jax.ShapeDtypeStruct((9, outs, chans), f32)
        out_specs = pl.BlockSpec((3, outs, chans), lambda i: (i, 0, 0))
    return pl.pallas_call(
        lambda *refs: kernel_grad_kernel(rows, cols, chans, part, x_at, g_at, staged, *refs),
        grid=(3,),
        in_specs=[
            pl.BlockSpec(memory_space=pltpu.SMEM),
            whole(cur.shape),
            whole(cur.shape),
            whole((cols, chans)),
            pl.BlockSpec((cols, chans), lambda i: (0, 0)),
            whole(g_own.shape),
            whole(g_own.shape),
        ],
        out_specs=out_specs,
        out_shape=shapes,
        scratch_shapes=scratch,
        compiler_params=pltpu.CompilerParams(vmem_limit_bytes=(56 if g_at else 36) * MIB),
        cost_estimate=COST,
        name="kernel_grad",
    )(ids, cur, partner, outer, far, g_own, g_far)


def head_grad_kernel(staged, part, ids, mine, own, got, *refs):
    half = mine.shape[1]
    dims = (((0,), (0,)), ((), ()))
    value = lax.dot_general(mine[...], own[:, half:], dims, preferred_element_type=f32)
    value += lax.dot_general(got[:, :half], got[:, half:], dims, preferred_element_type=f32)
    if not staged:
        refs[0][...] = value
        return
    keep_a, keep_b, send_a, send_b, stage, pow_a, pow_b = refs
    stage[...] = value
    pow_a[...] = jnp.zeros(pow_a.shape, jnp.int32)
    pow_b[...] = jnp.zeros(pow_b.shape, jnp.int32)
    for n in range(half // part):
        split_first(stage, n * part, n, ids[1], ids[2], keep_a, keep_b, send_a, send_b, pow_a, pow_b)
    close_powers(half // part, part // 2, (send_a, send_b), (pow_a, pow_b))


def head_grad_call(ids, mine, own, got, part, staged):
    vmem = pl.BlockSpec(memory_space=pltpu.VMEM)
    half = mine.shape[1]
    chans = own.shape[1] - half
    shapes = [jax.ShapeDtypeStruct((half, chans), f32)]
    scratch = []
    if staged:
        shapes = first_shapes(half // part, part, chans)
        scratch = [pltpu.VMEM((half, chans), f32)] + first_scratch(chans)
    return pl.pallas_call(
        lambda *refs: head_grad_kernel(staged, part, *refs),
        in_specs=[pl.BlockSpec(memory_space=pltpu.SMEM)] + [vmem] * 3,
        out_specs=[vmem for _ in shapes],
        out_shape=shapes,
        scratch_shapes=scratch,
        compiler_params=pltpu.CompilerParams(vmem_limit_bytes=16 * MIB),
        cost_estimate=COST,
        name="head_grad",
    )(ids, mine, own, got)


def scales_of(rows):
    return jnp.exp2(rows.astype(jnp.int32).astype(f32)) * (1.0 / CODE)


def second_kernel(ids, keep_a, keep_b, got_a, got_b, keep, send_a, send_b, step_a, step_b, pow_a, pow_b):
    count, rows, w = keep_a.shape
    half = rows // 2
    step_a[...] = scales_of(got_a[pl.ds(count * rows, POWERS), :])
    step_b[...] = scales_of(got_b[pl.ds(count * rows, POWERS), :])
    pow_a[...] = jnp.zeros(pow_a.shape, jnp.int32)
    pow_b[...] = jnp.zeros(pow_b.shape, jnp.int32)
    sides = (
        (keep_a, got_a, step_a, send_a, pow_a, ids[2], 0),
        (keep_b, got_b, step_b, send_b, pow_b, ids[1], w),
    )

    def body(n, carry):
        for held, got, step, send, power, bit, lane in sides:
            stays = pl.multiple_of(bit * half, half)
            goes = pl.multiple_of((1 - bit) * half, half)
            base = pl.multiple_of(n * rows, rows)

            def total(at):
                arrived = got[pl.ds(base + at, half), :].astype(jnp.int32).astype(f32)
                return held[n, pl.ds(at, half), :] + arrived * step[pl.ds(n, 1), :]

            keep[n, :, pl.ds(lane, w)] = total(stays)
            codes, top = coded(total(goes))
            send[pl.ds(pl.multiple_of(n * half, half), half), :] = codes.astype(jnp.int16)
            power[pl.ds(n, 1), :] = top
        return carry

    lax.fori_loop(0, count, body, 0)
    close_powers(count, half, (send_a, send_b), (pow_a, pow_b))


def second_call(ids, keep_a, keep_b, got_a, got_b):
    vmem = pl.BlockSpec(memory_space=pltpu.VMEM)
    count, rows, w = keep_a.shape
    send = jax.ShapeDtypeStruct((count * rows // 2 + POWERS, w), jnp.int16)
    return pl.pallas_call(
        second_kernel,
        in_specs=[pl.BlockSpec(memory_space=pltpu.SMEM)] + [vmem] * 4,
        out_specs=[vmem] * 3,
        out_shape=[jax.ShapeDtypeStruct((count, rows // 2, 2 * w), f32), send, send],
        scratch_shapes=[pltpu.VMEM((POWERS, w), f32)] * 2 + first_scratch(2 * w),
        compiler_params=pltpu.CompilerParams(vmem_limit_bytes=16 * MIB),
        cost_estimate=LONG,
        name="sum_second",
    )(ids, keep_a, keep_b, got_a, got_b)


def third_kernel(counts, scales, *refs):
    pieces = len(counts)
    out, codes, step_a, step_b, powers = refs[3 * pieces :]
    total = sum(counts)
    rows = refs[0].shape[1]
    w = refs[0].shape[2] // 2
    fine = rows // scales
    tail = codes.shape[1] - total * fine
    codes[:, pl.ds(total * fine, tail), :] = jnp.zeros((scales, tail, 2 * w), jnp.int32)
    base = 0
    for piece, count in enumerate(counts):
        keep, got_a, got_b = refs[3 * piece : 3 * piece + 3]
        step_a[...] = scales_of(got_a[pl.ds(count * rows, POWERS), :])
        step_b[...] = scales_of(got_b[pl.ds(count * rows, POWERS), :])

        def body(n, carry, keep=keep, got_a=got_a, got_b=got_b, base=base):
            at = pl.ds(pl.multiple_of(n * rows, rows), rows)
            arrived = jnp.concatenate(
                [
                    got[at, :].astype(jnp.int32).astype(f32) * step[pl.ds(n, 1), :]
                    for got, step in ((got_a, step_a), (got_b, step_b))
                ],
                1,
            )
            value = keep[n] + arrived
            for s in range(scales):
                code, power = coded_wide(value[s * fine : (s + 1) * fine])
                codes[s, pl.ds(pl.multiple_of((base + n) * fine, fine), fine), :] = code
                powers[s, pl.ds(base + n, 1), :] = power
            return carry

        lax.fori_loop(0, count, body, 0)
        base += count
    for s in range(scales):
        for n in range(total):
            row, lanes = power_place(n)
            codes[s, total * fine + row : total * fine + row + 1, lanes] = powers[s, n : n + 1, :]
        out[s] = codes[s].astype(jnp.int16)


def third_call(pieces, scales):
    vmem = pl.BlockSpec(memory_space=pltpu.VMEM)
    counts = [piece[0].shape[0] for piece in pieces]
    rows, cols = pieces[0][0].shape[1:]
    total = sum(counts) * rows // scales + -(-sum(counts) // 4)
    total += -total % 16
    return pl.pallas_call(
        lambda *refs: third_kernel(counts, scales, *refs),
        in_specs=[vmem] * (3 * len(pieces)),
        out_specs=vmem,
        out_shape=jax.ShapeDtypeStruct((scales, total, cols), jnp.int16),
        scratch_shapes=[pltpu.VMEM((scales, total, cols), jnp.int32)]
        + [pltpu.VMEM((POWERS, cols // 2), f32)] * 2
        + [pltpu.VMEM((scales, POWERS, cols // 4), jnp.int32)],
        compiler_params=pltpu.CompilerParams(vmem_limit_bytes=(56 if len(pieces) == 1 else 16) * MIB),
        cost_estimate=COST,
        name="sum_third",
    )(*[ref for piece in pieces for ref in piece])


def route_kernel(devices, here, spans, block_of, *refs):
    inputs = refs[: len(spans)]
    out, blocks, steps = refs[len(spans) : len(spans) + 3]
    values = refs[len(spans) + 3 :]
    lanes = 128
    fine, chans = blocks.shape[1:]
    groups = chans // lanes
    unit = groups * fine
    squares = jnp.zeros((fine, chans), f32)
    for got, value, runs in zip(inputs, values, spans):
        scales = got.shape[0]
        pieces = sum(run[2] for run in runs)
        for s in range(scales):
            value[s] = got[s].astype(jnp.int32).astype(f32)
            for n in range(pieces):
                line, place = power_place(n)
                power = value[s, pieces * fine + line : pieces * fine + line + 1, place]
                steps[s, n : n + 1, :] = jnp.exp2(power) * (1.0 / CODE)
        for piece, block, count in runs:

            def body(i, carry, value=value, piece=piece, block=block, pieces=pieces):
                n = piece + i
                total = jnp.zeros((fine, chans), f32)
                for s in range(value.shape[0]):
                    step = jnp.concatenate([steps[s, pl.ds(n, 1), :]] * 4, 1)
                    total += value[s, pl.ds(pl.multiple_of(n * fine, fine), fine), :] * step
                blocks[block + i] = total
                return carry + total * total

            squares = lax.fori_loop(0, count, body, squares)
    squares = jnp.maximum(jnp.sum(jnp.sum(squares, 0, keepdims=True), 1, keepdims=True), 1e-37)
    sq_pow = jnp.floor(jnp.log2(squares))
    mant = squares * jnp.exp2(-sq_pow) * 8192.0
    mant_high = jnp.floor(mant)
    mant_low = jnp.floor((mant - mant_high) * 16384.0)
    row = lax.broadcasted_iota(jnp.int32, (16, lanes), 0)
    lane = lax.broadcasted_iota(jnp.int32, (16, lanes), 1)
    base = jnp.where(lane == 0, sq_pow, jnp.where(lane == 1, mant_high, mant_low)).astype(jnp.int32)
    base = jnp.where(row == here, base, 0)

    def send(d, carry):
        tail = base
        for k in range(here):
            b = block_of[here * d + k]
            value = blocks[jnp.maximum(b, 0)] * (b >= 0).astype(f32)
            value = jnp.concatenate(
                [value[:, g * lanes : (g + 1) * lanes] for g in range(groups)], 0
            )
            codes, power = coded(value)
            out[d, pl.ds(k * unit, unit), :] = codes.astype(jnp.int16)
            tail = jnp.where(row == k, power, tail)
        out[d, pl.ds(here * unit, 16), :] = tail.astype(jnp.int16)
        return carry

    lax.fori_loop(0, devices, send, 0, unroll=4)


def route_call(inputs, spans, block_of, devices, fine):
    here = block_of.shape[0] // devices
    chans = inputs[0].shape[2]
    rows = here * fine * chans // 128 + 16
    blocks = sum(run[2] for runs in spans for run in runs)
    vmem = pl.BlockSpec(memory_space=pltpu.VMEM)
    return pl.pallas_call(
        lambda *refs: route_kernel(devices, here, spans, *refs),
        in_specs=[pl.BlockSpec(memory_space=pltpu.SMEM)] + [vmem] * len(inputs),
        out_specs=vmem,
        out_shape=jax.ShapeDtypeStruct((devices, rows, 128), jnp.int16),
        scratch_shapes=[
            pltpu.VMEM((blocks, fine, chans), f32),
            pltpu.VMEM((inputs[0].shape[0], POWERS, chans // 4), f32),
        ]
        + [pltpu.VMEM(value.shape, f32) for value in inputs],
        compiler_params=pltpu.CompilerParams(vmem_limit_bytes=16 * MIB),
        name="route",
    )(block_of, *inputs)


def dot_split(a, b, dims):
    dims = (dims, ((), ()))
    value = lax.dot_general(a[0], b[0], dims, preferred_element_type=f32)
    value += lax.dot_general(a[1], b[0], dims, preferred_element_type=f32)
    return value + lax.dot_general(a[0], b[1], dims, preferred_element_type=f32)


def update_kernel(starts, scalars, got, *refs):
    outside, refs = refs[:5], refs[5:]
    master_new, moment_new, second_new, fresh, norm, grads, sums = refs[:7]
    master, moment, second, left, right, sems = refs[7:]
    inside = (left, right, moment, second, master)
    order = (outside[3], outside[4], outside[1], outside[2], outside[0])
    loads = [pltpu.make_async_copy(a, b, sems.at[n]) for n, (a, b) in enumerate(zip(order, inside))]
    for load in loads:
        load.start()
    here, chans, half = master.shape
    lanes = 128
    groups = chans // lanes
    unit = (got.shape[1] - 16) // here
    fine = unit // groups
    for d, start in enumerate(starts):
        tail = got[d, pl.ds(here * unit, 16), :].astype(jnp.int32).astype(f32)
        sums[pl.ds(d, 1), :] = tail[here : here + 1]
        for k in range(here):
            value = got[d, pl.ds(k * unit, unit), :].astype(jnp.int32).astype(f32)
            value = value * (jnp.exp2(tail[k : k + 1]) * (1.0 / CODE))
            for g in range(groups):
                grads[k, pl.ds(start, fine), g * lanes : (g + 1) * lanes] = value[g * fine : (g + 1) * fine]
    rows = sums[...]
    lane = lax.broadcasted_iota(jnp.int32, rows.shape, 1)

    def column(index):
        return jnp.sum(jnp.where(lane == index, rows, 0.0), 1, keepdims=True)

    squares = (column(1) + column(2) * (1.0 / 16384.0)) * (1.0 / 8192.0) * jnp.exp2(column(0))
    squares = jnp.sum(squares, 0, keepdims=True) + scalars[0]
    grad_norm = jnp.sqrt(squares) / scalars[1]
    factor = clip_level / jnp.maximum(grad_norm, clip_level) / scalars[1]
    place = lax.broadcasted_iota(jnp.int32, (1, lanes), 1)
    norm[...] = jnp.where(place == 0, grad_norm, factor)
    for load in loads:
        load.wait()
    for k in range(here):
        side = halves(left[k])
        other = halves(right[k])
        turned = dot_split(side, halves(grads[k]), ((0,), (1,)))
        turned = dot_split(halves(turned), other, ((1,), (0,))) * factor
        first = beta_one * moment[k] + (1.0 - beta_one) * turned
        spread = beta_two * second[k] + (1.0 - beta_two) * turned * turned
        moment_new[k] = first
        second_new[k] = spread
        ratio = (first / (1.0 - beta_one**STEP)) / (jnp.sqrt(spread / (1.0 - beta_two**STEP)) + adam_eps)
        back = dot_split(side, halves(ratio), ((1,), (0,)))
        back = dot_split(halves(back), other, ((1,), (1,)))
        value = master[k] - rate_matrix * (back + weight_decay * master[k])
        master_new[k] = value
        fresh[k] = value.astype(bf16)


def update_call(scalars, got, starts, master, moment, second, left, right):
    vmem = pl.BlockSpec(memory_space=pltpu.VMEM)
    here, chans, half = master.shape
    like = jax.ShapeDtypeStruct(master.shape, f32)
    return pl.pallas_call(
        lambda *refs: update_kernel(starts, *refs),
        in_specs=[pl.BlockSpec(memory_space=pltpu.SMEM), vmem]
        + [pl.BlockSpec(memory_space=pl.ANY)] * 5,
        out_specs=[vmem] * 5,
        out_shape=[
            like,
            like,
            like,
            jax.ShapeDtypeStruct(master.shape, bf16),
            jax.ShapeDtypeStruct((1, 128), f32),
        ],
        scratch_shapes=[
            pltpu.VMEM((here, half, chans), f32),
            pltpu.VMEM((len(starts), 128), f32),
        ]
        + [pltpu.VMEM(ref.shape, f32) for ref in (master, moment, second, left, right)]
        + [pltpu.SemaphoreType.DMA((5,))],
        compiler_params=pltpu.CompilerParams(vmem_limit_bytes=56 * MIB),
        name="update",
    )(scalars, got, master, moment, second, left, right)


def place_kernel(depth, taps, half, arrays, array, item, *refs):
    sources = refs[:arrays]
    conv, head, sems = refs[arrays:]
    blocks = array.shape[0]
    count = 2 * depth * taps

    def save(b, source):
        if b < count:
            tap = b // 2
            target = conv.at[tap // taps, tap % taps, :, pl.ds((b % 2) * half, half)]
        else:
            target = head.at[b - count]
        return pltpu.make_async_copy(source, target, sems.at[b])

    for b in range(blocks):
        for g in range(arrays):

            @pl.when(array[b] == g)
            def _(b=b, g=g):
                save(b, sources[g].at[item[b]]).start()

    for b in range(blocks):
        save(b, sources[0].at[0]).wait()


def place_blocks(sources, array, item, depth, taps):
    blocks = array.shape[0]
    chans, half = sources[0].shape[1:]
    heads = blocks - 2 * depth * taps
    anywhere = pl.BlockSpec(memory_space=pl.ANY)
    vmem = pl.BlockSpec(memory_space=pltpu.VMEM)
    smem = pl.BlockSpec(memory_space=pltpu.SMEM)
    size = sum(source.size for source in sources) * 2
    return pl.pallas_call(
        lambda *refs: place_kernel(depth, taps, half, len(sources), *refs),
        in_specs=[smem, smem] + [vmem] * len(sources),
        out_specs=[anywhere, anywhere],
        out_shape=[
            jax.ShapeDtypeStruct((depth, taps, chans, 2 * half), bf16),
            jax.ShapeDtypeStruct((heads, chans, half), bf16),
        ],
        scratch_shapes=[pltpu.SemaphoreType.DMA((blocks,))],
        compiler_params=pltpu.CompilerParams(vmem_limit_bytes=size + 4 * MIB),
        name="place_blocks",
    )(array, item, *sources)


def spread_slots(own, lay, z, beside):
    def line(value, pairs):
        return permute(
            value, [(lay.dev(a, i), lay.dev(b, i)) for a, b in pairs for i in range(lay.imgs)]
        )

    def over_x(value):
        return permute(value, lay.swap(2))

    def over_y(value):
        return permute(value, lay.swap(4))

    inner = (z == 1) | (z == 2)
    z_one = line(own, [(0, 1), (1, 0), (2, 3), (3, 2)])
    x_own = over_x(own)
    y_own = over_y(own)
    middle_own = line(own, [(1, 2), (2, 1)])
    z_one, x_own, y_own = lax.optimization_barrier((z_one, x_own, y_own))
    x_one = over_x(z_one)
    y_one = over_y(z_one)
    middle_one = line(z_one, [(1, 2), (2, 1)])
    outer_own = line(middle_own, [(1, 0), (2, 3)])
    xy_own = over_x(y_own)
    z_two = jnp.where(inner, middle_one, outer_own)
    y_two = over_y(after(z_two, *beside))
    outer_one = line(middle_one, [(1, 0), (2, 3)])
    x_two = over_x(after(z_two, x_one))
    xy_one = over_y(after(x_one, y_one))
    z_three = jnp.where(inner, middle_own, outer_one)
    x_three = over_x(after(z_three, xy_own))
    y_three = over_y(after(z_three, y_two))
    xy_two = over_x(after(y_two, x_two))
    xy_three = over_y(after(x_three, xy_one))
    bundles = [
        jnp.concatenate(v, 0)
        for v in (
            (own, z_one, x_own, y_own),
            (z_two, z_three, xy_own, x_one, y_one),
            (x_two, y_two, xy_one, x_three, y_three),
            (xy_two, xy_three),
        )
    ]
    return bundles + [permute(v, lay.swap(1)) for v in bundles]


PLACES = (0, 1, 8, 9, 3, 12, 17, 20, 2, 11, 16, 19, 10, 18, 24, 25)


def pick(value, index, axis):
    return lax.dynamic_index_in_dim(value, index, axis, keepdims=False)


class Sum:
    def __init__(self, made, ids, lay):
        self.keep, self.send = made[:2], made[2:]
        self.ids, self.lay = ids, lay

    def first(self):
        self.got = [permute(self.send[0], self.lay.swap(2)), permute(self.send[1], self.lay.swap(4))]

    def second(self, *wait):
        got = lax.optimization_barrier((*self.got, *wait))
        self.keep, *self.send = second_call(self.ids, *self.keep, *got[:2])
        self.got = [permute(self.send[0], self.lay.swap(4)), permute(self.send[1], self.lay.swap(2))]

    def third(self, *wait):
        got = lax.optimization_barrier((*self.got, *wait))
        return [self.keep, *got[:2]]


def soap_update(master, moment, second, left, right, grads):
    turned = jnp.einsum("sij,ski->sjk", left, grads, precision=highest)
    turned = jnp.einsum("sjk,skl->sjl", turned, right, precision=highest)
    moment = beta_one * moment + (1.0 - beta_one) * turned
    second = beta_two * second + (1.0 - beta_two) * turned * turned
    ratio = moment / (1.0 - beta_one**STEP) / (jnp.sqrt(second / (1.0 - beta_two**STEP)) + adam_eps)
    back = jnp.einsum("sij,sjk->sik", left, ratio, precision=highest)
    back = jnp.einsum("sik,slk->sil", back, right, precision=highest)
    return (master - rate_matrix * (back + weight_decay * master), moment, second)


def vector_update(params, moment, second, grads):
    moment = beta_one * moment + (1.0 - beta_one) * grads
    second = beta_two * second + (1.0 - beta_two) * grads * grads
    ratio = moment / (1.0 - beta_one**STEP) / (jnp.sqrt(second / (1.0 - beta_two**STEP)) + adam_eps)
    return (params - rate_vector * (ratio + weight_decay * params), moment, second)


def butterfly(value, lay):
    bit = 1
    while bit < lay.imgs:
        value = value + permute(value, lay.swap(bit))
        bit *= 2
    bit = 1
    while bit < lay.scales:
        value = value + permute(value, lay.scale_swap(bit))
        bit *= 2
    return value


def local(
    images,
    valid_mask,
    scale_cols,
    boxes,
    normal_targets,
    dense_targets,
    affine_scale,
    affine_shift,
    conv_bf16,
    head_bf16,
    vectors,
    vec_m,
    vec_v,
    master,
    slot_m,
    slot_v,
    basis_left,
    basis_right,
    owner_slot,
):
    held, width, chans = (images.shape[1], images.shape[2], images.shape[3])
    heads_count, head_width = (head_bf16.shape[0], head_bf16.shape[2])
    wide = heads_count * head_width
    depth, taps = (conv_bf16.shape[0], conv_bf16.shape[1])
    scales, imgs = lax.axis_size("scale"), lax.axis_size("img")
    lay = Layout(scales, imgs)
    rows = held // scales
    z = lax.axis_index("scale")
    img = lax.axis_index("img")
    group, core = img // 2, img % 2
    place = jnp.where(group % 2 == 0, z, scales - 1 - z)
    mine = 2 * (place % 2) + core

    widths = [width >> s for s in range(scales)]
    starts = []
    at = 0
    for w in widths:
        starts.append(at)
        at += w + GAP
    cols = at
    col_iota = jnp.arange(cols, dtype=jnp.int32)
    valid_col = jnp.zeros((cols,), jnp.bool_)
    for s in range(scales):
        valid_col |= (col_iota >= starts[s]) & (col_iota < starts[s] + scale_cols[s])
    col_mask = valid_col.astype(f32)[None, :, None]

    own = images[0]
    fine = [
        permute(own[rows * k : rows * (k + 1)], lay.rows_round(k, [0])) for k in range(scales)
    ]
    coarse = []
    for k in range(scales):
        piece = (k + z) % scales
        send = lax.dynamic_slice_in_dim(own[:, : widths[1]], piece * rows, rows, 0)
        coarse.append(permute(send, lay.rows_round(k, range(1, scales))))
    target_rows = after(dense_targets, fine[-1]).reshape(held // (2 * rows), 2, rows, width, dense_targets.shape[2])
    kept_rows = pick(target_rows, core, 1)
    traded = permute(pick(target_rows, 1 - core, 1), lay.swap(1))
    lower = jnp.where(core == 0, kept_rows, traded)
    upper = jnp.where(core == 0, traded, kept_rows)
    ordered = jnp.concatenate([lower, upper], 0)
    ordered = jnp.where(group % 2 == 0, ordered, ordered[::-1])

    parts = [(fine[0] + fine[1]) + (fine[2] + fine[3])]
    for s in range(1, scales):
        got = 0.0
        for k in range(scales):
            got = got + jnp.where((mine - k) % scales == s, coarse[k][:, : widths[s]], 0)
        parts.append(got.astype(bf16))
    spread = []
    for s in range(scales):
        spread.append(parts[s])
        spread.append(jnp.zeros((rows, GAP, chans), bf16))
    x_zero = (jnp.concatenate(spread, 1) * col_mask.astype(bf16)).reshape(rows * cols, chans)

    valid_mask, boxes, normal_targets, scale_cols, *_ = lax.optimization_barrier(
        (valid_mask, boxes, normal_targets, scale_cols, *fine, *coarse)
    )

    mask_all = valid_mask.astype(f32)
    pixels = jnp.arange(held * width, dtype=jnp.int32)
    hits = jnp.sum((boxes[:, None] == pixels[None, :]).astype(f32), 0).reshape(held, width)
    packed = jnp.concatenate(
        [mask_all[None], (mask_all + box_weight * hits)[None], normal_targets], 0
    )
    packed_other = permute(packed, lay.swap(1))
    from_own = place // (scales // 2) == core
    packed = jnp.where(from_own, packed, packed_other)
    packed = lax.dynamic_slice_in_dim(packed, mine * rows, rows, 1).reshape(5, rows * width)
    valid, weight = packed[0][:, None], packed[1][:, None]
    normals = jnp.pad(packed[2:].T, ((0, 0), (0, 128 - 3)))
    tables = table_call(scale_cols, starts, widths, width, cols)
    gamma = vectors[:chans]
    bias = vectors[chans:]
    core_here = core.reshape(1)
    flat_mask = jnp.broadcast_to(col_mask, (rows, cols, 1)).reshape(rows * cols, 1)

    all_taps = conv_bf16.reshape(depth, 3, 3 * chans, chans)

    size = rows * cols

    def neighbours(value, facing):
        return permute(value, lay.swap(1)), permute(facing, lay.outward())

    def gain_of(depth_idx):
        return affine_scale[depth_idx].reshape(1, chans), affine_shift[depth_idx].reshape(1, chans)

    pre_shape = jax.ShapeDtypeStruct((size, chans), f32)
    buffer_shape = jax.ShapeDtypeStruct((size + cols, chans), bf16)
    grad_shape = jax.ShapeDtypeStruct((size, chans), bf16)
    facing_zero = lax.dynamic_slice_in_dim(x_zero, core * (rows - 1) * cols, cols, 0)
    partner_zero, outer_zero = neighbours(x_zero, facing_zero)
    arrived = lax.all_to_all(after(ordered, outer_zero), "scale", 0, 0, tiled=True)
    arrived = arrived.reshape(scales, rows * width, dense_targets.shape[2])
    pre_zero, x_one, facing_one = conv_call(
        first_conv_kernel,
        core_here,
        x_zero,
        partner_zero,
        outer_zero,
        *gain_of(0),
        flat_mask,
        [],
        all_taps,
        0,
        [pre_shape, buffer_shape, jax.ShapeDtypeStruct((cols, chans), bf16)],
        False,
        "conv_rows",
    )
    partner_one, outer_one = neighbours(x_one, facing_one)
    grad_one, facing_grad, grad_mine, grad_pack, grad_gamma, grad_bias, loss_parts = head_call(
        core_here,
        x_one,
        partner_one,
        outer_one,
        (*gain_of(1), flat_mask, gamma.reshape(1, chans), bias.reshape(1, wide)),
        (weight, valid, normals),
        head_bf16,
        arrived,
        tables,
        all_taps,
        1,
    )
    part = head_width // 2
    half = chans // 2
    staged = imgs == 8 and scales == 4
    x, y = (img // 2) % 2, img // 4
    ids = jnp.stack([core, x, y])
    grad_partner, grad_outer = neighbours(grad_one, facing_grad)
    pack_got = permute(grad_pack, lay.swap(1))
    conv_grad_one = kernel_grad(
        ids, x_one, partner_one, outer_one, grad_partner, grad_one, grad_partner, part, staged
    )
    if staged:
        early = Sum(conv_grad_one, ids, lay)
        early.first()
        pack_got = after(pack_got, *early.send)
    head_grad = head_grad_call(ids, grad_mine, grad_pack, pack_got, part, staged)
    if staged:
        middle = Sum(head_grad, ids, lay)
        middle.first()
        grad_outer = after(grad_outer, *middle.send)
    (grad_zero,) = conv_call(
        back_conv_kernel,
        core_here,
        grad_one,
        grad_partner,
        grad_outer,
        *gain_of(0),
        flat_mask,
        [pre_zero],
        all_taps,
        1,
        [grad_shape],
        True,
        "conv_back",
    )
    grad_zero_partner = permute(grad_zero, lay.swap(1))
    if staged:
        early.second(grad_zero)
        grad_zero_partner = after(grad_zero_partner, *early.send)
    conv_grad_zero = kernel_grad(
        ids,
        x_zero,
        partner_zero,
        outer_zero,
        partner_one,
        grad_zero,
        grad_zero_partner,
        part,
        staged,
    )
    if staged:
        late = Sum(conv_grad_zero, ids, lay)
        late.first()
    grad_gamma, grad_bias = grad_gamma.reshape(chans), grad_bias.reshape(wide)
    own_count = jnp.where(z == 0, jnp.sum(mask_all), 0.0).reshape(1)
    loss_parts = jnp.concatenate([loss_parts[0, :2], own_count])

    vec_rows = jnp.concatenate(
        [grad_gamma, grad_bias, loss_parts, jnp.zeros((-(chans + wide + 3) % 1024,), f32)]
    ).reshape(-1, 128)
    vec_sum = butterfly(vec_rows, lay).reshape(-1)
    totals = vec_sum[chans + wide : chans + wide + 2]
    count = vec_sum[chans + wide + 2]
    grad_vec = vec_sum[: chans + wide]
    vec_squares = jnp.sum(grad_vec * grad_vec)

    blocks_count = owner_slot.shape[0]
    slots_here = master.shape[0]
    slots = slots_here * scales * imgs
    slot_ids = jnp.arange(slots, dtype=jnp.int32)
    match = slot_ids[:, None] == owner_slot[None, :]
    block_of = jnp.sum(
        jnp.where(match, jnp.arange(blocks_count, dtype=jnp.int32)[None, :], 0), 1
    )
    owned_f = jnp.any(match, 1).astype(f32)

    if staged:
        early_line = third_call([early.third(*late.send)], scales)
        early_line = lax.all_to_all(early_line, "scale", 0, 0, tiled=True)
        middle.second(*late.send)
        late.second(*middle.send)
        late_line = third_call([late.third(), middle.third()], scales)
        late_line = lax.all_to_all(late_line, "scale", 0, 0, tiled=True)
        conv_pieces = 2 * taps
        payload = route_call(
            [early_line, late_line],
            [
                [(0, conv_pieces, conv_pieces)],
                [(0, 0, conv_pieces), (conv_pieces, 2 * conv_pieces, heads_count)],
            ],
            jnp.where(owned_f > 0, block_of, -1),
            scales * imgs,
            part // 4 // scales,
        )
        got = lax.all_to_all(payload, AXES, 0, 0, tiled=True)
        starts_here = [
            (i % 2) * (half // 2) + (i // 2 % 2) * (half // 4) + (i // 4) * (half // 8) + s * (half // 32)
            for s, i in lay.all_devices()
        ]
        master_new, slot_m_new, slot_v_new, fresh, norm = update_call(
            jnp.stack([vec_squares, count]),
            got,
            starts_here,
            master,
            slot_m,
            slot_v,
            basis_left,
            basis_right,
        )
        grad_norm, factor = norm[0, 0], norm[0, 1]
        vec_out = vector_update(vectors, vec_m, vec_v, grad_vec * factor)
        sources = spread_slots(fresh, lay, z, vec_out)
        owner = owner_slot // slots_here
        other_img = owner % imgs
        turn = other_img ^ img
        step = ((turn >> 1) & 1) * 8 + (turn >> 2) * 4 + ((owner // imgs) ^ z)
        place = jnp.sum(
            jnp.where(
                step[:, None] == jnp.arange(16, dtype=jnp.int32)[None, :],
                jnp.asarray(PLACES, jnp.int32)[None, :],
                0,
            ),
            1,
        )
        array = place // 8 + 4 * (turn & 1)
        item = (place % 8) * slots_here + owner_slot % slots_here
    else:
        parts = jnp.concatenate(
            [v.reshape(2 * taps, part, chans) for v in (conv_grad_zero, conv_grad_one)]
            + [head_grad[0].reshape(heads_count, part, chans)],
            0,
        )
        none = jnp.zeros_like(parts)
        blocks = jnp.concatenate(
            [jnp.where(core == 0, parts, none), jnp.where(core == 1, parts, none)], 1
        )
        by_slot = blocks[block_of] * owned_f[:, None, None]
        owned = lax.psum_scatter(by_slot, AXES, scatter_dimension=0, tiled=True)
        squares_sum = lax.psum(jnp.sum(owned * owned), AXES) + vec_squares

        grad_norm = jnp.sqrt(squares_sum) / count
        factor = clip_level / jnp.maximum(grad_norm, clip_level) / count
        master_new, slot_m_new, slot_v_new = soap_update(
            master, slot_m, slot_v, basis_left, basis_right, owned * factor
        )
        sources = [lax.all_gather(master_new.astype(bf16), AXES, axis=0, tiled=True)]
        array, item = jnp.zeros_like(owner_slot), owner_slot
        vec_out = vector_update(vectors, vec_m, vec_v, grad_vec * factor)
    vec_new, vec_m_new, vec_v_new = vec_out
    conv_copy, head_copy = place_blocks(sources, array, item, depth, taps)
    loss = jnp.stack([totals[0] / wide + totals[1], count])
    return (
        loss,
        grad_norm,
        vec_new,
        vec_m_new,
        vec_v_new,
        master_new,
        slot_m_new,
        slot_v_new,
        conv_copy,
        head_copy,
    )


def solution(mesh):
    in_specs = (
        P("scale", "img", None, None),
        P("img", None),
        P(),
        P("img"),
        P(None, "img", None),
        P("img", None, "scale"),
        P(),
        P(),
        P(),
        P(),
        P(),
        P(),
        P(),
        P(("scale", "img"), None, None),
        P(("scale", "img"), None, None),
        P(("scale", "img"), None, None),
        P(("scale", "img"), None, None),
        P(("scale", "img"), None, None),
        P(),
    )
    out_specs = (
        P(),
        P(),
        P(),
        P(),
        P(),
        P(("scale", "img"), None, None),
        P(("scale", "img"), None, None),
        P(("scale", "img"), None, None),
        P(),
        P(),
    )
    return jax.shard_map(local, mesh=mesh, in_specs=in_specs, out_specs=out_specs, check_vma=False)
```
